32 devices in a mesh: slide: 2 (over x), col: 16 (over z, y, core).
Axes of the slice: x: 2, y: 2, z: 4, core: 2. Of those that a mesh axis runs over, the one named last changes fastest.
Arguments:
- patches: bfloat16 [256, 128, 512], P(('slide', 'col')), parts along dimension 0, may hold values from -6 to 6
- tissue: int32 [256, 128], P(('slide', 'col')), parts along dimension 0, may hold values from 0 to 1, as said below
- w_query: bfloat16 [512, 512], replicated, may hold values from -0.25 to 0.25
- w_key: bfloat16 [512, 512], replicated, may hold values from -0.25 to 0.25
- w_value: bfloat16 [512, 512], replicated, may hold values from -0.25 to 0.25
- w_out: bfloat16 [512, 512], replicated, may hold values from -0.25 to 0.25
- agent_tokens: bfloat16 [256, 512], replicated, may hold values from -100 to 100
- kernel_seven: float32 [7, 7, 512], replicated, may hold values from -0.875 to 0.875
- kernel_five: float32 [5, 5, 512], replicated, may hold values from -1.25 to 1.25
- kernel_three: float32 [3, 3, 512], replicated, may hold values from -2 to 2
Outputs:
- mixed: bfloat16 [256, 128, 512], P(('slide', 'col')), parts along dimension 0
The draws below stay inside these ranges and needn't reach their ends.
There are 2 independent parts, one for each index of `slide`. The reference program is written for one: setup_inputs(seed, part) draws one part's arguments, and reference() takes and returns one part's arrays. A program takes and returns all parts, laid end to end along the dimension named above; an argument that names none is the same for every part. Nothing has to cross between parts.
Inputs may be any that keep to these rules, and one draw needn't show every extreme that they name: tissue holds 0 or 1; each slide has at least one tissue patch.
All inputs are finite; a program needn't handle non-finite values.
Results may differ from the reference program's by a relative error of at most 0.007.
The reference program's roundings to bfloat16 on the way (of `agent_values`, `token_weights` and `blended`) count: a program that leaves them out, or rounds other values in their place, can miss the bound.
Values may be sent and summed in bfloat16 or wider, within the bound.
No kernel may reach another device: no remote copies, remote signals or barrier semaphores. Data moves between devices by JAX's collectives and lax.ppermute only.
A program may use at most 128 MiB of HBM per device.

```python
import jax
import jax.numpy as jnp
from jax import lax

D = 512
HEADS = 8
HEAD_DIM = 64
AGENTS = 256
GRID_W = 128
ROWS_DEV = 8
GRID_H = 128
N_COL = 16


def draw_tissue(key, part):
    subkeys = jax.random.split(key, 4)
    side_cells = min(GRID_H, GRID_W)
    center_rows = jax.random.randint(subkeys[0], (8,), 0, GRID_H)
    center_cols = jax.random.randint(subkeys[1], (8,), 0, GRID_W)
    radii = jax.random.randint(subkeys[2], (8,), max(side_cells // 8, 1), side_cells // 4 + 1)
    row_ids = jnp.arange(GRID_H, dtype=jnp.int32)[:, None, None]
    col_ids = jnp.arange(GRID_W, dtype=jnp.int32)[None, :, None]
    row_gap = row_ids - center_rows[None, None, :]
    col_gap = col_ids - center_cols[None, None, :]
    inside = jnp.any(row_gap * row_gap + col_gap * col_gap <= (radii * radii)[None, None, :], axis=2)
    kept_cells = jax.random.randint(subkeys[3], (GRID_H, GRID_W), 0, 8) != 0
    result = jnp.logical_and(inside, kept_cells).astype(jnp.int32)
    return result.at[center_rows[0], center_cols[0]].set(1)


def draw_agent_tokens(key, part):
    subkeys = jax.random.split(key, 1)
    return jnp.clip(3.0 * jax.random.normal(subkeys[0], (AGENTS, D), jnp.float32), -18.0, 18.0).astype(jnp.bfloat16)


def shard_levels(rng, shape, cuts, low, high):
    factor_of, own = 1.0, jax.random.fold_in(rng, 6)
    for axis_at, parts in cuts:
        heights = jnp.exp(jax.random.uniform(jax.random.fold_in(own, axis_at), (parts,), jnp.float32, low / len(cuts), high / len(cuts)))
        factor_of = factor_of * jnp.repeat(heights, shape[axis_at] // parts).reshape([-1 if axis == axis_at else 1 for axis in range(len(shape))])
    return factor_of


def bell_draw(own_key, extent, scale, reach, cuts=(), held_as=jnp.bfloat16):
    values = scale * jax.random.normal(own_key, extent, jnp.float32)
    if cuts:
        values = values * shard_levels(own_key, extent, cuts, -0.22, 0.18)
    return jnp.clip(values, -reach, reach).astype(held_as)


def setup_inputs(seed: int = 0, part: int = 0) -> dict:
    keys = jax.random.split(jax.random.key(seed), 11)
    part_splits = jax.random.split(jax.random.fold_in(keys[10], part), 11)
    return {
        "patches": bell_draw(part_splits[0], (GRID_H, GRID_W, D), 1.0, 6.0, ((0, 16),)),
        "tissue": draw_tissue(jax.random.fold_in(jax.random.fold_in(keys[10], part), 71), part),
        "w_query": bell_draw(keys[2], (D, D), D ** -0.5, 0.25),
        "w_key": bell_draw(keys[3], (D, D), D ** -0.5, 0.25),
        "w_value": bell_draw(keys[4], (D, D), D ** -0.5, 0.25),
        "w_out": bell_draw(keys[5], (D, D), D ** -0.5, 0.25),
        "agent_tokens": draw_agent_tokens(jax.random.fold_in(keys[10], 71), part),
        "kernel_seven": bell_draw(keys[7], (7, 7, D), 49 ** -0.5, 0.875, (), jnp.float32),
        "kernel_five": bell_draw(keys[8], (5, 5, D), 25 ** -0.5, 1.25, (), jnp.float32),
        "kernel_three": bell_draw(keys[9], (3, 3, D), 9 ** -0.5, 2.0, (), jnp.float32),
    }


def depthwise(extended, kernel, reach_rows, band_rows, grid_width):
    padded = jnp.pad(extended.astype(jnp.float32), ((0, 0), (reach_rows, reach_rows), (0, 0)))
    span_taps = kernel.shape[0]
    total = jnp.zeros((band_rows, grid_width, kernel.shape[2]), jnp.float32)
    for row_tap in range(span_taps):
        for col_tap in range(span_taps):
            total = total + padded[row_tap:row_tap + band_rows, col_tap:col_tap + grid_width] * kernel[row_tap, col_tap]
    return total


def reference(patches, tissue, w_query, w_key, w_value, w_out, agent_tokens, kernel_seven, kernel_five, kernel_three):
    score_scale = HEAD_DIM ** -0.5
    band_tokens = ROWS_DEV * GRID_W
    flat_tokens = patches.reshape(-1, D)
    queries = jnp.dot(flat_tokens, w_query, preferred_element_type=jnp.float32).astype(jnp.bfloat16)
    keys_all = jnp.dot(flat_tokens, w_key, preferred_element_type=jnp.float32).astype(jnp.bfloat16)
    values_all = jnp.dot(flat_tokens, w_value, preferred_element_type=jnp.float32).astype(jnp.bfloat16)
    agent_heads = agent_tokens.astype(jnp.float32).reshape(AGENTS, HEADS, HEAD_DIM)
    tissue_flat = tissue.reshape(-1)
    band_ids = jnp.arange(N_COL, dtype=jnp.int32)

    def band_stats(band_index):
        start = (band_index * band_tokens).astype(jnp.int32)
        key_band = lax.dynamic_slice_in_dim(keys_all, start, band_tokens, 0).astype(jnp.float32).reshape(band_tokens, HEADS, HEAD_DIM)
        value_band = lax.dynamic_slice_in_dim(values_all, start, band_tokens, 0).astype(jnp.float32).reshape(band_tokens, HEADS, HEAD_DIM)
        valid_band = lax.dynamic_slice_in_dim(tissue_flat, start, band_tokens, 0)[None, None, :] > 0
        scores = jnp.einsum('ahd,thd->hat', agent_heads, key_band) * score_scale
        peak_band = jnp.max(jnp.where(valid_band, scores, -1e30), axis=2)
        expo = jnp.where(valid_band, jnp.exp(scores - peak_band[:, :, None]), jnp.float32(0.0))
        total_band = jnp.sum(expo, axis=2)
        weighted_band = jnp.einsum('hat,thd->had', expo.astype(jnp.bfloat16).astype(jnp.float32), value_band)
        return peak_band, total_band, weighted_band

    band_peaks, band_totals, band_weighted = lax.map(band_stats, band_ids)
    peak = jnp.max(band_peaks, axis=0)
    factor = jnp.exp(band_peaks - peak[None])
    totals = jnp.sum(band_totals * factor, axis=0)
    weighted = jnp.sum(band_weighted * factor[..., None], axis=0)
    agent_values = (weighted / totals[..., None]).astype(jnp.bfloat16)

    value_grid = values_all.reshape(GRID_H, GRID_W, D)
    value_padded = jnp.pad(value_grid, ((3, 3), (0, 0), (0, 0)))

    def band_output(band_index):
        start = (band_index * band_tokens).astype(jnp.int32)
        query_band = lax.dynamic_slice_in_dim(queries, start, band_tokens, 0).astype(jnp.float32).reshape(band_tokens, HEADS, HEAD_DIM)
        scores = jnp.einsum('thd,ahd->tha', query_band, agent_heads) * score_scale
        top_score = jnp.max(scores, axis=2, keepdims=True)
        expo = jnp.exp(scores - top_score)
        token_weights = (expo / jnp.sum(expo, axis=2, keepdims=True)).astype(jnp.bfloat16)
        attended = jnp.einsum('tha,had->thd', token_weights.astype(jnp.float32), agent_values.astype(jnp.float32)).reshape(ROWS_DEV, GRID_W, D)
        extended = lax.dynamic_slice_in_dim(value_padded, (band_index * ROWS_DEV).astype(jnp.int32), ROWS_DEV + 6, 0)
        position = depthwise(extended, kernel_seven, 3, ROWS_DEV, GRID_W)
        position = position + depthwise(extended[1:-1], kernel_five, 2, ROWS_DEV, GRID_W)
        position = position + depthwise(extended[2:-2], kernel_three, 1, ROWS_DEV, GRID_W)
        blended = (attended + position).astype(jnp.bfloat16).reshape(band_tokens, D)
        return jnp.dot(blended, w_out, preferred_element_type=jnp.float32).astype(jnp.bfloat16).reshape(ROWS_DEV, GRID_W, D)

    return lax.map(band_output, band_ids).reshape(GRID_H, GRID_W, D)
```

```python
import functools

import jax
import jax.numpy as jnp
from jax import lax
from jax.experimental import pallas as pl
from jax.experimental.pallas import tpu as pltpu
from jax.sharding import PartitionSpec as P

HEADS = 8
NO_SCORE = -1e30
F32 = jnp.float32
BF16 = jnp.bfloat16
VMEM = pltpu.VMEM


def dot_nt(a, b):
    return lax.dot_general(a, b, (((1,), (1,)), ((), ())), preferred_element_type=F32)


def dot_nn(a, b):
    return lax.dot_general(a, b, (((1,), (0,)), ((), ())), preferred_element_type=F32)


def head_tokens(pair, half, scale):
    lane = lax.broadcasted_iota(jnp.int32, pair.shape, 1)
    mine = (lane >= 64) if half else (lane < 64)
    return jnp.where(mine, pair.astype(F32) * scale, 0.0).astype(BF16)


def chunk_of_device():
    place = lax.axis_index("col")
    return (place & 1) * 2 + ((place >> 1) & 1)


def band_kernel(scale, own_ref, patches, tissue, w_key, w_value, agents, values, keep, send, keys, values_t, bias):
    tokens = patches.shape[0]
    grid_rows, grid_width = tissue.shape
    block = 256
    for at in range(0, tokens, block):
        rows = pl.ds(at, block)
        part = patches[rows, :]
        keys[rows, :] = dot_nn(part, w_key[...]).astype(BF16)
        value = dot_nn(part, w_value[...]).astype(BF16)
        values[rows, :] = value
        values_t[:, rows] = value.T
    for row in range(grid_rows):
        line = jnp.where(tissue[row : row + 1, :] > 0, 0.0, NO_SCORE).astype(F32)
        bias[row * grid_width : (row + 1) * grid_width, :] = jnp.broadcast_to(line, (128, grid_width)).T
    own = own_ref[0]
    for index in range(4):
        chunk = index ^ own
        lanes = pl.ds(pl.multiple_of(chunk * 128, 128), 128)
        pair_keys = keys[:, lanes]
        pair_agents = agents[:, lanes]
        out = keep if index < 2 else send
        for half in range(2):
            scores = dot_nt(pair_keys, head_tokens(pair_agents, half, scale))
            column = bias[...]
            scores = scores + jnp.concatenate([column, column], axis=1)
            peak = jnp.max(scores, axis=0, keepdims=True)
            expo = jnp.exp(scores - peak)
            total = jnp.sum(expo, axis=0, keepdims=True)
            value_rows = pl.ds(pl.multiple_of(chunk * 128 + half * 64, 64), 64)
            weighted = dot_nn(values_t[value_rows, :], expo.astype(BF16))
            cols = slice(half * 256, half * 256 + 256)
            out[index % 2, 0:64, cols] = weighted
            row_id = lax.broadcasted_iota(jnp.int32, (8, 256), 0)
            stats = jnp.where(row_id == 0, peak, jnp.where(row_id == 1, total, 0.0))
            out[index % 2, 64:72, cols] = stats


def merge(first, second):
    peak_1, total_1, weighted_1 = first
    peak_2, total_2, weighted_2 = second
    peak = jnp.maximum(peak_1, peak_2)
    factor_1 = jnp.exp(peak_1 - peak)
    factor_2 = jnp.exp(peak_2 - peak)
    return peak, total_1 * factor_1 + total_2 * factor_2, weighted_1 * factor_1 + weighted_2 * factor_2


def wide(ref, index=None):
    array = ref[...] if index is None else ref[index]
    return array[64:65], array[65:66], array[0:64]


def thirds(value):
    high = value.astype(BF16).astype(F32)
    rest = value - high
    middle = rest.astype(BF16).astype(F32)
    return high, middle, rest - middle


def put_wide(ref, state):
    peak, total, weighted = state
    row_id = lax.broadcasted_iota(jnp.int32, (8, weighted.shape[1]), 0)
    ref[0:64] = weighted
    ref[64:72] = jnp.where(row_id == 0, peak, jnp.where(row_id == 1, total, 0.0))


def put_narrow(ref, state):
    peak, total, weighted = state
    row_id = lax.broadcasted_iota(jnp.int32, (16, weighted.shape[1]), 0)
    stats = jnp.zeros((16, weighted.shape[1]), F32)
    for at, part in enumerate(thirds(peak) + thirds(total)):
        stats = jnp.where(row_id == at, part, stats)
    ref[0:64] = weighted.astype(BF16)
    ref[64:80] = stats.astype(BF16)


def narrow(ref):
    stats = ref[64:80].astype(F32)
    peak = stats[0:1] + stats[1:2] + stats[2:3]
    total = stats[3:4] + stats[4:5] + stats[5:6]
    return peak, total, ref[0:64].astype(F32)


def first_merge_kernel(keep, got, own, payload):
    put_narrow(payload, merge(wide(keep, 1), wide(got, 1)))
    put_wide(own, merge(wide(keep, 0), wide(got, 0)))


def next_merge_kernel(held, got, own, payload):
    state = merge(wide(held), narrow(got))
    put_narrow(payload, state)
    put_wide(own, state)


def last_merge_kernel(held, got, agent_values):
    _, total, weighted = merge(wide(held), narrow(got))
    agent_values[...] = (weighted / total).astype(BF16)


def token_kernel(scale, patches, w_query, agents, weights):
    queries = dot_nn(patches[...], w_query[...]).astype(BF16)
    for head in range(HEADS):
        lanes = slice(head // 2 * 128, head // 2 * 128 + 128)
        scores = dot_nt(queries[:, lanes], head_tokens(agents[:, lanes], head % 2, scale))
        expo = jnp.exp(scores - jnp.max(scores, axis=1, keepdims=True))
        part = expo * (1.0 / jnp.sum(expo, axis=1, keepdims=True))
        weights[:, head * 256 : head * 256 + 256] = part.astype(BF16)


def conv_kernel(values, above, below, seven, five, three, position, padded, taps):
    out_rows, width = values.shape[0], values.shape[1]
    lanes = values.shape[2]
    merged = [[seven[p, q : q + 1, :] for q in range(7)] for p in range(7)]
    for p in range(5):
        for q in range(5):
            merged[p + 1][q + 1] = merged[p + 1][q + 1] + five[p, q : q + 1, :]
    for p in range(3):
        for q in range(3):
            merged[p + 2][q + 2] = merged[p + 2][q + 2] + three[p, q : q + 1, :]
    for p in range(7):
        for q in range(7):
            taps[p, q] = jnp.broadcast_to(merged[p][q], (8, lanes))
    edge = jnp.zeros((out_rows + 6, 8, lanes), F32)
    padded[:, 0:8, :] = edge
    padded[:, 8 + width : 16 + width, :] = edge
    padded[0:3, 8 : 8 + width, :] = above[...].astype(F32)
    padded[3 : 3 + out_rows, 8 : 8 + width, :] = values[...].astype(F32)
    padded[3 + out_rows : 6 + out_rows, 8 : 8 + width, :] = below[...].astype(F32)
    for at in range(0, width, 8):
        totals = [jnp.zeros((8, lanes), F32)] * out_rows
        for q in range(7):
            lines = [padded[row, at + 5 + q : at + 13 + q, :] for row in range(out_rows + 6)]
            for p in range(7):
                tap = taps[p, q]
                for row in range(out_rows):
                    totals[row] = totals[row] + lines[row + p] * tap
        for row in range(out_rows):
            position[row, at : at + 8, :] = totals[row]


def out_kernel(own_ref, weights, own, near, side, far, position, w_out, mixed, spread):
    @pl.when(pl.program_id(0) == 0)
    def _():
        spread[...] = jnp.zeros_like(spread)
        for index, part in enumerate((own, near, side, far)):
            chunk = index ^ own_ref[0]
            group, place = chunk // 2, chunk % 2
            for half in range(2):
                rows = pl.ds(pl.multiple_of(place * 128 + half * 64, 64), 64)
                cols = pl.ds(pl.multiple_of(place * 512 + half * 256, 256), 256)
                spread[group, rows, cols] = part[:, half * 256 : half * 256 + 256]

    blended = []
    for group in range(2):
        attended = dot_nt(weights[:, group * 1024 : group * 1024 + 1024], spread[group])
        blended.append((attended + position[:, group * 256 : group * 256 + 256]).astype(BF16))
    mixed[...] = dot_nn(jnp.concatenate(blended, axis=1), w_out[...]).astype(BF16)


def params(megabytes=48):
    return pltpu.CompilerParams(vmem_limit_bytes=megabytes << 20)


def cost(flops, moved, exps=0):
    return pl.CostEstimate(flops=int(flops), bytes_accessed=int(moved), transcendentals=int(exps))


def shape(dims, dtype):
    return jax.ShapeDtypeStruct(dims, dtype)


def exchange(x, bit):
    peers = lax.axis_size("col")
    return lax.ppermute(x, "col", [(i, i ^ bit) for i in range(peers)])


def halo_rows(values):
    peers, rows = lax.axis_size("col"), values.shape[0]
    odd = lax.axis_index("col") % 2 == 1
    first, last = values[:3], values[rows - 3 :]
    pair = [(i, i ^ 1) for i in range(peers)]
    rest = [(i, i + 1) for i in range(1, peers - 1, 2)]
    inner = lax.ppermute(jnp.where(odd, first, last), "col", pair)
    outer = lax.ppermute(jnp.where(odd, last, first), "col", rest + [(j, i) for i, j in rest])
    return jnp.where(odd, inner, outer), jnp.where(odd, outer, inner)


def on_device(patches, tissue, w_query, w_key, w_value, w_out, agent_tokens, seven, five, three):
    band_rows, width, dim = patches.shape
    tokens = band_rows * width
    agents = agent_tokens.shape[0]
    scale = (dim // HEADS) ** (-0.5)
    flat = patches.reshape(tokens, dim)
    own_chunk = jnp.reshape(chunk_of_device(), (1,)).astype(jnp.int32)
    smem = pl.BlockSpec(memory_space=pltpu.SMEM)
    vmem = pl.BlockSpec(memory_space=VMEM)

    values, keep, send = pl.pallas_call(
        functools.partial(band_kernel, scale),
        out_shape=(shape((tokens, dim), BF16), shape((2, 72, 512), F32), shape((2, 72, 512), F32)),
        in_specs=[smem] + [vmem] * 5,
        out_specs=[vmem] * 3,
        scratch_shapes=[
            VMEM((tokens, dim), BF16),
            VMEM((dim, tokens), BF16),
            VMEM((tokens, 128), F32),
        ],
        compiler_params=params(),
        cost_estimate=cost(1.6e9, 4e6, 2e6),
        name="band",
    )(own_chunk, flat, tissue, w_key, w_value, agent_tokens)

    small = dict(in_specs=[vmem] * 2, compiler_params=params(16))
    wide_shape, narrow_shape = shape((72, 512), F32), shape((80, 512), BF16)
    got = exchange(send, 1)
    held, payload = pl.pallas_call(
        first_merge_kernel, out_shape=(wide_shape, narrow_shape), out_specs=[vmem] * 2,
        cost_estimate=cost(1e6, 1e6), name="merge_first", **small,
    )(keep, got)
    peers = lax.axis_size("col")
    bit = 2
    while bit * 2 < peers:
        got = exchange(payload, bit)
        held, payload = pl.pallas_call(
            next_merge_kernel, out_shape=(wide_shape, narrow_shape), out_specs=[vmem] * 2,
            cost_estimate=cost(1e6, 1e6), name="merge_next", **small,
        )(held, got)
        bit *= 2
    got = exchange(payload, bit)
    own = pl.pallas_call(
        last_merge_kernel, out_shape=shape((64, 512), BF16), out_specs=vmem,
        cost_estimate=cost(1e6, 1e6), name="merge_last", **small,
    )(held, got)
    near = exchange(own, 2)
    side = exchange(own, 1)
    far = exchange(near, 1)

    block = 256
    weights = pl.pallas_call(
        functools.partial(token_kernel, scale),
        grid=(tokens // block,),
        out_shape=shape((tokens, HEADS * agents), BF16),
        in_specs=[pl.BlockSpec((block, dim), lambda i: (i, 0)), vmem, vmem],
        out_specs=pl.BlockSpec((block, HEADS * agents), lambda i: (i, 0)),
        compiler_params=params(),
        cost_estimate=cost(1.1e9, 6e6, 2e6),
        name="token",
    )(flat, w_query, agent_tokens)

    grid_values = values.reshape(band_rows, width, dim)
    above, below = halo_rows(grid_values)

    def lane_block(rows, cols):
        return pl.BlockSpec((rows, cols, 128), lambda i: (0, 0, i))

    position = pl.pallas_call(
        conv_kernel,
        grid=(dim // 128,),
        out_shape=shape((band_rows, width, dim), F32),
        in_specs=[
            lane_block(band_rows, width),
            lane_block(3, width),
            lane_block(3, width),
            lane_block(7, 7),
            lane_block(5, 5),
            lane_block(3, 3),
        ],
        out_specs=lane_block(band_rows, width),
        scratch_shapes=[VMEM((band_rows + 6, width + 16, 128), F32), VMEM((7, 7, 8, 128), F32)],
        compiler_params=params(),
        cost_estimate=cost(3e9, 4e6),
        name="conv",
    )(grid_values, above, below, seven, five, three).reshape(tokens, dim)

    mixed = pl.pallas_call(
        out_kernel,
        grid=(tokens // block,),
        out_shape=shape((tokens, dim), BF16),
        in_specs=[
            smem,
            pl.BlockSpec((block, HEADS * agents), lambda i: (i, 0)),
            vmem,
            vmem,
            vmem,
            vmem,
            pl.BlockSpec((block, dim), lambda i: (i, 0)),
            vmem,
        ],
        out_specs=pl.BlockSpec((block, dim), lambda i: (i, 0)),
        scratch_shapes=[VMEM((2, 256, 1024), BF16)],
        compiler_params=params(),
        cost_estimate=cost(1.1e9, 8e6),
        name="out",
    )(own_chunk, weights, own, near, side, far, position, w_out)
    return mixed.reshape(band_rows, width, dim)


def solution(mesh):
    return jax.shard_map(
        on_device,
        mesh=mesh,
        in_specs=(
            P(("slide", "col"), None, None),
            P(("slide", "col"), None),
            P(),
            P(),
            P(),
            P(),
            P(),
            P(),
            P(),
            P(),
        ),
        out_specs=P(("slide", "col"), None, None),
        check_vma=False,
    )
```

```python
import functools

import jax
import jax.numpy as jnp
from jax import lax
from jax.experimental import pallas as pl
from jax.experimental.pallas import tpu as pltpu
from jax.sharding import PartitionSpec as P

HEADS = 8
NO_SCORE = -1e30
F32 = jnp.float32
BF16 = jnp.bfloat16
VMEM = pltpu.VMEM


def dot_nt(a, b):
    return lax.dot_general(a, b, (((1,), (1,)), ((), ())), preferred_element_type=F32)


def dot_nn(a, b):
    return lax.dot_general(a, b, (((1,), (0,)), ((), ())), preferred_element_type=F32)


def head_tokens(pair, half, scale):
    lane = lax.broadcasted_iota(jnp.int32, pair.shape, 1)
    mine = (lane >= 64) if half else (lane < 64)
    return jnp.where(mine, pair.astype(F32) * scale, 0.0).astype(BF16)


def chunk_of_device():
    place = lax.axis_index("col")
    return (place & 1) * 2 + ((place >> 1) & 1)


def band_kernel(
    scale, own_ref, mine, other, tissue, other_tissue, w_key, w_value, agents, values, keep, payload, keys, vals
):
    tokens = mine.shape[0]
    block = 256
    own = own_ref[0]
    half_lanes = pl.ds(pl.multiple_of((own // 2) * 256, 256), 256)
    key_half = w_key[:, half_lanes]
    value_half = w_value[:, half_lanes]
    for at in range(0, tokens, block):
        rows = pl.ds(at, block)
        part = mine[rows, :]
        keys[rows, :] = dot_nn(part, key_half).astype(BF16)
        values[rows, :] = dot_nn(part, w_value[...]).astype(BF16)
        vals[rows, :] = values[rows, half_lanes]
    for at in range(0, tokens, block):
        rows = pl.ds(tokens + at, block)
        part = other[pl.ds(at, block), :]
        keys[rows, :] = dot_nn(part, key_half).astype(BF16)
        vals[rows, :] = dot_nn(part, value_half).astype(BF16)
    lines = []
    for grid in (tissue, other_tissue):
        bias = jnp.where(grid[...] > 0, 0.0, NO_SCORE).astype(F32)
        lines += [bias[row : row + 1] for row in range(bias.shape[0])]
    bias_line = jnp.concatenate(lines, axis=1)

    def lanes_of(index):
        return pl.ds(pl.multiple_of(((own % 2) ^ index) * 128, 128), 128)

    def scores_of(index, half):
        chunk_lanes = pl.ds(pl.multiple_of((own ^ index) * 128, 128), 128)
        tokens_of = head_tokens(agents[:, chunk_lanes], half, scale)
        return dot_nt(tokens_of, keys[:, lanes_of(index)]) + bias_line

    order = [(1, 0), (1, 1), (0, 0), (0, 1)]
    ahead = scores_of(*order[0])
    done = []
    for step, (index, half) in enumerate(order):
        scores = ahead
        if step + 1 < len(order):
            ahead = scores_of(*order[step + 1])
        peak = jnp.max(scores, axis=1, keepdims=True)
        expo = jnp.exp(scores - peak)
        total = jnp.sum(expo, axis=1, keepdims=True)
        done.append((peak, total, dot_nn(expo.astype(BF16), vals[:, lanes_of(index)])))
        if half == 1:
            lane = lax.broadcasted_iota(jnp.int32, (256, 128), 1)
            weighted = jnp.where(lane < 64, done[0][2], done[1][2]).T
            stats = jnp.zeros((256, 128), F32)
            for at, value in enumerate(done[0][:2] + done[1][:2]):
                stats = jnp.where(lane == at, value, stats)
            stats = stats.T
            sides = []
            for at in range(2):
                sides.append((stats[2 * at : 2 * at + 1], stats[2 * at + 1 : 2 * at + 2], weighted[64 * at : 64 * at + 64]))
            state = tuple(jnp.concatenate(pair, axis=1) for pair in zip(*sides))
            if index == 1:
                put_narrow(payload, state)
            else:
                put_wide(keep, state)
            done = []


def merge(first, second):
    peak_1, total_1, weighted_1 = first
    peak_2, total_2, weighted_2 = second
    peak = jnp.maximum(peak_1, peak_2)
    factor_1 = jnp.exp(peak_1 - peak)
    factor_2 = jnp.exp(peak_2 - peak)
    return peak, total_1 * factor_1 + total_2 * factor_2, weighted_1 * factor_1 + weighted_2 * factor_2


def wide(ref, index=None):
    array = ref[...] if index is None else ref[index]
    return array[64:65], array[65:66], array[0:64]


def thirds(value):
    high = value.astype(BF16).astype(F32)
    rest = value - high
    middle = rest.astype(BF16).astype(F32)
    return high, middle, rest - middle


def put_wide(ref, state):
    peak, total, weighted = state
    row_id = lax.broadcasted_iota(jnp.int32, (8, weighted.shape[1]), 0)
    ref[0:64] = weighted
    ref[64:72] = jnp.where(row_id == 0, peak, jnp.where(row_id == 1, total, 0.0))


def put_narrow(ref, state):
    peak, total, weighted = state
    row_id = lax.broadcasted_iota(jnp.int32, (16, weighted.shape[1]), 0)
    stats = jnp.zeros((16, weighted.shape[1]), F32)
    for at, part in enumerate(thirds(peak) + thirds(total)):
        stats = jnp.where(row_id == at, part, stats)
    ref[0:64] = weighted.astype(BF16)
    ref[64:80] = stats.astype(BF16)


def narrow(ref):
    stats = ref[64:80].astype(F32)
    peak = stats[0:1] + stats[1:2] + stats[2:3]
    total = stats[3:4] + stats[4:5] + stats[5:6]
    return peak, total, ref[0:64].astype(F32)


def next_merge_kernel(held, got, before, own, payload):
    state = merge(wide(held), narrow(got))
    put_narrow(payload, state)
    put_wide(own, state)


def last_merge_kernel(held, got, before, agent_values):
    _, total, weighted = merge(wide(held), narrow(got))
    agent_values[...] = (weighted / total).astype(BF16)


def token_kernel(scale, patches, w_query, agents, after, weights, queries):
    heads = weights.shape[1] // agents.shape[0]
    queries[...] = dot_nn(patches[...], w_query[...]).astype(BF16)

    def scores_of(head):
        lanes = slice(head // 2 * 128, head // 2 * 128 + 128)
        return dot_nt(queries[:, lanes], head_tokens(agents[:, lanes], head % 2, scale))

    ahead = scores_of(0)
    for head in range(heads):
        scores = ahead
        if head + 1 < heads:
            ahead = scores_of(head + 1)
        expo = jnp.exp(scores - jnp.max(scores, axis=1, keepdims=True))
        part = expo * (1.0 / jnp.sum(expo, axis=1, keepdims=True))
        weights[:, head * 256 : head * 256 + 256] = part.astype(BF16)


def halo_kernel(odd_ref, other, outer, w_value, above, below):
    rows = 3 * 128
    odd = odd_ref[0] == 1
    inner_part = other[pl.ds(pl.multiple_of(odd_ref[0] * (other.shape[0] - rows), 128), rows), :]
    inner = dot_nn(inner_part, w_value[...]).astype(BF16)
    outside = dot_nn(outer[...], w_value[...]).astype(BF16)
    above[...] = jnp.where(odd, inner, outside)
    below[...] = jnp.where(odd, outside, inner)


def border_kernel(odd_ref, flat, border, sem):
    rows = border.shape[0]
    start = pl.multiple_of(odd_ref[0] * (flat.shape[0] - rows), 128)
    copy = pltpu.make_async_copy(flat.at[pl.ds(start, rows), :], border, sem)
    copy.start()
    copy.wait()


def conv_kernel(first_lane, values, above, below, seven, five, three, after, position, padded, taps):
    out_rows, width = position.shape[0], position.shape[1]
    lanes = 128
    span = 3 * width
    edge = jnp.zeros((out_rows + 6, 8, lanes), F32)
    padded[:, 0:8, :] = edge
    padded[:, 8 + width : 16 + width, :] = edge
    for group in range(position.shape[2] // lanes):
        here = slice(first_lane + group * lanes, first_lane + (group + 1) * lanes)
        merged = [[seven[p, q : q + 1, here] for q in range(7)] for p in range(7)]
        for p in range(5):
            for q in range(5):
                merged[p + 1][q + 1] = merged[p + 1][q + 1] + five[p, q : q + 1, here]
        for p in range(3):
            for q in range(3):
                merged[p + 2][q + 2] = merged[p + 2][q + 2] + three[p, q : q + 1, here]
        for p in range(7):
            for q in range(7):
                taps[p, q] = jnp.broadcast_to(merged[p][q], (8, lanes))
        inside = slice(8, 8 + width)
        padded[0:3, inside, :] = above[0:span, here].astype(F32).reshape(3, width, lanes)
        padded[3 : 3 + out_rows, inside, :] = values[:, here].astype(F32).reshape(out_rows, width, lanes)
        padded[3 + out_rows : 6 + out_rows, inside, :] = below[0:span, here].astype(F32).reshape(3, width, lanes)
        for at in range(0, width, 8):
            totals = [jnp.zeros((8, lanes), F32)] * out_rows
            for q in range(7):
                lines = [padded[row, at + 5 + q : at + 13 + q, :] for row in range(out_rows + 6)]
                for p in range(7):
                    tap = taps[p, q]
                    for row in range(out_rows):
                        totals[row] = totals[row] + lines[row + p] * tap
            for row in range(out_rows):
                position[row, at : at + 8, group * lanes : (group + 1) * lanes] = totals[row]


def out_kernel(own_ref, weights_low, weights_high, own, near, side, far, position_low, position_high, w_out, mixed, spread):
    @pl.when(pl.program_id(0) == 0)
    def _():
        spread[...] = jnp.zeros_like(spread)
        for index, part in enumerate((own, near, side, far)):
            chunk = index ^ own_ref[0]
            group, place = chunk // 2, chunk % 2
            for half in range(2):
                rows = pl.ds(pl.multiple_of(place * 128 + half * 64, 64), 64)
                cols = pl.ds(pl.multiple_of(place * 512 + half * 256, 256), 256)
                spread[group, rows, cols] = part[:, half * 256 : half * 256 + 256]

    block = mixed.shape[0]
    here = pl.ds(pl.multiple_of(pl.program_id(0) * block, block), block)
    blended = []
    for group, (weights, position) in enumerate(((weights_low, position_low), (weights_high, position_high))):
        attended = dot_nt(weights[here, :], spread[group])
        blended.append((attended + position[here, :]).astype(BF16))
    mixed[...] = dot_nn(jnp.concatenate(blended, axis=1), w_out[...]).astype(BF16)


def params(megabytes=48):
    return pltpu.CompilerParams(vmem_limit_bytes=megabytes << 20)


def cost(flops, moved, exps=0):
    return pl.CostEstimate(flops=int(flops), bytes_accessed=int(moved), transcendentals=int(exps))


def shape(dims, dtype):
    return jax.ShapeDtypeStruct(dims, dtype)


def exchange(x, bit):
    peers = lax.axis_size("col")
    return lax.ppermute(x, "col", [(i, i ^ bit) for i in range(peers)])


def on_device(patches, tissue, w_query, w_key, w_value, w_out, agent_tokens, seven, five, three):
    band_rows, width, dim = patches.shape
    tokens = band_rows * width
    agents = agent_tokens.shape[0]
    half_dim = dim // 2
    scale = (dim // HEADS) ** (-0.5)
    flat = patches.reshape(tokens, dim)
    peers = lax.axis_size("col")
    place = lax.axis_index("col")
    odd = place % 2
    odd_word = jnp.reshape(odd, (1,)).astype(jnp.int32)
    own_chunk = jnp.reshape(chunk_of_device(), (1,)).astype(jnp.int32)
    smem = pl.BlockSpec(memory_space=pltpu.SMEM)
    vmem = pl.BlockSpec(memory_space=VMEM)
    anywhere = pl.BlockSpec(memory_space=pl.ANY)

    other = exchange(flat, 1)
    other_tissue = exchange(tissue, 1)
    rest = [(i, i + 1) for i in range(1, peers - 1, 2)]
    border = pl.pallas_call(
        border_kernel,
        out_shape=shape((3 * width, dim), BF16),
        in_specs=[smem, pl.BlockSpec(memory_space=pltpu.HBM)],
        out_specs=vmem,
        scratch_shapes=[pltpu.SemaphoreType.DMA],
        compiler_params=params(60),
        cost_estimate=cost(1e10, 1e6),
        name="border",
    )(odd_word, flat)
    outer = lax.ppermute(border, "col", rest + [(j, i) for i, j in rest])

    wide_shape, narrow_shape = shape((72, 512), F32), shape((80, 512), BF16)
    values, held, payload = pl.pallas_call(
        functools.partial(band_kernel, scale),
        out_shape=(shape((tokens, dim), BF16), wide_shape, narrow_shape),
        in_specs=[smem] + [vmem] * 7,
        out_specs=[vmem] * 3,
        scratch_shapes=[VMEM((2 * tokens, half_dim), BF16), VMEM((2 * tokens, half_dim), BF16)],
        compiler_params=params(24),
        cost_estimate=cost(1.8e9, 4e6, 2e6),
        name="band",
    )(own_chunk, flat, other, tissue, other_tissue, w_key, w_value, agent_tokens)

    def token(at, after):
        lanes = slice(at * half_dim, (at + 1) * half_dim)
        return pl.pallas_call(
            functools.partial(token_kernel, scale),
            out_shape=shape((tokens, HEADS // 2 * agents), BF16),
            grid=(1,),
            in_specs=[
                vmem,
                pl.BlockSpec((dim, half_dim), lambda i: (0, at)),
                pl.BlockSpec((agents, half_dim), lambda i: (0, at)),
                anywhere,
            ],
            out_specs=vmem,
            scratch_shapes=[VMEM((tokens, half_dim), BF16)],
            compiler_params=params(20),
            cost_estimate=cost(1.1e9, 6e6, 1e6),
            name="token",
        )(flat, w_query, agent_tokens, after)

    def conv(at, after):
        return pl.pallas_call(
            functools.partial(conv_kernel, at * half_dim),
            out_shape=shape((band_rows, width, half_dim), F32),
            in_specs=[vmem] * 6 + [anywhere],
            out_specs=vmem,
            scratch_shapes=[VMEM((band_rows + 6, width + 16, 128), F32), VMEM((7, 7, 8, 128), F32)],
            compiler_params=params(20),
            cost_estimate=cost(3e9, 4e6),
            name="conv",
        )(values, above, below, seven, five, three, after).reshape(tokens, half_dim)

    hop = dict(in_specs=[vmem, vmem, anywhere], compiler_params=params(16), cost_estimate=cost(1e6, 1e6))

    def next_merge(held, got, before):
        return pl.pallas_call(
            next_merge_kernel, out_shape=(wide_shape, narrow_shape), out_specs=[vmem] * 2, name="merge_next", **hop
        )(held, got, before)

    got = exchange(payload, 2)
    weights_low = token(0, payload)
    above, below = pl.pallas_call(
        halo_kernel,
        out_shape=(shape((3 * width, dim), BF16), shape((3 * width, dim), BF16)),
        in_specs=[smem] + [vmem] * 3,
        out_specs=[vmem] * 2,
        compiler_params=params(16),
        cost_estimate=cost(4e8, 2e6),
        name="halo",
    )(odd_word, other, outer, w_value)
    held, payload = next_merge(held, got, weights_low)
    bit = 4
    filler = weights_high = None
    while bit * 2 < peers:
        got = exchange(payload, bit)
        if weights_high is None:
            weights_high = filler = token(1, payload)
        held, payload = next_merge(held, got, filler)
        bit *= 2
    got = exchange(payload, bit)
    position_low = conv(0, payload)
    own = pl.pallas_call(
        last_merge_kernel, out_shape=shape((64, 512), BF16), out_specs=vmem, name="merge_last", **hop
    )(held, got, position_low)
    near = exchange(own, 2)
    side = exchange(own, 1)
    position_high = conv(1, own)
    far = exchange(near, 1)

    block = 256
    mixed = pl.pallas_call(
        out_kernel,
        grid=(tokens // block,),
        out_shape=shape((tokens, dim), BF16),
        in_specs=[smem] + [vmem] * 9,
        out_specs=pl.BlockSpec((block, dim), lambda i: (i, 0)),
        scratch_shapes=[VMEM((2, 256, 1024), BF16)],
        compiler_params=params(20),
        cost_estimate=cost(1.1e9, 8e6),
        name="out",
    )(own_chunk, weights_low, weights_high, own, near, side, far, position_low, position_high, w_out)
    return mixed.reshape(band_rows, width, dim)


def solution(mesh):
    return jax.shard_map(
        on_device,
        mesh=mesh,
        in_specs=(
            P(("slide", "col"), None, None),
            P(("slide", "col"), None),
            P(),
            P(),
            P(),
            P(),
            P(),
            P(),
            P(),
            P(),
        ),
        out_specs=P(("slide", "col"), None, None),
        check_vma=False,
    )
```

```python
import functools

import jax
import jax.numpy as jnp
from jax import lax
from jax.experimental import pallas as pl
from jax.experimental.pallas import tpu as pltpu
from jax.sharding import PartitionSpec as P

HEADS = 8
NO_SCORE = -1e30
F32 = jnp.float32
BF16 = jnp.bfloat16
VMEM = pltpu.VMEM


def dot_nt(a, b):
    return lax.dot_general(a, b, (((1,), (1,)), ((), ())), preferred_element_type=F32)


def dot_nn(a, b):
    return lax.dot_general(a, b, (((1,), (0,)), ((), ())), preferred_element_type=F32)


def head_tokens(pair, half, scale):
    lane = lax.broadcasted_iota(jnp.int32, pair.shape, 1)
    mine = (lane >= 64) if half else (lane < 64)
    return jnp.where(mine, pair.astype(F32) * scale, 0.0).astype(BF16)


def chunk_of_device():
    place = lax.axis_index("col")
    return (place & 1) * 2 + ((place >> 1) & 1)


def chunk_state(index, own, scale, keys, vals, tissue, other_tissue, agents):
    lines = []
    for grid in (tissue, other_tissue):
        bias = jnp.where(grid[...] > 0, 0.0, NO_SCORE).astype(F32)
        lines += [bias[row : row + 1] for row in range(bias.shape[0])]
    bias_line = jnp.concatenate(lines, axis=1)
    lanes = pl.ds(pl.multiple_of(((own % 2) ^ index) * 128, 128), 128)
    pair_agents = agents[:, pl.ds(pl.multiple_of((own ^ index) * 128, 128), 128)]
    both = [dot_nt(head_tokens(pair_agents, half, scale), keys[:, lanes]) + bias_line for half in range(2)]
    done = []
    for scores in both:
        peak = jnp.max(scores, axis=1, keepdims=True)
        expo = jnp.exp(scores - peak)
        total = jnp.sum(expo, axis=1, keepdims=True)
        done.append((peak, total, dot_nn(expo.astype(BF16), vals[:, lanes])))
    lane = lax.broadcasted_iota(jnp.int32, done[0][2].shape, 1)
    weighted = jnp.where(lane < 64, done[0][2], done[1][2]).T
    stats = jnp.zeros(weighted.T.shape, F32)
    for at, value in enumerate(done[0][:2] + done[1][:2]):
        stats = jnp.where(lane == at, value, stats)
    stats = stats.T
    sides = []
    for at in range(2):
        sides.append((stats[2 * at : 2 * at + 1], stats[2 * at + 1 : 2 * at + 2], weighted[64 * at : 64 * at + 64]))
    return tuple(jnp.concatenate(pair, axis=1) for pair in zip(*sides))


def band_kernel(
    scale, own_ref, mine, other, tissue, other_tissue, w_key, w_value, agents, after, values, keys, vals, payload
):
    tokens = mine.shape[0]
    block = 256
    own = own_ref[0]
    half_lanes = pl.ds(pl.multiple_of((own // 2) * 256, 256), 256)
    key_half = w_key[:, half_lanes]
    value_half = w_value[:, half_lanes]
    for at in range(0, tokens, block):
        rows = pl.ds(at, block)
        part = mine[rows, :]
        keys[rows, :] = dot_nn(part, key_half).astype(BF16)
        values[rows, :] = dot_nn(part, w_value[...]).astype(BF16)
        vals[rows, :] = values[rows, half_lanes]
    for at in range(0, tokens, block):
        rows = pl.ds(tokens + at, block)
        part = other[pl.ds(at, block), :]
        keys[rows, :] = dot_nn(part, key_half).astype(BF16)
        vals[rows, :] = dot_nn(part, value_half).astype(BF16)
    put_narrow(payload, chunk_state(1, own, scale, keys, vals, tissue, other_tissue, agents))


def second_band_kernel(scale, own_ref, keys, vals, tissue, other_tissue, agents, keep):
    put_wide(keep, chunk_state(0, own_ref[0], scale, keys, vals, tissue, other_tissue, agents))


def merge(first, second):
    peak_1, total_1, weighted_1 = first
    peak_2, total_2, weighted_2 = second
    peak = jnp.maximum(peak_1, peak_2)
    factor_1 = jnp.exp(peak_1 - peak)
    factor_2 = jnp.exp(peak_2 - peak)
    return peak, total_1 * factor_1 + total_2 * factor_2, weighted_1 * factor_1 + weighted_2 * factor_2


def wide(ref, index=None):
    array = ref[...] if index is None else ref[index]
    return array[64:65], array[65:66], array[0:64]


def thirds(value):
    high = value.astype(BF16).astype(F32)
    rest = value - high
    middle = rest.astype(BF16).astype(F32)
    return high, middle, rest - middle


def put_wide(ref, state):
    peak, total, weighted = state
    row_id = lax.broadcasted_iota(jnp.int32, (8, weighted.shape[1]), 0)
    ref[0:64] = weighted
    ref[64:72] = jnp.where(row_id == 0, peak, jnp.where(row_id == 1, total, 0.0))


def put_narrow(ref, state):
    peak, total, weighted = state
    row_id = lax.broadcasted_iota(jnp.int32, (16, weighted.shape[1]), 0)
    stats = jnp.zeros((16, weighted.shape[1]), F32)
    for at, part in enumerate(thirds(peak) + thirds(total)):
        stats = jnp.where(row_id == at, part, stats)
    ref[0:64] = weighted.astype(BF16)
    ref[64:80] = stats.astype(BF16)


def narrow(ref):
    stats = ref[64:80].astype(F32)
    peak = stats[0:1] + stats[1:2] + stats[2:3]
    total = stats[3:4] + stats[4:5] + stats[5:6]
    return peak, total, ref[0:64].astype(F32)


def next_merge_kernel(held, got, before, own, payload):
    state = merge(wide(held), narrow(got))
    put_narrow(payload, state)
    put_wide(own, state)


def last_merge_kernel(held, got, before, agent_values):
    _, total, weighted = merge(wide(held), narrow(got))
    agent_values[...] = (weighted / total).astype(BF16)


def token_kernel(scale, patches, w_query, agents, after, weights, queries):
    heads = weights.shape[1] // agents.shape[0]
    queries[...] = dot_nn(patches[...], w_query[...]).astype(BF16)

    def scores_of(head):
        lanes = slice(head // 2 * 128, head // 2 * 128 + 128)
        return dot_nt(queries[:, lanes], head_tokens(agents[:, lanes], head % 2, scale))

    ahead = scores_of(0)
    for head in range(heads):
        scores = ahead
        if head + 1 < heads:
            ahead = scores_of(head + 1)
        expo = jnp.exp(scores - jnp.max(scores, axis=1, keepdims=True))
        part = expo * (1.0 / jnp.sum(expo, axis=1, keepdims=True))
        weights[:, head * 256 : head * 256 + 256] = part.astype(BF16)


def border_kernel(odd_ref, values, after, border):
    rows = border.shape[0]
    border[...] = values[pl.ds(pl.multiple_of(odd_ref[0] * (values.shape[0] - rows), 128), rows), :]


def halo_kernel(odd_ref, other, outer, w_value, above, below):
    rows = outer.shape[0]
    odd = odd_ref[0] == 1
    inner_part = other[pl.ds(pl.multiple_of(odd_ref[0] * (other.shape[0] - rows), 128), rows), :]
    inner = dot_nn(inner_part, w_value[...]).astype(BF16)
    above[...] = jnp.where(odd, inner, outer[...])
    below[...] = jnp.where(odd, outer[...], inner)


TAP_COUNTS = (2, 2, 2, 2, 2, 2, 2, 2, 1)


def split_rows(rows):
    return [
        [rows[at] - rows[at + 1] for at in range(0, len(rows) - 1, 2)],
        [rows[at + 1] for at in range(0, len(rows) - 1, 2)],
        [rows[at + 2] - rows[at + 1] for at in range(0, len(rows) - 2, 2)],
    ]


def split_taps(taps):
    even, odd = taps[0::2], taps[1::2]
    both = [even[at] + odd[at] if at < len(odd) else even[at] for at in range(len(even))]
    return [even, both, odd]


def joined_rows(first, second, third):
    return [row for a, b, c in zip(first, second, third) for row in (a + b, b + c)]


def taps_kernel(seven, five, three, taps, mark):
    mark[...] = jnp.zeros_like(mark)
    for q in range(7):
        column = [seven[p, q : q + 1, :] for p in range(7)]
        if 1 <= q <= 5:
            column[1:6] = [tap + five[p, q - 1 : q, :] for p, tap in enumerate(column[1:6])]
        if 2 <= q <= 4:
            column[2:5] = [tap + three[p, q - 2 : q - 1, :] for p, tap in enumerate(column[2:5])]
        parts = [tap for part in split_taps(column) for piece in split_taps(part) for tap in piece]
        parts += [jnp.zeros_like(parts[0])] * (taps.shape[1] - len(parts))
        taps[q] = jnp.concatenate(parts, axis=0)


def conv_kernel(first_lane, values, above, below, all_taps, after, position, points, taps):
    width = position.shape[1]
    lanes, step = 128, 16
    tap_count = sum(TAP_COUNTS)
    zero = jnp.zeros((8, lanes), F32)
    for group in range(position.shape[2] // lanes):
        here = slice(first_lane + group * lanes, first_lane + (group + 1) * lanes)
        there = slice(group * lanes, (group + 1) * lanes)
        for q in range(7):
            for at in range(tap_count):
                taps[q, at] = jnp.broadcast_to(all_taps[q, at : at + 1, here], (8, lanes))
        for at in range(points.shape[0]):
            points[at, 0:8, :] = zero
            points[at, 8 + width : 16 + width, :] = zero
        for at in range(0, width, step):
            rows = []
            for ref in (above, values, below):
                for row in range(0, ref.shape[0], width):
                    rows.append(ref[row + at : row + at + step, here].astype(F32))
            even, odd = rows[0::2], rows[1::2]
            streams = (
                [a - b for a, b in zip(even, odd)],
                odd,
                [a - b for a, b in zip(even[1:], odd)],
            )
            parts = [plane for stream in streams for piece in split_rows(stream) for plane in piece]
            for index, plane in enumerate(parts):
                points[index, 8 + at : 8 + at + step, :] = plane
        for at in range(0, width, step):
            columns = (at, at + 8)
            sums = [[[zero, zero] for _ in TAP_COUNTS] for _ in columns]
            for q in range(7):
                first_point = first_tap = 0
                for piece, count in enumerate(TAP_COUNTS):
                    tap = [taps[q, first_tap + k] for k in range(count)]
                    for total, column in zip(sums, columns):
                        start = column + 5 + q
                        point = [points[first_point + k, start : start + 8, :] for k in range(count + 1)]
                        for out in range(2):
                            for k in range(count):
                                total[piece][out] = total[piece][out] + point[out + k] * tap[k]
                    first_point += count + 1
                    first_tap += count
            for total, column in zip(sums, columns):
                thirds_of = [joined_rows(*total[3 * part : 3 * part + 3]) for part in range(3)]
                for row, plane in enumerate(joined_rows(*thirds_of)):
                    position[row, column : column + 8, there] = plane


def out_kernel(
    own_ref, weights_low, weights_high, own, near, side, far, position_low, position_high, w_out, mixed, spread, buffer, sems
):
    spread[...] = jnp.zeros_like(spread)
    for index, part in enumerate((own, near, side, far)):
        chunk = index ^ own_ref[0]
        group, place = chunk // 2, chunk % 2
        for half in range(2):
            rows = pl.ds(pl.multiple_of(place * 128 + half * 64, 64), 64)
            cols = pl.ds(pl.multiple_of(place * 512 + half * 256, 256), 256)
            spread[group, rows, cols] = part[:, half * 256 : half * 256 + 256]
    tokens = mixed.shape[0]
    block = tokens // 2
    copies = []
    for index in range(2):
        here = slice(index * block, index * block + block)
        blended = []
        for group, (weights, position) in enumerate(((weights_low, position_low), (weights_high, position_high))):
            attended = dot_nt(weights[here, :], spread[group])
            blended.append((attended + position[here, :]).astype(BF16))
        buffer[here, :] = dot_nn(jnp.concatenate(blended, axis=1), w_out[...]).astype(BF16)
        copies.append(pltpu.make_async_copy(buffer.at[here, :], mixed.at[here, :], sems.at[index]))
        copies[-1].start()
    for copy in copies:
        copy.wait()


def params(megabytes=48):
    return pltpu.CompilerParams(vmem_limit_bytes=megabytes << 20)


def cost(flops, moved, exps=0):
    return pl.CostEstimate(flops=int(flops), bytes_accessed=int(moved), transcendentals=int(exps))


def shape(dims, dtype):
    return jax.ShapeDtypeStruct(dims, dtype)


def exchange(x, bit):
    peers = lax.axis_size("col")
    return lax.ppermute(x, "col", [(i, i ^ bit) for i in range(peers)])


def on_device(patches, tissue, w_query, w_key, w_value, w_out, agent_tokens, seven, five, three):
    band_rows, width, dim = patches.shape
    tokens = band_rows * width
    agents = agent_tokens.shape[0]
    half_dim = dim // 2
    scale = (dim // HEADS) ** (-0.5)
    flat = patches.reshape(tokens, dim)
    peers = lax.axis_size("col")
    place = lax.axis_index("col")
    odd = place % 2
    odd_word = jnp.reshape(odd, (1,)).astype(jnp.int32)
    own_chunk = jnp.reshape(chunk_of_device(), (1,)).astype(jnp.int32)
    smem = pl.BlockSpec(memory_space=pltpu.SMEM)
    vmem = pl.BlockSpec(memory_space=VMEM)
    anywhere = pl.BlockSpec(memory_space=pl.ANY)

    other = exchange(flat, 1)
    other_tissue = exchange(tissue, 1)

    taps, mark = pl.pallas_call(
        taps_kernel,
        out_shape=(shape((7, 24, dim), F32), shape((8, 128), F32)),
        in_specs=[vmem] * 3,
        out_specs=[vmem] * 2,
        compiler_params=params(60),
        cost_estimate=cost(1e10, 1e6),
        name="taps",
    )(seven, five, three)

    wide_shape, narrow_shape = shape((72, 512), F32), shape((80, 512), BF16)
    both_bands = shape((2 * tokens, half_dim), BF16)
    values, keys, vals, payload = pl.pallas_call(
        functools.partial(band_kernel, scale),
        out_shape=(shape((tokens, dim), BF16), both_bands, both_bands, narrow_shape),
        in_specs=[smem] + [vmem] * 7 + [anywhere],
        out_specs=[vmem] * 4,
        compiler_params=params(20),
        cost_estimate=cost(1.8e9, 4e6, 1e6),
        name="band",
    )(own_chunk, flat, other, tissue, other_tissue, w_key, w_value, agent_tokens, mark)

    def token(at, after):
        lanes = slice(at * half_dim, (at + 1) * half_dim)
        return pl.pallas_call(
            functools.partial(token_kernel, scale),
            out_shape=shape((tokens, HEADS // 2 * agents), BF16),
            grid=(1,),
            in_specs=[
                vmem,
                pl.BlockSpec((dim, half_dim), lambda i: (0, at)),
                pl.BlockSpec((agents, half_dim), lambda i: (0, at)),
                anywhere,
            ],
            out_specs=vmem,
            scratch_shapes=[VMEM((tokens, half_dim), BF16)],
            compiler_params=params(20),
            cost_estimate=cost((1 + 4 * at) * 2e9, 6e6, 1e6),
            name="token",
        )(flat, w_query, agent_tokens, after)

    def conv(at, after):
        return pl.pallas_call(
            functools.partial(conv_kernel, at * half_dim),
            out_shape=shape((band_rows, width, half_dim), F32),
            in_specs=[vmem] * 4 + [anywhere],
            out_specs=vmem,
            scratch_shapes=[
                VMEM((sum(TAP_COUNTS) + len(TAP_COUNTS), width + 16, 128), F32),
                VMEM((7, sum(TAP_COUNTS), 8, 128), F32),
            ],
            compiler_params=params(20),
            cost_estimate=cost(3e9, 4e6),
            name="conv",
        )(values, above, below, taps, after).reshape(tokens, half_dim)

    hop = dict(in_specs=[vmem, vmem, anywhere], compiler_params=params(16), cost_estimate=cost(1e6, 1e6))

    def next_merge(held, got, before):
        return pl.pallas_call(
            next_merge_kernel, out_shape=(wide_shape, narrow_shape), out_specs=[vmem] * 2, name="merge_next", **hop
        )(held, got, before)

    got = exchange(payload, 2)
    held = pl.pallas_call(
        functools.partial(second_band_kernel, scale),
        out_shape=wide_shape,
        in_specs=[smem] + [vmem] * 5,
        out_specs=vmem,
        compiler_params=params(20),
        cost_estimate=cost(6e8, 4e6, 1e6),
        name="band_second",
    )(own_chunk, keys, vals, tissue, other_tissue, agent_tokens)
    weights_low = token(0, payload)
    held, payload = next_merge(held, got, weights_low)
    border = pl.pallas_call(
        border_kernel,
        out_shape=shape((3 * width, dim), BF16),
        in_specs=[smem, vmem, anywhere],
        out_specs=vmem,
        compiler_params=params(16),
        cost_estimate=cost(3e9, 1e6),
        name="border",
    )(odd_word, values, payload)
    rest = [(i, i + 1) for i in range(1, peers - 1, 2)]
    outer = lax.ppermute(border, "col", rest + [(j, i) for i, j in rest])
    bit = 4
    while bit * 2 < peers:
        got = exchange(payload, bit)
        held, payload = next_merge(held, got, border)
        bit *= 2
    got = exchange(payload, bit)
    weights_high = token(1, payload)
    above, below = pl.pallas_call(
        halo_kernel,
        out_shape=(shape((3 * width, dim), BF16), shape((3 * width, dim), BF16)),
        in_specs=[smem] + [vmem] * 3,
        out_specs=[vmem] * 2,
        compiler_params=params(16),
        cost_estimate=cost(4e8, 2e6),
        name="halo",
    )(odd_word, other, outer, w_value)
    position_low = conv(0, weights_high)
    own = pl.pallas_call(
        last_merge_kernel, out_shape=shape((64, 512), BF16), out_specs=vmem, name="merge_last", **hop
    )(held, got, position_low)
    near = exchange(own, 2)
    far = exchange(own, 3)
    side = exchange(own, 1)
    position_high = conv(1, own)

    mixed = pl.pallas_call(
        out_kernel,
        out_shape=shape((tokens, dim), BF16),
        in_specs=[smem] + [vmem] * 9,
        out_specs=anywhere,
        scratch_shapes=[
            VMEM((2, 256, 1024), BF16),
            VMEM((tokens, dim), BF16),
            pltpu.SemaphoreType.DMA((2,)),
        ],
        compiler_params=params(20),
        cost_estimate=cost(1.1e9, 8e6),
        name="out",
    )(own_chunk, weights_low, weights_high, own, near, side, far, position_low, position_high, w_out)
    return mixed.reshape(band_rows, width, dim)


def solution(mesh):
    return jax.shard_map(
        on_device,
        mesh=mesh,
        in_specs=(
            P(("slide", "col"), None, None),
            P(("slide", "col"), None),
            P(),
            P(),
            P(),
            P(),
            P(),
            P(),
            P(),
            P(),
        ),
        out_specs=P(("slide", "col"), None, None),
        check_vma=False,
    )
```

```python
import functools

import jax
import jax.numpy as jnp
from jax import lax
from jax.experimental import pallas as pl
from jax.experimental.pallas import tpu as pltpu
from jax.sharding import PartitionSpec as P

HEADS = 8
NO_SCORE = -1e30
F32 = jnp.float32
BF16 = jnp.bfloat16
VMEM = pltpu.VMEM


def dot_nt(a, b):
    return lax.dot_general(a, b, (((1,), (1,)), ((), ())), preferred_element_type=F32)


def dot_nn(a, b):
    return lax.dot_general(a, b, (((1,), (0,)), ((), ())), preferred_element_type=F32)


def head_tokens(pair, half, scale):
    lane = lax.broadcasted_iota(jnp.int32, pair.shape, 1)
    mine = (lane >= 64) if half else (lane < 64)
    return jnp.where(mine, pair.astype(F32) * scale, 0.0).astype(BF16)


def chunk_of_device():
    place = lax.axis_index("col")
    return (place & 1) * 2 + ((place >> 1) & 1)


def chunk_state(index, own, scale, keys, vals, tissue, other_tissue, agents):
    lines = []
    for grid in (tissue, other_tissue):
        bias = jnp.where(grid[...] > 0, 0.0, NO_SCORE).astype(F32)
        lines += [bias[row : row + 1] for row in range(bias.shape[0])]
    bias_line = jnp.concatenate(lines, axis=1)
    lanes = pl.ds(pl.multiple_of(((own % 2) ^ index) * 128, 128), 128)
    pair_agents = agents[:, pl.ds(pl.multiple_of((own ^ index) * 128, 128), 128)]
    both = [dot_nt(head_tokens(pair_agents, half, scale), keys[:, lanes]) + bias_line for half in range(2)]
    done = []
    for scores in both:
        peak = jnp.max(scores, axis=1, keepdims=True)
        expo = jnp.exp(scores - peak)
        total = jnp.sum(expo, axis=1, keepdims=True)
        done.append((peak, total, dot_nn(expo.astype(BF16), vals[:, lanes])))
    lane = lax.broadcasted_iota(jnp.int32, done[0][2].shape, 1)
    weighted = jnp.where(lane < 64, done[0][2], done[1][2]).T
    stats = jnp.zeros(weighted.T.shape, F32)
    for at, value in enumerate(done[0][:2] + done[1][:2]):
        stats = jnp.where(lane == at, value, stats)
    stats = stats.T
    sides = []
    for at in range(2):
        sides.append((stats[2 * at : 2 * at + 1], stats[2 * at + 1 : 2 * at + 2], weighted[64 * at : 64 * at + 64]))
    return tuple(jnp.concatenate(pair, axis=1) for pair in zip(*sides))


def project_kernel(own_ref, mine, other, w_key, w_value, values, keys, vals):
    tokens = mine.shape[0]
    block = 256
    half_lanes = pl.ds(pl.multiple_of((own_ref[0] // 2) * 256, 256), 256)
    key_half = w_key[:, half_lanes]
    value_half = w_value[:, half_lanes]
    for at in range(0, tokens, block):
        rows = pl.ds(at, block)
        part = mine[rows, :]
        keys[rows, :] = dot_nn(part, key_half).astype(BF16)
        values[rows, :] = dot_nn(part, w_value[...]).astype(BF16)
        vals[rows, :] = values[rows, half_lanes]
    for at in range(0, tokens, block):
        rows = pl.ds(tokens + at, block)
        part = other[pl.ds(at, block), :]
        keys[rows, :] = dot_nn(part, key_half).astype(BF16)
        vals[rows, :] = dot_nn(part, value_half).astype(BF16)


def first_band_kernel(scale, own_ref, keys, vals, tissue, other_tissue, agents, payload):
    put_narrow(payload, chunk_state(1, own_ref[0], scale, keys, vals, tissue, other_tissue, agents))


def second_band_kernel(scale, own_ref, keys, vals, tissue, other_tissue, agents, keep):
    put_wide(keep, chunk_state(0, own_ref[0], scale, keys, vals, tissue, other_tissue, agents))


def merge(first, second):
    peak_1, total_1, weighted_1 = first
    peak_2, total_2, weighted_2 = second
    peak = jnp.maximum(peak_1, peak_2)
    factor_1 = jnp.exp(peak_1 - peak)
    factor_2 = jnp.exp(peak_2 - peak)
    return peak, total_1 * factor_1 + total_2 * factor_2, weighted_1 * factor_1 + weighted_2 * factor_2


def wide(ref, index=None):
    array = ref[...] if index is None else ref[index]
    return array[64:65], array[65:66], array[0:64]


def thirds(value):
    high = value.astype(BF16).astype(F32)
    rest = value - high
    middle = rest.astype(BF16).astype(F32)
    return high, middle, rest - middle


def put_wide(ref, state):
    peak, total, weighted = state
    row_id = lax.broadcasted_iota(jnp.int32, (8, weighted.shape[1]), 0)
    ref[0:64] = weighted
    ref[64:72] = jnp.where(row_id == 0, peak, jnp.where(row_id == 1, total, 0.0))


def put_narrow(ref, state):
    peak, total, weighted = state
    row_id = lax.broadcasted_iota(jnp.int32, (16, weighted.shape[1]), 0)
    stats = jnp.zeros((16, weighted.shape[1]), F32)
    for at, part in enumerate(thirds(peak) + thirds(total)):
        stats = jnp.where(row_id == at, part, stats)
    ref[0:64] = weighted.astype(BF16)
    ref[64:80] = stats.astype(BF16)


def narrow(ref):
    stats = ref[64:80].astype(F32)
    peak = stats[0:1] + stats[1:2] + stats[2:3]
    total = stats[3:4] + stats[4:5] + stats[5:6]
    return peak, total, ref[0:64].astype(F32)


def next_merge_kernel(held, got, before, own, payload):
    state = merge(wide(held), narrow(got))
    put_narrow(payload, state)
    put_wide(own, state)


def last_merge_kernel(held, got, before, agent_values):
    _, total, weighted = merge(wide(held), narrow(got))
    agent_values[...] = (weighted / total).astype(BF16)


def token_kernel(scale, patches, w_query, agents, after, weights, queries):
    heads = weights.shape[1] // agents.shape[0]
    queries[...] = dot_nn(patches[...], w_query[...]).astype(BF16)

    def scores_of(head):
        lanes = slice(head // 2 * 128, head // 2 * 128 + 128)
        return dot_nt(queries[:, lanes], head_tokens(agents[:, lanes], head % 2, scale))

    ahead = scores_of(0)
    for head in range(heads):
        scores = ahead
        if head + 1 < heads:
            ahead = scores_of(head + 1)
        expo = jnp.exp(scores - jnp.max(scores, axis=1, keepdims=True))
        part = expo * (1.0 / jnp.sum(expo, axis=1, keepdims=True))
        weights[:, head * 256 : head * 256 + 256] = part.astype(BF16)


def border_kernel(odd_ref, flat, border, sem):
    rows = border.shape[0]
    start = pl.multiple_of(odd_ref[0] * (flat.shape[0] - rows), 128)
    copy = pltpu.make_async_copy(flat.at[pl.ds(start, rows), :], border, sem)
    copy.start()
    copy.wait()


def halo_kernel(odd_ref, other, outer, w_value, after, above, below):
    rows = outer.shape[0]
    odd = odd_ref[0] == 1
    inner_part = other[pl.ds(pl.multiple_of(odd_ref[0] * (other.shape[0] - rows), 128), rows), :]
    inner = dot_nn(inner_part, w_value[...]).astype(BF16)
    outside = dot_nn(outer[...], w_value[...]).astype(BF16)
    above[...] = jnp.where(odd, inner, outside)
    below[...] = jnp.where(odd, outside, inner)


def relay_kernel(near, after, again):
    again[...] = near[...]


TAP_COUNTS = (2, 2, 2, 2, 2, 2, 2, 2, 1)


def split_rows(rows):
    return [
        [rows[at] - rows[at + 1] for at in range(0, len(rows) - 1, 2)],
        [rows[at + 1] for at in range(0, len(rows) - 1, 2)],
        [rows[at + 2] - rows[at + 1] for at in range(0, len(rows) - 2, 2)],
    ]


def split_taps(taps):
    even, odd = taps[0::2], taps[1::2]
    both = [even[at] + odd[at] if at < len(odd) else even[at] for at in range(len(even))]
    return [even, both, odd]


def joined_rows(first, second, third):
    return [row for a, b, c in zip(first, second, third) for row in (a + b, b + c)]


def taps_kernel(seven, five, three, after, taps):
    for q in range(7):
        column = [seven[p, q : q + 1, :] for p in range(7)]
        if 1 <= q <= 5:
            column[1:6] = [tap + five[p, q - 1 : q, :] for p, tap in enumerate(column[1:6])]
        if 2 <= q <= 4:
            column[2:5] = [tap + three[p, q - 2 : q - 1, :] for p, tap in enumerate(column[2:5])]
        parts = [tap for part in split_taps(column) for piece in split_taps(part) for tap in piece]
        parts += [jnp.zeros_like(parts[0])] * (taps.shape[1] - len(parts))
        taps[q] = jnp.concatenate(parts, axis=0)


def conv_kernel(first_lane, values, above, below, all_taps, after, position, points, taps):
    width = position.shape[1]
    lanes, step = 128, 16
    tap_count = sum(TAP_COUNTS)
    zero = jnp.zeros((8, lanes), F32)
    for group in range(position.shape[2] // lanes):
        here = slice(first_lane + group * lanes, first_lane + (group + 1) * lanes)
        there = slice(group * lanes, (group + 1) * lanes)
        for q in range(7):
            for at in range(tap_count):
                taps[q, at] = jnp.broadcast_to(all_taps[q, at : at + 1, here], (8, lanes))
        for at in range(points.shape[0]):
            points[at, 0:8, :] = zero
            points[at, 8 + width : 16 + width, :] = zero
        for at in range(0, width, step):
            rows = []
            for ref in (above, values, below):
                for row in range(0, ref.shape[0], width):
                    rows.append(ref[row + at : row + at + step, here].astype(F32))
            even, odd = rows[0::2], rows[1::2]
            streams = (
                [a - b for a, b in zip(even, odd)],
                odd,
                [a - b for a, b in zip(even[1:], odd)],
            )
            parts = [plane for stream in streams for piece in split_rows(stream) for plane in piece]
            for index, plane in enumerate(parts):
                points[index, 8 + at : 8 + at + step, :] = plane
        for at in range(0, width, step):
            columns = (at, at + 8)
            sums = [[[zero, zero] for _ in TAP_COUNTS] for _ in columns]
            for q in range(7):
                first_point = first_tap = 0
                for piece, count in enumerate(TAP_COUNTS):
                    tap = [taps[q, first_tap + k] for k in range(count)]
                    for total, column in zip(sums, columns):
                        start = column + 5 + q
                        point = [points[first_point + k, start : start + 8, :] for k in range(count + 1)]
                        for out in range(2):
                            for k in range(count):
                                total[piece][out] = total[piece][out] + point[out + k] * tap[k]
                    first_point += count + 1
                    first_tap += count
            for total, column in zip(sums, columns):
                thirds_of = [joined_rows(*total[3 * part : 3 * part + 3]) for part in range(3)]
                for row, plane in enumerate(joined_rows(*thirds_of)):
                    position[row, column : column + 8, there] = plane


def out_kernel(
    own_ref, weights_low, weights_high, own, near, side, far, position_low, position_high, w_out, mixed, spread, buffer, sems
):
    spread[...] = jnp.zeros_like(spread)
    for index, part in enumerate((own, near, side, far)):
        chunk = index ^ own_ref[0]
        group, place = chunk // 2, chunk % 2
        for half in range(2):
            rows = pl.ds(pl.multiple_of(place * 128 + half * 64, 64), 64)
            cols = pl.ds(pl.multiple_of(place * 512 + half * 256, 256), 256)
            spread[group, rows, cols] = part[:, half * 256 : half * 256 + 256]
    tokens = mixed.shape[0]
    block = tokens // 2
    copies = []
    for index in range(2):
        here = slice(index * block, index * block + block)
        blended = []
        for group, (weights, position) in enumerate(((weights_low, position_low), (weights_high, position_high))):
            attended = dot_nt(weights[here, :], spread[group])
            blended.append((attended + position[here, :]).astype(BF16))
        buffer[here, :] = dot_nn(jnp.concatenate(blended, axis=1), w_out[...]).astype(BF16)
        copies.append(pltpu.make_async_copy(buffer.at[here, :], mixed.at[here, :], sems.at[index]))
        copies[-1].start()
    for copy in copies:
        copy.wait()


def params(megabytes=48):
    return pltpu.CompilerParams(vmem_limit_bytes=megabytes << 20)


def cost(flops, moved, exps=0):
    return pl.CostEstimate(flops=int(flops), bytes_accessed=int(moved), transcendentals=int(exps))


def shape(dims, dtype):
    return jax.ShapeDtypeStruct(dims, dtype)


def exchange(x, bit):
    peers = lax.axis_size("col")
    return lax.ppermute(x, "col", [(i, i ^ bit) for i in range(peers)])


def on_device(patches, tissue, w_query, w_key, w_value, w_out, agent_tokens, seven, five, three):
    band_rows, width, dim = patches.shape
    tokens = band_rows * width
    agents = agent_tokens.shape[0]
    half_dim = dim // 2
    scale = (dim // HEADS) ** (-0.5)
    flat = patches.reshape(tokens, dim)
    peers = lax.axis_size("col")
    place = lax.axis_index("col")
    odd = place % 2
    odd_word = jnp.reshape(odd, (1,)).astype(jnp.int32)
    own_chunk = jnp.reshape(chunk_of_device(), (1,)).astype(jnp.int32)
    smem = pl.BlockSpec(memory_space=pltpu.SMEM)
    vmem = pl.BlockSpec(memory_space=VMEM)
    anywhere = pl.BlockSpec(memory_space=pl.ANY)

    other = exchange(flat, 1)
    other_tissue = exchange(tissue, 1)

    border = pl.pallas_call(
        border_kernel,
        out_shape=shape((3 * width, dim), BF16),
        in_specs=[smem, anywhere],
        out_specs=anywhere,
        scratch_shapes=[pltpu.SemaphoreType.DMA],
        compiler_params=params(60),
        cost_estimate=cost(1e10, 1e6),
        name="border",
    )(odd_word, flat)
    rest = [(i, i + 1) for i in range(1, peers - 1, 2)]
    outer = lax.ppermute(border, "col", rest + [(j, i) for i, j in rest])

    wide_shape, narrow_shape = shape((72, 512), F32), shape((80, 512), BF16)
    both_bands = shape((2 * tokens, half_dim), BF16)
    values, keys, vals = pl.pallas_call(
        project_kernel,
        out_shape=(shape((tokens, dim), BF16), both_bands, both_bands),
        in_specs=[smem] + [vmem] * 4,
        out_specs=[vmem] * 3,
        compiler_params=params(20),
        cost_estimate=cost(1.3e9, 4e6),
        name="project",
    )(own_chunk, flat, other, w_key, w_value)

    def band(kernel, out_shape):
        return pl.pallas_call(
            functools.partial(kernel, scale),
            out_shape=out_shape,
            in_specs=[smem] + [vmem] * 5,
            out_specs=vmem,
            compiler_params=params(20),
            cost_estimate=cost(6e8, 4e6, 1e6),
            name="band",
        )(own_chunk, keys, vals, tissue, other_tissue, agent_tokens)

    payload = band(first_band_kernel, narrow_shape)

    def token(at, after):
        lanes = slice(at * half_dim, (at + 1) * half_dim)
        return pl.pallas_call(
            functools.partial(token_kernel, scale),
            out_shape=shape((tokens, HEADS // 2 * agents), BF16),
            grid=(1,),
            in_specs=[
                vmem,
                pl.BlockSpec((dim, half_dim), lambda i: (0, at)),
                pl.BlockSpec((agents, half_dim), lambda i: (0, at)),
                anywhere,
            ],
            out_specs=vmem,
            scratch_shapes=[VMEM((tokens, half_dim), BF16)],
            compiler_params=params(20),
            cost_estimate=cost(2e9, 6e6, 1e6),
            name="token",
        )(flat, w_query, agent_tokens, after)

    def conv(at, after):
        return pl.pallas_call(
            functools.partial(conv_kernel, at * half_dim),
            out_shape=shape((band_rows, width, half_dim), F32),
            in_specs=[vmem] * 4 + [anywhere],
            out_specs=vmem,
            scratch_shapes=[
                VMEM((sum(TAP_COUNTS) + len(TAP_COUNTS), width + 16, 128), F32),
                VMEM((7, sum(TAP_COUNTS), 8, 128), F32),
            ],
            compiler_params=params(20),
            cost_estimate=cost(3e9, 4e6),
            name="conv",
        )(values, above, below, taps, after).reshape(tokens, half_dim)

    hop = dict(in_specs=[vmem, vmem, anywhere], compiler_params=params(16), cost_estimate=cost(1e6, 1e6))

    def next_merge(held, got, before):
        return pl.pallas_call(
            next_merge_kernel, out_shape=(wide_shape, narrow_shape), out_specs=[vmem] * 2, name="merge_next", **hop
        )(held, got, before)

    got = exchange(payload, 2)
    held = band(second_band_kernel, wide_shape)
    taps = pl.pallas_call(
        taps_kernel,
        out_shape=shape((7, 24, dim), F32),
        in_specs=[vmem] * 3 + [anywhere],
        out_specs=vmem,
        compiler_params=params(16),
        cost_estimate=cost(5e8, 1e6),
        name="taps",
    )(seven, five, three, payload)
    held, payload = next_merge(held, got, taps)
    bit = 4
    weights_low = None
    while bit * 2 < peers:
        got = exchange(payload, bit)
        if weights_low is None:
            weights_low = token(0, payload)
            above, below = pl.pallas_call(
                halo_kernel,
                out_shape=(shape((3 * width, dim), BF16), shape((3 * width, dim), BF16)),
                in_specs=[smem] + [vmem] * 3 + [anywhere],
                out_specs=[vmem] * 2,
                compiler_params=params(16),
                cost_estimate=cost(4e8, 2e6),
                name="halo",
            )(odd_word, other, outer, w_value, weights_low)
        held, payload = next_merge(held, got, weights_low)
        bit *= 2
    got = exchange(payload, bit)
    weights_high = token(1, payload)
    position_low = conv(0, weights_high)
    own = pl.pallas_call(
        last_merge_kernel, out_shape=shape((64, 512), BF16), out_specs=vmem, name="merge_last", **hop
    )(held, got, position_low)
    near = exchange(own, 2)
    side = exchange(own, 1)
    position_high = conv(1, own)
    again = pl.pallas_call(
        relay_kernel,
        out_shape=shape((64, 512), BF16),
        in_specs=[vmem, anywhere],
        out_specs=vmem,
        compiler_params=params(16),
        cost_estimate=cost(1e6, 1e6),
        name="relay",
    )(near, position_high)
    far = exchange(again, 1)

    mixed = pl.pallas_call(
        out_kernel,
        out_shape=shape((tokens, dim), BF16),
        in_specs=[smem] + [vmem] * 9,
        out_specs=anywhere,
        scratch_shapes=[
            VMEM((2, 256, 1024), BF16),
            VMEM((tokens, dim), BF16),
            pltpu.SemaphoreType.DMA((2,)),
        ],
        compiler_params=params(20),
        cost_estimate=cost(1.1e9, 8e6),
        name="out",
    )(own_chunk, weights_low, weights_high, own, near, side, far, position_low, position_high, w_out)
    return mixed.reshape(band_rows, width, dim)


def solution(mesh):
    return jax.shard_map(
        on_device,
        mesh=mesh,
        in_specs=(
            P(("slide", "col"), None, None),
            P(("slide", "col"), None),
            P(),
            P(),
            P(),
            P(),
            P(),
            P(),
            P(),
            P(),
        ),
        out_specs=P(("slide", "col"), None, None),
        check_vma=False,
    )
```

```python
import functools

import jax
import jax.numpy as jnp
from jax import lax
from jax.experimental import pallas as pl
from jax.experimental.pallas import tpu as pltpu
from jax.sharding import PartitionSpec as P

HEADS = 8
NO_SCORE = -1e30
F32 = jnp.float32
BF16 = jnp.bfloat16
VMEM = pltpu.VMEM


def dot_nt(a, b):
    return lax.dot_general(a, b, (((1,), (1,)), ((), ())), preferred_element_type=F32)


def dot_nn(a, b):
    return lax.dot_general(a, b, (((1,), (0,)), ((), ())), preferred_element_type=F32)


def head_tokens(pair, half, scale):
    lane = lax.broadcasted_iota(jnp.int32, pair.shape, 1)
    mine = (lane >= 64) if half else (lane < 64)
    return jnp.where(mine, pair.astype(F32) * scale, 0.0).astype(BF16)


def chunk_of_device():
    place = lax.axis_index("col")
    return (place & 1) * 2 + ((place >> 1) & 1)


def chunk_state(index, own, scale, keys, vals, tissue, other_tissue, agents):
    lines = []
    for grid in (tissue, other_tissue):
        bias = jnp.where(grid[...] > 0, 0.0, NO_SCORE).astype(F32)
        lines += [bias[row : row + 1] for row in range(bias.shape[0])]
    bias_line = jnp.concatenate(lines, axis=1)
    lanes = pl.ds(pl.multiple_of(((own % 2) ^ index) * 128, 128), 128)
    pair_agents = agents[:, pl.ds(pl.multiple_of((own ^ index) * 128, 128), 128)]
    both = [dot_nt(head_tokens(pair_agents, half, scale), keys[:, lanes]) + bias_line for half in range(2)]
    done = []
    for scores in both:
        peak = jnp.max(scores, axis=1, keepdims=True)
        expo = jnp.exp(scores - peak)
        total = jnp.sum(expo, axis=1, keepdims=True)
        done.append((peak, total, dot_nn(expo.astype(BF16), vals[:, lanes])))
    lane = lax.broadcasted_iota(jnp.int32, done[0][2].shape, 1)
    weighted = jnp.where(lane < 64, done[0][2], done[1][2]).T
    stats = jnp.zeros(weighted.T.shape, F32)
    for at, value in enumerate(done[0][:2] + done[1][:2]):
        stats = jnp.where(lane == at, value, stats)
    stats = stats.T
    sides = []
    for at in range(2):
        sides.append((stats[2 * at : 2 * at + 1], stats[2 * at + 1 : 2 * at + 2], weighted[64 * at : 64 * at + 64]))
    return tuple(jnp.concatenate(pair, axis=1) for pair in zip(*sides))


def project_kernel(own_ref, mine, other, w_key, w_value, values, keys, vals):
    tokens = mine.shape[0]
    block = 256
    half_lanes = pl.ds(pl.multiple_of((own_ref[0] // 2) * 256, 256), 256)
    key_half = w_key[:, half_lanes]
    value_half = w_value[:, half_lanes]
    for at in range(0, tokens, block):
        rows = pl.ds(at, block)
        part = mine[rows, :]
        keys[rows, :] = dot_nn(part, key_half).astype(BF16)
        values[rows, :] = dot_nn(part, w_value[...]).astype(BF16)
        vals[rows, :] = values[rows, half_lanes]
    for at in range(0, tokens, block):
        rows = pl.ds(tokens + at, block)
        part = other[pl.ds(at, block), :]
        keys[rows, :] = dot_nn(part, key_half).astype(BF16)
        vals[rows, :] = dot_nn(part, value_half).astype(BF16)


def first_band_kernel(scale, own_ref, keys, vals, tissue, other_tissue, agents, payload):
    put_narrow(payload, chunk_state(1, own_ref[0], scale, keys, vals, tissue, other_tissue, agents))


def second_band_kernel(scale, own_ref, keys, vals, tissue, other_tissue, agents, keep):
    put_wide(keep, chunk_state(0, own_ref[0], scale, keys, vals, tissue, other_tissue, agents))


def merge(first, second):
    peak_1, total_1, weighted_1 = first
    peak_2, total_2, weighted_2 = second
    peak = jnp.maximum(peak_1, peak_2)
    factor_1 = jnp.exp(peak_1 - peak)
    factor_2 = jnp.exp(peak_2 - peak)
    return peak, total_1 * factor_1 + total_2 * factor_2, weighted_1 * factor_1 + weighted_2 * factor_2


def wide(ref, index=None):
    array = ref[...] if index is None else ref[index]
    return array[64:65], array[65:66], array[0:64]


def thirds(value):
    high = value.astype(BF16).astype(F32)
    rest = value - high
    middle = rest.astype(BF16).astype(F32)
    return high, middle, rest - middle


def put_wide(ref, state):
    peak, total, weighted = state
    row_id = lax.broadcasted_iota(jnp.int32, (8, weighted.shape[1]), 0)
    ref[0:64] = weighted
    ref[64:72] = jnp.where(row_id == 0, peak, jnp.where(row_id == 1, total, 0.0))


def put_narrow(ref, state):
    peak, total, weighted = state
    row_id = lax.broadcasted_iota(jnp.int32, (16, weighted.shape[1]), 0)
    stats = jnp.zeros((16, weighted.shape[1]), F32)
    for at, part in enumerate(thirds(peak) + thirds(total)):
        stats = jnp.where(row_id == at, part, stats)
    ref[0:64] = weighted.astype(BF16)
    ref[64:80] = stats.astype(BF16)


def narrow(ref):
    stats = ref[64:80].astype(F32)
    peak = stats[0:1] + stats[1:2] + stats[2:3]
    total = stats[3:4] + stats[4:5] + stats[5:6]
    return peak, total, ref[0:64].astype(F32)


def next_merge_kernel(held, got, before, own, payload):
    state = merge(wide(held), narrow(got))
    put_narrow(payload, state)
    put_wide(own, state)


def last_merge_kernel(held, got, before, agent_values):
    _, total, weighted = merge(wide(held), narrow(got))
    agent_values[...] = (weighted / total).astype(BF16)


def token_kernel(scale, patches, w_query, agents, after, weights, queries):
    heads = weights.shape[1] // agents.shape[0]
    queries[...] = dot_nn(patches[...], w_query[...]).astype(BF16)

    def scores_of(head):
        lanes = slice(head // 2 * 128, head // 2 * 128 + 128)
        return dot_nt(queries[:, lanes], head_tokens(agents[:, lanes], head % 2, scale))

    ahead = scores_of(0)
    for head in range(heads):
        scores = ahead
        if head + 1 < heads:
            ahead = scores_of(head + 1)
        expo = jnp.exp(scores - jnp.max(scores, axis=1, keepdims=True))
        part = expo * (1.0 / jnp.sum(expo, axis=1, keepdims=True))
        weights[:, head * 256 : head * 256 + 256] = part.astype(BF16)


def border_kernel(odd_ref, flat, border):
    rows = border.shape[0]
    border[...] = flat[pl.ds(pl.multiple_of(odd_ref[0] * (flat.shape[0] - rows), 128), rows), :]


def halo_kernel(odd_ref, other, outer, w_value, after, above, below):
    rows = outer.shape[0]
    odd = odd_ref[0] == 1
    inner_part = other[pl.ds(pl.multiple_of(odd_ref[0] * (other.shape[0] - rows), 128), rows), :]
    inner = dot_nn(inner_part, w_value[...]).astype(BF16)
    outside = dot_nn(outer[...], w_value[...]).astype(BF16)
    above[...] = jnp.where(odd, inner, outside)
    below[...] = jnp.where(odd, outside, inner)


def relay_kernel(near, after, again):
    again[...] = near[...]


TAP_COUNTS = (2, 2, 2, 2, 2, 2, 2, 2, 1)


def split_rows(rows):
    return [
        [rows[at] - rows[at + 1] for at in range(0, len(rows) - 1, 2)],
        [rows[at + 1] for at in range(0, len(rows) - 1, 2)],
        [rows[at + 2] - rows[at + 1] for at in range(0, len(rows) - 2, 2)],
    ]


def split_taps(taps):
    even, odd = taps[0::2], taps[1::2]
    both = [even[at] + odd[at] if at < len(odd) else even[at] for at in range(len(even))]
    return [even, both, odd]


def joined_rows(first, second, third):
    return [row for a, b, c in zip(first, second, third) for row in (a + b, b + c)]


def taps_kernel(seven, five, three, after, taps):
    for q in range(7):
        column = [seven[p, q : q + 1, :] for p in range(7)]
        if 1 <= q <= 5:
            column[1:6] = [tap + five[p, q - 1 : q, :] for p, tap in enumerate(column[1:6])]
        if 2 <= q <= 4:
            column[2:5] = [tap + three[p, q - 2 : q - 1, :] for p, tap in enumerate(column[2:5])]
        parts = [tap for part in split_taps(column) for piece in split_taps(part) for tap in piece]
        parts += [jnp.zeros_like(parts[0])] * (taps.shape[1] - len(parts))
        taps[q] = jnp.concatenate(parts, axis=0)


def conv_kernel(first_lane, values, above, below, all_taps, after, position, points, taps):
    width = position.shape[1]
    lanes, step = 128, 16
    tap_count = sum(TAP_COUNTS)
    zero = jnp.zeros((8, lanes), F32)
    for group in range(position.shape[2] // lanes):
        here = slice(first_lane + group * lanes, first_lane + (group + 1) * lanes)
        there = slice(group * lanes, (group + 1) * lanes)
        for q in range(7):
            for at in range(tap_count):
                taps[q, at] = jnp.broadcast_to(all_taps[q, at : at + 1, here], (8, lanes))
        for at in range(points.shape[0]):
            points[at, 0:8, :] = zero
            points[at, 8 + width : 16 + width, :] = zero
        for at in range(0, width, step):
            rows = []
            for ref in (above, values, below):
                for row in range(0, ref.shape[0], width):
                    rows.append(ref[row + at : row + at + step, here].astype(F32))
            even, odd = rows[0::2], rows[1::2]
            streams = (
                [a - b for a, b in zip(even, odd)],
                odd,
                [a - b for a, b in zip(even[1:], odd)],
            )
            parts = [plane for stream in streams for piece in split_rows(stream) for plane in piece]
            for index, plane in enumerate(parts):
                points[index, 8 + at : 8 + at + step, :] = plane
        for at in range(0, width, step):
            columns = (at, at + 8)
            sums = [[[zero, zero] for _ in TAP_COUNTS] for _ in columns]
            for q in range(7):
                first_point = first_tap = 0
                for piece, count in enumerate(TAP_COUNTS):
                    tap = [taps[q, first_tap + k] for k in range(count)]
                    for total, column in zip(sums, columns):
                        start = column + 5 + q
                        point = [points[first_point + k, start : start + 8, :] for k in range(count + 1)]
                        for out in range(2):
                            for k in range(count):
                                total[piece][out] = total[piece][out] + point[out + k] * tap[k]
                    first_point += count + 1
                    first_tap += count
            for total, column in zip(sums, columns):
                thirds_of = [joined_rows(*total[3 * part : 3 * part + 3]) for part in range(3)]
                for row, plane in enumerate(joined_rows(*thirds_of)):
                    position[row, column : column + 8, there] = plane


def out_kernel(
    own_ref, weights_low, weights_high, own, near, side, far, position_low, position_high, w_out, mixed, spread, buffer, sems
):
    spread[...] = jnp.zeros_like(spread)
    for index, part in enumerate((own, near, side, far)):
        chunk = index ^ own_ref[0]
        group, place = chunk // 2, chunk % 2
        for half in range(2):
            rows = pl.ds(pl.multiple_of(place * 128 + half * 64, 64), 64)
            cols = pl.ds(pl.multiple_of(place * 512 + half * 256, 256), 256)
            spread[group, rows, cols] = part[:, half * 256 : half * 256 + 256]
    tokens = mixed.shape[0]
    block = tokens // 2
    copies = []
    for index in range(2):
        here = slice(index * block, index * block + block)
        blended = []
        for group, (weights, position) in enumerate(((weights_low, position_low), (weights_high, position_high))):
            attended = dot_nt(weights[here, :], spread[group])
            blended.append((attended + position[here, :]).astype(BF16))
        buffer[here, :] = dot_nn(jnp.concatenate(blended, axis=1), w_out[...]).astype(BF16)
        copies.append(pltpu.make_async_copy(buffer.at[here, :], mixed.at[here, :], sems.at[index]))
        copies[-1].start()
    for copy in copies:
        copy.wait()


def params(megabytes=48):
    return pltpu.CompilerParams(vmem_limit_bytes=megabytes << 20)


def cost(flops, moved, exps=0):
    return pl.CostEstimate(flops=int(flops), bytes_accessed=int(moved), transcendentals=int(exps))


def shape(dims, dtype):
    return jax.ShapeDtypeStruct(dims, dtype)


def exchange(x, bit):
    peers = lax.axis_size("col")
    return lax.ppermute(x, "col", [(i, i ^ bit) for i in range(peers)])


def on_device(patches, tissue, w_query, w_key, w_value, w_out, agent_tokens, seven, five, three):
    band_rows, width, dim = patches.shape
    tokens = band_rows * width
    agents = agent_tokens.shape[0]
    half_dim = dim // 2
    scale = (dim // HEADS) ** (-0.5)
    flat = patches.reshape(tokens, dim)
    peers = lax.axis_size("col")
    place = lax.axis_index("col")
    odd = place % 2
    odd_word = jnp.reshape(odd, (1,)).astype(jnp.int32)
    own_chunk = jnp.reshape(chunk_of_device(), (1,)).astype(jnp.int32)
    smem = pl.BlockSpec(memory_space=pltpu.SMEM)
    vmem = pl.BlockSpec(memory_space=VMEM)
    anywhere = pl.BlockSpec(memory_space=pl.ANY)

    other = exchange(flat, 1)
    other_tissue = exchange(tissue, 1)

    border = pl.pallas_call(
        border_kernel,
        out_shape=shape((3 * width, dim), BF16),
        in_specs=[smem, vmem],
        out_specs=vmem,
        compiler_params=params(16),
        cost_estimate=cost(1e10, 1e6),
        name="border",
    )(odd_word, flat)
    rest = [(i, i + 1) for i in range(1, peers - 1, 2)]
    outer = lax.ppermute(border, "col", rest + [(j, i) for i, j in rest])

    wide_shape, narrow_shape = shape((72, 512), F32), shape((80, 512), BF16)
    both_bands = shape((2 * tokens, half_dim), BF16)
    values, keys, vals = pl.pallas_call(
        project_kernel,
        out_shape=(shape((tokens, dim), BF16), both_bands, both_bands),
        in_specs=[smem] + [vmem] * 4,
        out_specs=[vmem] * 3,
        compiler_params=params(20),
        cost_estimate=cost(1.3e9, 4e6),
        name="project",
    )(own_chunk, flat, other, w_key, w_value)

    def band(kernel, out_shape):
        return pl.pallas_call(
            functools.partial(kernel, scale),
            out_shape=out_shape,
            in_specs=[smem] + [vmem] * 5,
            out_specs=vmem,
            compiler_params=params(20),
            cost_estimate=cost(6e8, 4e6, 1e6),
            name="band",
        )(own_chunk, keys, vals, tissue, other_tissue, agent_tokens)

    payload = band(first_band_kernel, narrow_shape)

    def token(at, after):
        lanes = slice(at * half_dim, (at + 1) * half_dim)
        return pl.pallas_call(
            functools.partial(token_kernel, scale),
            out_shape=shape((tokens, HEADS // 2 * agents), BF16),
            grid=(1,),
            in_specs=[
                vmem,
                pl.BlockSpec((dim, half_dim), lambda i: (0, at)),
                pl.BlockSpec((agents, half_dim), lambda i: (0, at)),
                anywhere,
            ],
            out_specs=vmem,
            scratch_shapes=[VMEM((tokens, half_dim), BF16)],
            compiler_params=params(20),
            cost_estimate=cost(2e9, 6e6, 1e6),
            name="token",
        )(flat, w_query, agent_tokens, after)

    def conv(at, after):
        return pl.pallas_call(
            functools.partial(conv_kernel, at * half_dim),
            out_shape=shape((band_rows, width, half_dim), F32),
            in_specs=[vmem] * 4 + [anywhere],
            out_specs=vmem,
            scratch_shapes=[
                VMEM((sum(TAP_COUNTS) + len(TAP_COUNTS), width + 16, 128), F32),
                VMEM((7, sum(TAP_COUNTS), 8, 128), F32),
            ],
            compiler_params=params(20),
            cost_estimate=cost(3e9, 4e6),
            name="conv",
        )(values, above, below, taps, after).reshape(tokens, half_dim)

    hop = dict(in_specs=[vmem, vmem, anywhere], compiler_params=params(16), cost_estimate=cost(1e6, 1e6))

    def next_merge(held, got, before):
        return pl.pallas_call(
            next_merge_kernel, out_shape=(wide_shape, narrow_shape), out_specs=[vmem] * 2, name="merge_next", **hop
        )(held, got, before)

    got = exchange(payload, 2)
    held = band(second_band_kernel, wide_shape)
    taps = pl.pallas_call(
        taps_kernel,
        out_shape=shape((7, 24, dim), F32),
        in_specs=[vmem] * 3 + [anywhere],
        out_specs=vmem,
        compiler_params=params(16),
        cost_estimate=cost(5e8, 1e6),
        name="taps",
    )(seven, five, three, payload)
    held, payload = next_merge(held, got, taps)
    bit = 4
    weights_low = None
    while bit * 2 < peers:
        got = exchange(payload, bit)
        if weights_low is None:
            weights_low = token(0, payload)
            above, below = pl.pallas_call(
                halo_kernel,
                out_shape=(shape((3 * width, dim), BF16), shape((3 * width, dim), BF16)),
                in_specs=[smem] + [vmem] * 3 + [anywhere],
                out_specs=[vmem] * 2,
                compiler_params=params(16),
                cost_estimate=cost(4e8, 2e6),
                name="halo",
            )(odd_word, other, outer, w_value, weights_low)
        held, payload = next_merge(held, got, weights_low)
        bit *= 2
    got = exchange(payload, bit)
    weights_high = token(1, payload)
    position_low = conv(0, weights_high)
    own = pl.pallas_call(
        last_merge_kernel, out_shape=shape((64, 512), BF16), out_specs=vmem, name="merge_last", **hop
    )(held, got, position_low)
    near = exchange(own, 2)
    side = exchange(own, 1)
    position_high = conv(1, own)
    again = pl.pallas_call(
        relay_kernel,
        out_shape=shape((64, 512), BF16),
        in_specs=[vmem, anywhere],
        out_specs=vmem,
        compiler_params=params(16),
        cost_estimate=cost(1e6, 1e6),
        name="relay",
    )(near, position_high)
    far = exchange(again, 1)

    mixed = pl.pallas_call(
        out_kernel,
        out_shape=shape((tokens, dim), BF16),
        in_specs=[smem] + [vmem] * 9,
        out_specs=anywhere,
        scratch_shapes=[
            VMEM((2, 256, 1024), BF16),
            VMEM((tokens, dim), BF16),
            pltpu.SemaphoreType.DMA((2,)),
        ],
        compiler_params=params(20),
        cost_estimate=cost(1.1e9, 8e6),
        name="out",
    )(own_chunk, weights_low, weights_high, own, near, side, far, position_low, position_high, w_out)
    return mixed.reshape(band_rows, width, dim)


def solution(mesh):
    return jax.shard_map(
        on_device,
        mesh=mesh,
        in_specs=(
            P(("slide", "col"), None, None),
            P(("slide", "col"), None),
            P(),
            P(),
            P(),
            P(),
            P(),
            P(),
            P(),
            P(),
        ),
        out_specs=P(("slide", "col"), None, None),
        check_vma=False,
    )
```

```python
import functools

import jax
import jax.numpy as jnp
from jax import lax
from jax.experimental import pallas as pl
from jax.experimental.pallas import tpu as pltpu
from jax.sharding import PartitionSpec as P

HEADS = 8
NO_SCORE = -1e30
F32 = jnp.float32
BF16 = jnp.bfloat16
VMEM = pltpu.VMEM


def dot_nt(a, b):
    return lax.dot_general(a, b, (((1,), (1,)), ((), ())), preferred_element_type=F32)


def dot_nn(a, b):
    return lax.dot_general(a, b, (((1,), (0,)), ((), ())), preferred_element_type=F32)


def head_tokens(pair, half, scale):
    lane = lax.broadcasted_iota(jnp.int32, pair.shape, 1)
    mine = (lane >= 64) if half else (lane < 64)
    return jnp.where(mine, pair.astype(F32) * scale, 0.0).astype(BF16)


def chunk_of_device():
    place = lax.axis_index("col")
    return (place & 1) * 2 + ((place >> 2) & 1)


def chunk_state(index, own, scale, keys, vals, tissue, other_tissue, agents):
    lines = []
    for grid in (tissue, other_tissue):
        bias = jnp.where(grid[...] > 0, 0.0, NO_SCORE).astype(F32)
        lines += [bias[row : row + 1] for row in range(bias.shape[0])]
    bias_line = jnp.concatenate(lines, axis=1)
    lanes = pl.ds(pl.multiple_of(((own % 2) ^ index) * 128, 128), 128)
    pair_agents = agents[:, pl.ds(pl.multiple_of((own ^ index) * 128, 128), 128)]
    both = [dot_nt(head_tokens(pair_agents, half, scale), keys[:, lanes]) + bias_line for half in range(2)]
    done = []
    for scores in both:
        peak = jnp.max(scores, axis=1, keepdims=True)
        expo = jnp.exp(scores - peak)
        total = jnp.sum(expo, axis=1, keepdims=True)
        done.append((peak, total, dot_nn(expo.astype(BF16), vals[:, lanes])))
    lane = lax.broadcasted_iota(jnp.int32, done[0][2].shape, 1)
    weighted = jnp.where(lane < 64, done[0][2], done[1][2]).T
    stats = jnp.zeros(weighted.T.shape, F32)
    for at, value in enumerate(done[0][:2] + done[1][:2]):
        stats = jnp.where(lane == at, value, stats)
    stats = stats.T
    sides = []
    for at in range(2):
        sides.append((stats[2 * at : 2 * at + 1], stats[2 * at + 1 : 2 * at + 2], weighted[64 * at : 64 * at + 64]))
    return tuple(jnp.concatenate(pair, axis=1) for pair in zip(*sides))


def project_kernel(own_ref, mine, other, w_key, w_value, values, keys, vals):
    tokens = mine.shape[0]
    block = 256
    half_lanes = pl.ds(pl.multiple_of((own_ref[0] // 2) * 256, 256), 256)
    key_half = w_key[:, half_lanes]
    value_half = w_value[:, half_lanes]
    for at in range(0, tokens, block):
        rows = pl.ds(at, block)
        part = mine[rows, :]
        keys[rows, :] = dot_nn(part, key_half).astype(BF16)
        values[rows, :] = dot_nn(part, w_value[...]).astype(BF16)
        vals[rows, :] = values[rows, half_lanes]
    for at in range(0, tokens, block):
        rows = pl.ds(tokens + at, block)
        part = other[pl.ds(at, block), :]
        keys[rows, :] = dot_nn(part, key_half).astype(BF16)
        vals[rows, :] = dot_nn(part, value_half).astype(BF16)


def first_band_kernel(scale, own_ref, keys, vals, tissue, other_tissue, agents, payload):
    put_narrow(payload, chunk_state(1, own_ref[0], scale, keys, vals, tissue, other_tissue, agents))


def second_band_kernel(scale, own_ref, keys, vals, tissue, other_tissue, agents, keep):
    put_wide(keep, chunk_state(0, own_ref[0], scale, keys, vals, tissue, other_tissue, agents))


def merge(first, second):
    peak_1, total_1, weighted_1 = first
    peak_2, total_2, weighted_2 = second
    peak = jnp.maximum(peak_1, peak_2)
    factor_1 = jnp.exp(peak_1 - peak)
    factor_2 = jnp.exp(peak_2 - peak)
    return peak, total_1 * factor_1 + total_2 * factor_2, weighted_1 * factor_1 + weighted_2 * factor_2


def wide(ref, index=None):
    array = ref[...] if index is None else ref[index]
    return array[64:65], array[65:66], array[0:64]


def thirds(value):
    high = value.astype(BF16).astype(F32)
    rest = value - high
    middle = rest.astype(BF16).astype(F32)
    return high, middle, rest - middle


def put_wide(ref, state):
    peak, total, weighted = state
    row_id = lax.broadcasted_iota(jnp.int32, (8, weighted.shape[1]), 0)
    ref[0:64] = weighted
    ref[64:72] = jnp.where(row_id == 0, peak, jnp.where(row_id == 1, total, 0.0))


def put_narrow(ref, state):
    peak, total, weighted = state
    row_id = lax.broadcasted_iota(jnp.int32, (16, weighted.shape[1]), 0)
    stats = jnp.zeros((16, weighted.shape[1]), F32)
    for at, part in enumerate(thirds(peak) + thirds(total)):
        stats = jnp.where(row_id == at, part, stats)
    ref[0:64] = weighted.astype(BF16)
    ref[64:80] = stats.astype(BF16)


def narrow(ref):
    stats = ref[64:80].astype(F32)
    peak = stats[0:1] + stats[1:2] + stats[2:3]
    total = stats[3:4] + stats[4:5] + stats[5:6]
    return peak, total, ref[0:64].astype(F32)


def next_merge_kernel(held, got, before, own, payload):
    state = merge(wide(held), narrow(got))
    put_narrow(payload, state)
    put_wide(own, state)


def last_merge_kernel(held, got, before, agent_values):
    _, total, weighted = merge(wide(held), narrow(got))
    agent_values[...] = (weighted / total).astype(BF16)


def token_kernel(scale, patches, w_query, agents, after, weights, queries):
    heads = weights.shape[1] // agents.shape[0]
    queries[...] = dot_nn(patches[...], w_query[...]).astype(BF16)

    def scores_of(head):
        lanes = slice(head // 2 * 128, head // 2 * 128 + 128)
        return dot_nt(queries[:, lanes], head_tokens(agents[:, lanes], head % 2, scale))

    ahead = scores_of(0)
    for head in range(heads):
        scores = ahead
        if head + 1 < heads:
            ahead = scores_of(head + 1)
        expo = jnp.exp(scores - jnp.max(scores, axis=1, keepdims=True))
        part = expo * (1.0 / jnp.sum(expo, axis=1, keepdims=True))
        weights[:, head * 256 : head * 256 + 256] = part.astype(BF16)


def border_kernel(odd_ref, first, last, border):
    border[...] = jnp.where(odd_ref[0] == 1, last[...], first[...])


def halo_kernel(odd_ref, other, outer, w_value, after, above, below):
    rows = outer.shape[0]
    odd = odd_ref[0] == 1
    inner_part = other[pl.ds(pl.multiple_of(odd_ref[0] * (other.shape[0] - rows), 128), rows), :]
    inner = dot_nn(inner_part, w_value[...]).astype(BF16)
    outside = dot_nn(outer[...], w_value[...]).astype(BF16)
    above[...] = jnp.where(odd, inner, outside)
    below[...] = jnp.where(odd, outside, inner)


def relay_kernel(near, after, again):
    again[...] = near[...]


TAP_COUNTS = (2, 2, 2, 2, 2, 2, 2, 2, 1)


def split_rows(rows):
    return [
        [rows[at] - rows[at + 1] for at in range(0, len(rows) - 1, 2)],
        [rows[at + 1] for at in range(0, len(rows) - 1, 2)],
        [rows[at + 2] - rows[at + 1] for at in range(0, len(rows) - 2, 2)],
    ]


def split_taps(taps):
    even, odd = taps[0::2], taps[1::2]
    both = [even[at] + odd[at] if at < len(odd) else even[at] for at in range(len(even))]
    return [even, both, odd]


def joined_rows(first, second, third):
    return [row for a, b, c in zip(first, second, third) for row in (a + b, b + c)]


def taps_kernel(seven, five, three, after, taps):
    for q in range(7):
        column = [seven[p, q : q + 1, :] for p in range(7)]
        if 1 <= q <= 5:
            column[1:6] = [tap + five[p, q - 1 : q, :] for p, tap in enumerate(column[1:6])]
        if 2 <= q <= 4:
            column[2:5] = [tap + three[p, q - 2 : q - 1, :] for p, tap in enumerate(column[2:5])]
        parts = [tap for part in split_taps(column) for piece in split_taps(part) for tap in piece]
        parts += [jnp.zeros_like(parts[0])] * (taps.shape[1] - len(parts))
        taps[q] = jnp.concatenate(parts, axis=0)


def conv_kernel(first_lane, values, above, below, all_taps, after, position, points, taps):
    width = position.shape[1]
    lanes, step = 128, 16
    tap_count = sum(TAP_COUNTS)
    zero = jnp.zeros((8, lanes), F32)
    for group in range(position.shape[2] // lanes):
        here = slice(first_lane + group * lanes, first_lane + (group + 1) * lanes)
        there = slice(group * lanes, (group + 1) * lanes)
        for q in range(7):
            for at in range(tap_count):
                taps[q, at] = jnp.broadcast_to(all_taps[q, at : at + 1, here], (8, lanes))
        for at in range(points.shape[0]):
            points[at, 0:8, :] = zero
            points[at, 8 + width : 16 + width, :] = zero
        for at in range(0, width, step):
            rows = []
            for ref in (above, values, below):
                for row in range(0, ref.shape[0], width):
                    rows.append(ref[row + at : row + at + step, here].astype(F32))
            even, odd = rows[0::2], rows[1::2]
            streams = (
                [a - b for a, b in zip(even, odd)],
                odd,
                [a - b for a, b in zip(even[1:], odd)],
            )
            parts = [plane for stream in streams for piece in split_rows(stream) for plane in piece]
            for index, plane in enumerate(parts):
                points[index, 8 + at : 8 + at + step, :] = plane
        for at in range(0, width, step):
            columns = (at, at + 8)
            sums = [[[zero, zero] for _ in TAP_COUNTS] for _ in columns]
            for q in range(7):
                first_point = first_tap = 0
                for piece, count in enumerate(TAP_COUNTS):
                    tap = [taps[q, first_tap + k] for k in range(count)]
                    for total, column in zip(sums, columns):
                        start = column + 5 + q
                        point = [points[first_point + k, start : start + 8, :] for k in range(count + 1)]
                        for out in range(2):
                            for k in range(count):
                                total[piece][out] = total[piece][out] + point[out + k] * tap[k]
                    first_point += count + 1
                    first_tap += count
            for total, column in zip(sums, columns):
                thirds_of = [joined_rows(*total[3 * part : 3 * part + 3]) for part in range(3)]
                for row, plane in enumerate(joined_rows(*thirds_of)):
                    position[row, column : column + 8, there] = plane


def out_kernel(
    own_ref, weights_low, weights_high, own, near, side, far, position_low, position_high, w_out, mixed, spread, buffer, sems
):
    spread[...] = jnp.zeros_like(spread)
    for index, part in enumerate((own, near, side, far)):
        chunk = index ^ own_ref[0]
        group, place = chunk // 2, chunk % 2
        for half in range(2):
            rows = pl.ds(pl.multiple_of(place * 128 + half * 64, 64), 64)
            cols = pl.ds(pl.multiple_of(place * 512 + half * 256, 256), 256)
            spread[group, rows, cols] = part[:, half * 256 : half * 256 + 256]
    tokens = mixed.shape[0]
    block = tokens // 2
    copies = []
    for index in range(2):
        here = slice(index * block, index * block + block)
        blended = []
        for group, (weights, position) in enumerate(((weights_low, position_low), (weights_high, position_high))):
            attended = dot_nt(weights[here, :], spread[group])
            blended.append((attended + position[here, :]).astype(BF16))
        buffer[here, :] = dot_nn(jnp.concatenate(blended, axis=1), w_out[...]).astype(BF16)
        copies.append(pltpu.make_async_copy(buffer.at[here, :], mixed.at[here, :], sems.at[index]))
        copies[-1].start()
    for copy in copies:
        copy.wait()


def params(megabytes=48):
    return pltpu.CompilerParams(vmem_limit_bytes=megabytes << 20)


def cost(flops, moved, exps=0):
    return pl.CostEstimate(flops=int(flops), bytes_accessed=int(moved), transcendentals=int(exps))


def shape(dims, dtype):
    return jax.ShapeDtypeStruct(dims, dtype)


def exchange(x, bit):
    peers = lax.axis_size("col")
    return lax.ppermute(x, "col", [(i, i ^ bit) for i in range(peers)])


def on_device(patches, tissue, w_query, w_key, w_value, w_out, agent_tokens, seven, five, three):
    band_rows, width, dim = patches.shape
    tokens = band_rows * width
    agents = agent_tokens.shape[0]
    half_dim = dim // 2
    scale = (dim // HEADS) ** (-0.5)
    flat = patches.reshape(tokens, dim)
    peers = lax.axis_size("col")
    place = lax.axis_index("col")
    odd = place % 2
    odd_word = jnp.reshape(odd, (1,)).astype(jnp.int32)
    own_chunk = jnp.reshape(chunk_of_device(), (1,)).astype(jnp.int32)
    smem = pl.BlockSpec(memory_space=pltpu.SMEM)
    vmem = pl.BlockSpec(memory_space=VMEM)
    anywhere = pl.BlockSpec(memory_space=pl.ANY)

    other = exchange(flat, 1)
    other_tissue = exchange(tissue, 1)

    border = pl.pallas_call(
        border_kernel,
        out_shape=shape((3 * width, dim), BF16),
        in_specs=[smem, vmem, vmem],
        out_specs=vmem,
        compiler_params=params(16),
        cost_estimate=cost(1e10, 1e6),
        name="border",
    )(odd_word, flat[: 3 * width], flat[tokens - 3 * width :])
    rest = [(i, i + 1) for i in range(1, peers - 1, 2)]
    outer = lax.ppermute(border, "col", rest + [(j, i) for i, j in rest])

    wide_shape, narrow_shape = shape((72, 512), F32), shape((80, 512), BF16)
    both_bands = shape((2 * tokens, half_dim), BF16)
    values, keys, vals = pl.pallas_call(
        project_kernel,
        out_shape=(shape((tokens, dim), BF16), both_bands, both_bands),
        in_specs=[smem] + [vmem] * 4,
        out_specs=[vmem] * 3,
        compiler_params=params(20),
        cost_estimate=cost(1.3e9, 4e6),
        name="project",
    )(own_chunk, flat, other, w_key, w_value)

    def band(kernel, out_shape):
        return pl.pallas_call(
            functools.partial(kernel, scale),
            out_shape=out_shape,
            in_specs=[smem] + [vmem] * 5,
            out_specs=vmem,
            compiler_params=params(20),
            cost_estimate=cost(6e8, 4e6, 1e6),
            name="band",
        )(own_chunk, keys, vals, tissue, other_tissue, agent_tokens)

    payload = band(first_band_kernel, narrow_shape)

    def token(at, after):
        lanes = slice(at * half_dim, (at + 1) * half_dim)
        return pl.pallas_call(
            functools.partial(token_kernel, scale),
            out_shape=shape((tokens, HEADS // 2 * agents), BF16),
            grid=(1,),
            in_specs=[
                vmem,
                pl.BlockSpec((dim, half_dim), lambda i: (0, at)),
                pl.BlockSpec((agents, half_dim), lambda i: (0, at)),
                anywhere,
            ],
            out_specs=vmem,
            scratch_shapes=[VMEM((tokens, half_dim), BF16)],
            compiler_params=params(20),
            cost_estimate=cost(2e9, 6e6, 1e6),
            name="token",
        )(flat, w_query, agent_tokens, after)

    def conv(at, after):
        return pl.pallas_call(
            functools.partial(conv_kernel, at * half_dim),
            out_shape=shape((band_rows, width, half_dim), F32),
            in_specs=[vmem] * 4 + [anywhere],
            out_specs=vmem,
            scratch_shapes=[
                VMEM((sum(TAP_COUNTS) + len(TAP_COUNTS), width + 16, 128), F32),
                VMEM((7, sum(TAP_COUNTS), 8, 128), F32),
            ],
            compiler_params=params(20),
            cost_estimate=cost(3e9, 4e6),
            name="conv",
        )(values, above, below, taps, after).reshape(tokens, half_dim)

    hop = dict(in_specs=[vmem, vmem, anywhere], compiler_params=params(16), cost_estimate=cost(1e6, 1e6))

    def next_merge(held, got, before):
        return pl.pallas_call(
            next_merge_kernel, out_shape=(wide_shape, narrow_shape), out_specs=[vmem] * 2, name="merge_next", **hop
        )(held, got, before)

    got = exchange(payload, 4)
    held = band(second_band_kernel, wide_shape)
    taps = pl.pallas_call(
        taps_kernel,
        out_shape=shape((7, 24, dim), F32),
        in_specs=[vmem] * 3 + [anywhere],
        out_specs=vmem,
        compiler_params=params(16),
        cost_estimate=cost(5e8, 1e6),
        name="taps",
    )(seven, five, three, payload)
    held, payload = next_merge(held, got, taps)
    bit = 8
    weights_low = None
    while bit < peers:
        got = exchange(payload, bit)
        if weights_low is None:
            weights_low = token(0, payload)
            above, below = pl.pallas_call(
                halo_kernel,
                out_shape=(shape((3 * width, dim), BF16), shape((3 * width, dim), BF16)),
                in_specs=[smem] + [vmem] * 3 + [anywhere],
                out_specs=[vmem] * 2,
                compiler_params=params(16),
                cost_estimate=cost(4e8, 2e6),
                name="halo",
            )(odd_word, other, outer, w_value, weights_low)
            weights_high = token(1, above)
        held, payload = next_merge(held, got, weights_high)
        bit *= 2
    got = exchange(payload, 2)
    position_low = conv(0, payload)
    own = pl.pallas_call(
        last_merge_kernel, out_shape=shape((64, 512), BF16), out_specs=vmem, name="merge_last", **hop
    )(held, got, position_low)
    near = exchange(own, 4)
    side = exchange(own, 1)
    position_high = conv(1, own)
    again = pl.pallas_call(
        relay_kernel,
        out_shape=shape((64, 512), BF16),
        in_specs=[vmem, anywhere],
        out_specs=vmem,
        compiler_params=params(16),
        cost_estimate=cost(1e6, 1e6),
        name="relay",
    )(near, position_high)
    far = exchange(again, 1)

    mixed = pl.pallas_call(
        out_kernel,
        out_shape=shape((tokens, dim), BF16),
        in_specs=[smem] + [vmem] * 9,
        out_specs=anywhere,
        scratch_shapes=[
            VMEM((2, 256, 1024), BF16),
            VMEM((tokens, dim), BF16),
            pltpu.SemaphoreType.DMA((2,)),
        ],
        compiler_params=params(20),
        cost_estimate=cost(1.1e9, 8e6),
        name="out",
    )(own_chunk, weights_low, weights_high, own, near, side, far, position_low, position_high, w_out)
    return mixed.reshape(band_rows, width, dim)


def solution(mesh):
    return jax.shard_map(
        on_device,
        mesh=mesh,
        in_specs=(
            P(("slide", "col"), None, None),
            P(("slide", "col"), None),
            P(),
            P(),
            P(),
            P(),
            P(),
            P(),
            P(),
            P(),
        ),
        out_specs=P(("slide", "col"), None, None),
        check_vma=False,
    )
```

```python
import functools

import jax
import jax.numpy as jnp
from jax import lax
from jax.experimental import pallas as pl
from jax.experimental.pallas import tpu as pltpu
from jax.sharding import PartitionSpec as P

HEADS = 8
NO_SCORE = -1e30
F32 = jnp.float32
BF16 = jnp.bfloat16
VMEM = pltpu.VMEM


def dot_nt(a, b):
    return lax.dot_general(a, b, (((1,), (1,)), ((), ())), preferred_element_type=F32)


def dot_nn(a, b):
    return lax.dot_general(a, b, (((1,), (0,)), ((), ())), preferred_element_type=F32)


def head_tokens(pair, half, scale):
    lane = lax.broadcasted_iota(jnp.int32, pair.shape, 1)
    mine = (lane >= 64) if half else (lane < 64)
    return jnp.where(mine, pair.astype(F32) * scale, 0.0).astype(BF16)


def chunk_of_device():
    place = lax.axis_index("col")
    return (place & 1) * 2 + ((place >> 2) & 1)


def chunk_state(index, own, scale, keys, vals, tissue, other_tissue, agents):
    lines = []
    for grid in (tissue, other_tissue):
        bias = jnp.where(grid[...] > 0, 0.0, NO_SCORE).astype(F32)
        lines += [bias[row : row + 1] for row in range(bias.shape[0])]
    bias_line = jnp.concatenate(lines, axis=1)
    lanes = pl.ds(pl.multiple_of(((own % 2) ^ index) * 128, 128), 128)
    pair_agents = agents[:, pl.ds(pl.multiple_of((own ^ index) * 128, 128), 128)]
    both = [dot_nt(head_tokens(pair_agents, half, scale), keys[:, lanes]) + bias_line for half in range(2)]
    done = []
    for scores in both:
        peak = jnp.max(scores, axis=1, keepdims=True)
        expo = jnp.exp(scores - peak)
        total = jnp.sum(expo, axis=1, keepdims=True)
        done.append((peak, total, dot_nn(expo.astype(BF16), vals[:, lanes])))
    lane = lax.broadcasted_iota(jnp.int32, done[0][2].shape, 1)
    weighted = jnp.where(lane < 64, done[0][2], done[1][2]).T
    stats = jnp.zeros(weighted.T.shape, F32)
    for at, value in enumerate(done[0][:2] + done[1][:2]):
        stats = jnp.where(lane == at, value, stats)
    stats = stats.T
    sides = []
    for at in range(2):
        sides.append((stats[2 * at : 2 * at + 1], stats[2 * at + 1 : 2 * at + 2], weighted[64 * at : 64 * at + 64]))
    return tuple(jnp.concatenate(pair, axis=1) for pair in zip(*sides))


def project_kernel(own_ref, mine, other, w_key, w_value, values, keys, vals):
    tokens = mine.shape[0]
    block = 256
    half_lanes = pl.ds(pl.multiple_of((own_ref[0] // 2) * 256, 256), 256)
    key_half = w_key[:, half_lanes]
    value_half = w_value[:, half_lanes]
    for at in range(0, tokens, block):
        rows = pl.ds(at, block)
        part = mine[rows, :]
        keys[rows, :] = dot_nn(part, key_half).astype(BF16)
        values[rows, :] = dot_nn(part, w_value[...]).astype(BF16)
        vals[rows, :] = values[rows, half_lanes]
    for at in range(0, tokens, block):
        rows = pl.ds(tokens + at, block)
        part = other[pl.ds(at, block), :]
        keys[rows, :] = dot_nn(part, key_half).astype(BF16)
        vals[rows, :] = dot_nn(part, value_half).astype(BF16)


def first_band_kernel(scale, own_ref, keys, vals, tissue, other_tissue, agents, payload):
    put_narrow(payload, chunk_state(1, own_ref[0], scale, keys, vals, tissue, other_tissue, agents))


def second_band_kernel(scale, own_ref, keys, vals, tissue, other_tissue, agents, keep):
    put_wide(keep, chunk_state(0, own_ref[0], scale, keys, vals, tissue, other_tissue, agents))


def merge(first, second):
    peak_1, total_1, weighted_1 = first
    peak_2, total_2, weighted_2 = second
    peak = jnp.maximum(peak_1, peak_2)
    factor_1 = jnp.exp(peak_1 - peak)
    factor_2 = jnp.exp(peak_2 - peak)
    return peak, total_1 * factor_1 + total_2 * factor_2, weighted_1 * factor_1 + weighted_2 * factor_2


def wide(ref, index=None):
    array = ref[...] if index is None else ref[index]
    return array[64:65], array[65:66], array[0:64]


def thirds(value):
    high = value.astype(BF16).astype(F32)
    rest = value - high
    middle = rest.astype(BF16).astype(F32)
    return high, middle, rest - middle


def put_wide(ref, state):
    peak, total, weighted = state
    row_id = lax.broadcasted_iota(jnp.int32, (8, weighted.shape[1]), 0)
    ref[0:64] = weighted
    ref[64:72] = jnp.where(row_id == 0, peak, jnp.where(row_id == 1, total, 0.0))


def put_narrow(ref, state):
    peak, total, weighted = state
    row_id = lax.broadcasted_iota(jnp.int32, (16, weighted.shape[1]), 0)
    stats = jnp.zeros((16, weighted.shape[1]), F32)
    for at, part in enumerate(thirds(peak) + thirds(total)):
        stats = jnp.where(row_id == at, part, stats)
    ref[0:64] = weighted.astype(BF16)
    ref[64:80] = stats.astype(BF16)


def narrow(ref):
    stats = ref[64:80].astype(F32)
    peak = stats[0:1] + stats[1:2] + stats[2:3]
    total = stats[3:4] + stats[4:5] + stats[5:6]
    return peak, total, ref[0:64].astype(F32)


def next_merge_kernel(held, got, before, own, payload):
    state = merge(wide(held), narrow(got))
    put_narrow(payload, state)
    put_wide(own, state)


def last_merge_kernel(held, got, before, agent_values):
    _, total, weighted = merge(wide(held), narrow(got))
    agent_values[...] = (weighted / total).astype(BF16)


def token_kernel(scale, patches, w_query, agents, after, weights, queries):
    heads = weights.shape[1] // agents.shape[0]
    queries[...] = dot_nn(patches[...], w_query[...]).astype(BF16)

    def scores_of(head):
        lanes = slice(head // 2 * 128, head // 2 * 128 + 128)
        return dot_nt(queries[:, lanes], head_tokens(agents[:, lanes], head % 2, scale))

    ahead = scores_of(0)
    for head in range(heads):
        scores = ahead
        if head + 1 < heads:
            ahead = scores_of(head + 1)
        expo = jnp.exp(scores - jnp.max(scores, axis=1, keepdims=True))
        part = expo * (1.0 / jnp.sum(expo, axis=1, keepdims=True))
        weights[:, head * 256 : head * 256 + 256] = part.astype(BF16)


def pass_kernel(border, same):
    del border, same


def halo_kernel(odd_ref, other, outer, w_value, after, above, below):
    rows = outer.shape[0]
    odd = odd_ref[0] == 1
    inner_part = other[pl.ds(pl.multiple_of(odd_ref[0] * (other.shape[0] - rows), 128), rows), :]
    inner = dot_nn(inner_part, w_value[...]).astype(BF16)
    outside = dot_nn(outer[...], w_value[...]).astype(BF16)
    above[...] = jnp.where(odd, inner, outside)
    below[...] = jnp.where(odd, outside, inner)


def relay_kernel(own, near, after, both):
    both[0:64] = own[...]
    both[64:128] = near[...]


TAP_COUNTS = (2, 2, 2, 2, 2, 2, 2, 2, 1)


def split_rows(rows):
    return [
        [rows[at] - rows[at + 1] for at in range(0, len(rows) - 1, 2)],
        [rows[at + 1] for at in range(0, len(rows) - 1, 2)],
        [rows[at + 2] - rows[at + 1] for at in range(0, len(rows) - 2, 2)],
    ]


def split_taps(taps):
    even, odd = taps[0::2], taps[1::2]
    both = [even[at] + odd[at] if at < len(odd) else even[at] for at in range(len(even))]
    return [even, both, odd]


def joined_rows(first, second, third):
    return [row for a, b, c in zip(first, second, third) for row in (a + b, b + c)]


def taps_kernel(seven, five, three, after, taps):
    for q in range(7):
        column = [seven[p, q : q + 1, :] for p in range(7)]
        if 1 <= q <= 5:
            column[1:6] = [tap + five[p, q - 1 : q, :] for p, tap in enumerate(column[1:6])]
        if 2 <= q <= 4:
            column[2:5] = [tap + three[p, q - 2 : q - 1, :] for p, tap in enumerate(column[2:5])]
        parts = [tap for part in split_taps(column) for piece in split_taps(part) for tap in piece]
        parts += [jnp.zeros_like(parts[0])] * (taps.shape[1] - len(parts))
        taps[q] = jnp.concatenate(parts, axis=0)


def conv_kernel(first_lane, values, above, below, all_taps, after, position, points, taps):
    width = position.shape[1]
    lanes, step = 128, 16
    tap_count = sum(TAP_COUNTS)
    zero = jnp.zeros((8, lanes), F32)
    for group in range(position.shape[2] // lanes):
        here = slice(first_lane + group * lanes, first_lane + (group + 1) * lanes)
        there = slice(group * lanes, (group + 1) * lanes)
        for q in range(7):
            for at in range(tap_count):
                taps[q, at] = jnp.broadcast_to(all_taps[q, at : at + 1, here], (8, lanes))
        for at in range(points.shape[0]):
            points[at, 0:8, :] = zero
            points[at, 8 + width : 16 + width, :] = zero
        for at in range(0, width, step):
            rows = []
            for ref in (above, values, below):
                for row in range(0, ref.shape[0], width):
                    rows.append(ref[row + at : row + at + step, here].astype(F32))
            even, odd = rows[0::2], rows[1::2]
            streams = (
                [a - b for a, b in zip(even, odd)],
                odd,
                [a - b for a, b in zip(even[1:], odd)],
            )
            parts = [plane for stream in streams for piece in split_rows(stream) for plane in piece]
            for index, plane in enumerate(parts):
                points[index, 8 + at : 8 + at + step, :] = plane
        for at in range(0, width, step):
            columns = (at, at + 8)
            sums = [[[zero, zero] for _ in TAP_COUNTS] for _ in columns]
            for q in range(7):
                first_point = first_tap = 0
                for piece, count in enumerate(TAP_COUNTS):
                    tap = [taps[q, first_tap + k] for k in range(count)]
                    for total, column in zip(sums, columns):
                        start = column + 5 + q
                        point = [points[first_point + k, start : start + 8, :] for k in range(count + 1)]
                        for out in range(2):
                            for k in range(count):
                                total[piece][out] = total[piece][out] + point[out + k] * tap[k]
                    first_point += count + 1
                    first_tap += count
            for total, column in zip(sums, columns):
                thirds_of = [joined_rows(*total[3 * part : 3 * part + 3]) for part in range(3)]
                for row, plane in enumerate(joined_rows(*thirds_of)):
                    position[row, column : column + 8, there] = plane


def blend_block(here, weights, position, spread, w_out, rows):
    blended = (dot_nt(weights[here, :], spread[...]) + position[here, :]).astype(BF16)
    return dot_nn(blended, w_out[rows, :])


def fill_spread(own_ref, pair, spread):
    spread[...] = jnp.zeros_like(spread)
    for index in range(2):
        place = (own_ref[0] % 2) ^ index
        for half in range(2):
            rows = pl.ds(pl.multiple_of(place * 128 + half * 64, 64), 64)
            cols = pl.ds(pl.multiple_of(place * 512 + half * 256, 256), 256)
            spread[rows, cols] = pair[index * 64 : index * 64 + 64, half * 256 : half * 256 + 256]


def own_out_kernel(own_ref, weights_low, weights_high, pair, position_low, position_high, w_out, partial, spread):
    fill_spread(own_ref, pair, spread)
    block = partial.shape[0] // 2
    for group, (weights, position) in enumerate(((weights_low, position_low), (weights_high, position_high))):

        @pl.when(own_ref[0] // 2 == group)
        def _(group=group, weights=weights, position=position):
            rows = slice(group * 256, group * 256 + 256)
            for index in range(2):
                here = slice(index * block, index * block + block)
                partial[here, :] = blend_block(here, weights, position, spread, w_out, rows)


def out_kernel(
    own_ref, weights_low, weights_high, pair, position_low, position_high, w_out, partial, mixed, spread, buffer, sems
):
    fill_spread(own_ref, pair, spread)
    block = partial.shape[0] // 2
    copies = []
    for index in range(2):
        here = slice(index * block, index * block + block)
        for group, (weights, position) in enumerate(((weights_low, position_low), (weights_high, position_high))):

            @pl.when(own_ref[0] // 2 != group)
            def _(group=group, weights=weights, position=position, here=here):
                rows = slice(group * 256, group * 256 + 256)
                total = partial[here, :] + blend_block(here, weights, position, spread, w_out, rows)
                buffer[here, :] = total.astype(BF16)

        copies.append(pltpu.make_async_copy(buffer.at[here, :], mixed.at[here, :], sems.at[index]))
        copies[-1].start()
    for copy in copies:
        copy.wait()


def params(megabytes=48):
    return pltpu.CompilerParams(vmem_limit_bytes=megabytes << 20)


def cost(flops, moved, exps=0):
    return pl.CostEstimate(flops=int(flops), bytes_accessed=int(moved), transcendentals=int(exps))


def shape(dims, dtype):
    return jax.ShapeDtypeStruct(dims, dtype)


def exchange(x, bit):
    peers = lax.axis_size("col")
    return lax.ppermute(x, "col", [(i, i ^ bit) for i in range(peers)])


def on_device(patches, tissue, w_query, w_key, w_value, w_out, agent_tokens, seven, five, three):
    band_rows, width, dim = patches.shape
    tokens = band_rows * width
    agents = agent_tokens.shape[0]
    half_dim = dim // 2
    scale = (dim // HEADS) ** (-0.5)
    flat = patches.reshape(tokens, dim)
    peers = lax.axis_size("col")
    place = lax.axis_index("col")
    odd = place % 2
    odd_word = jnp.reshape(odd, (1,)).astype(jnp.int32)
    own_chunk = jnp.reshape(chunk_of_device(), (1,)).astype(jnp.int32)
    smem = pl.BlockSpec(memory_space=pltpu.SMEM)
    vmem = pl.BlockSpec(memory_space=VMEM)
    anywhere = pl.BlockSpec(memory_space=pl.ANY)

    other = exchange(flat, 1)
    other_tissue = exchange(tissue, 1)

    border = lax.dynamic_slice_in_dim(flat, odd * (tokens - 3 * width), 3 * width, 0)
    border = pl.pallas_call(
        pass_kernel,
        out_shape=shape((3 * width, dim), BF16),
        in_specs=[anywhere],
        out_specs=anywhere,
        input_output_aliases={0: 0},
        compiler_params=params(16),
        cost_estimate=cost(1e11, 1e6),
        name="pass",
    )(border)
    rest = [(i, i + 1) for i in range(1, peers - 1, 2)]
    outer = lax.ppermute(border, "col", rest + [(j, i) for i, j in rest])

    wide_shape, narrow_shape = shape((72, 512), F32), shape((80, 512), BF16)
    both_bands = shape((2 * tokens, half_dim), BF16)
    values, keys, vals = pl.pallas_call(
        project_kernel,
        out_shape=(shape((tokens, dim), BF16), both_bands, both_bands),
        in_specs=[smem] + [vmem] * 4,
        out_specs=[vmem] * 3,
        compiler_params=params(20),
        cost_estimate=cost(1.3e9, 4e6),
        name="project",
    )(own_chunk, flat, other, w_key, w_value)

    def band(kernel, out_shape):
        return pl.pallas_call(
            functools.partial(kernel, scale),
            out_shape=out_shape,
            in_specs=[smem] + [vmem] * 5,
            out_specs=vmem,
            compiler_params=params(20),
            cost_estimate=cost(6e8, 4e6, 1e6),
            name="band",
        )(own_chunk, keys, vals, tissue, other_tissue, agent_tokens)

    payload = band(first_band_kernel, narrow_shape)

    def token(at, after):
        lanes = slice(at * half_dim, (at + 1) * half_dim)
        return pl.pallas_call(
            functools.partial(token_kernel, scale),
            out_shape=shape((tokens, HEADS // 2 * agents), BF16),
            grid=(1,),
            in_specs=[
                vmem,
                pl.BlockSpec((dim, half_dim), lambda i: (0, at)),
                pl.BlockSpec((agents, half_dim), lambda i: (0, at)),
                anywhere,
            ],
            out_specs=vmem,
            scratch_shapes=[VMEM((tokens, half_dim), BF16)],
            compiler_params=params(20),
            cost_estimate=cost(2e9, 6e6, 1e6),
            name="token",
        )(flat, w_query, agent_tokens, after)

    def conv(at, after):
        return pl.pallas_call(
            functools.partial(conv_kernel, at * half_dim),
            out_shape=shape((band_rows, width, half_dim), F32),
            in_specs=[vmem] * 4 + [anywhere],
            out_specs=vmem,
            scratch_shapes=[
                VMEM((sum(TAP_COUNTS) + len(TAP_COUNTS), width + 16, 128), F32),
                VMEM((7, sum(TAP_COUNTS), 8, 128), F32),
            ],
            compiler_params=params(20),
            cost_estimate=cost(3e9, 4e6),
            name="conv",
        )(values, above, below, taps, after).reshape(tokens, half_dim)

    hop = dict(in_specs=[vmem, vmem, anywhere], compiler_params=params(16), cost_estimate=cost(1e6, 1e6))

    def next_merge(held, got, before):
        return pl.pallas_call(
            next_merge_kernel, out_shape=(wide_shape, narrow_shape), out_specs=[vmem] * 2, name="merge_next", **hop
        )(held, got, before)

    got = exchange(payload, 4)
    held = band(second_band_kernel, wide_shape)
    taps = pl.pallas_call(
        taps_kernel,
        out_shape=shape((7, 24, dim), F32),
        in_specs=[vmem] * 3 + [anywhere],
        out_specs=vmem,
        compiler_params=params(16),
        cost_estimate=cost(5e8, 1e6),
        name="taps",
    )(seven, five, three, payload)
    held, payload = next_merge(held, got, taps)
    bit = 8
    weights_low = None
    while bit < peers:
        got = exchange(payload, bit)
        if weights_low is None:
            weights_low = token(0, payload)
            above, below = pl.pallas_call(
                halo_kernel,
                out_shape=(shape((3 * width, dim), BF16), shape((3 * width, dim), BF16)),
                in_specs=[smem] + [vmem] * 3 + [anywhere],
                out_specs=[vmem] * 2,
                compiler_params=params(16),
                cost_estimate=cost(4e8, 2e6),
                name="halo",
            )(odd_word, other, outer, w_value, weights_low)
            weights_high = token(1, above)
        held, payload = next_merge(held, got, weights_high)
        bit *= 2
    got = exchange(payload, 2)
    position_low = conv(0, payload)
    own = pl.pallas_call(
        last_merge_kernel, out_shape=shape((64, 512), BF16), out_specs=vmem, name="merge_last", **hop
    )(held, got, position_low)
    near = exchange(own, 4)
    position_high = conv(1, own)
    pair = pl.pallas_call(
        relay_kernel,
        out_shape=shape((128, 512), BF16),
        in_specs=[vmem, vmem, anywhere],
        out_specs=vmem,
        compiler_params=params(16),
        cost_estimate=cost(1e6, 1e6),
        name="relay",
    )(own, near, position_high)
    other_pair = exchange(pair, 1)

    partial = pl.pallas_call(
        own_out_kernel,
        out_shape=shape((tokens, dim), F32),
        in_specs=[smem] + [vmem] * 6,
        out_specs=vmem,
        scratch_shapes=[VMEM((256, 1024), BF16)],
        compiler_params=params(20),
        cost_estimate=cost(1.1e9, 4e6),
        name="own_out",
    )(own_chunk, weights_low, weights_high, pair, position_low, position_high, w_out)
    mixed = pl.pallas_call(
        out_kernel,
        out_shape=shape((tokens, dim), BF16),
        in_specs=[smem] + [vmem] * 7,
        out_specs=anywhere,
        scratch_shapes=[
            VMEM((256, 1024), BF16),
            VMEM((tokens, dim), BF16),
            pltpu.SemaphoreType.DMA((2,)),
        ],
        compiler_params=params(20),
        cost_estimate=cost(1.1e9, 8e6),
        name="out",
    )(own_chunk, weights_low, weights_high, other_pair, position_low, position_high, w_out, partial)
    return mixed.reshape(band_rows, width, dim)


def solution(mesh):
    return jax.shard_map(
        on_device,
        mesh=mesh,
        in_specs=(
            P(("slide", "col"), None, None),
            P(("slide", "col"), None),
            P(),
            P(),
            P(),
            P(),
            P(),
            P(),
            P(),
            P(),
        ),
        out_specs=P(("slide", "col"), None, None),
        check_vma=False,
    )
```

```python
import functools

import jax
import jax.numpy as jnp
from jax import lax
from jax.experimental import pallas as pl
from jax.experimental.pallas import tpu as pltpu
from jax.sharding import PartitionSpec as P

HEADS = 8
NO_SCORE = -1e30
F32 = jnp.float32
BF16 = jnp.bfloat16
VMEM = pltpu.VMEM


def dot_nt(a, b):
    return lax.dot_general(a, b, (((1,), (1,)), ((), ())), preferred_element_type=F32)


def dot_nn(a, b):
    return lax.dot_general(a, b, (((1,), (0,)), ((), ())), preferred_element_type=F32)


def head_tokens(pair, half, scale):
    lane = lax.broadcasted_iota(jnp.int32, pair.shape, 1)
    mine = (lane >= 64) if half else (lane < 64)
    return jnp.where(mine, pair.astype(F32) * scale, 0.0).astype(BF16)


def chunk_of_device():
    place = lax.axis_index("col")
    return (place & 1) * 2 + ((place >> 2) & 1)


def chunk_state(index, scale, both, tissue, other_tissue, agents):
    lines = []
    for grid in (tissue, other_tissue):
        bias = jnp.where(grid[...] > 0, 0.0, NO_SCORE).astype(F32)
        lines += [bias[row : row + 1] for row in range(bias.shape[0])]
    bias_line = jnp.concatenate(lines, axis=1)
    pair_agents = agents[:, chunk_lanes(index)]
    keys, vals = both[:, 0:128], both[:, 128:256]
    all_scores = [dot_nt(head_tokens(pair_agents, half, scale), keys) + bias_line for half in range(2)]
    done = []
    for scores in all_scores:
        peak = jnp.max(scores, axis=1, keepdims=True)
        expo = jnp.exp(scores - peak)
        total = jnp.sum(expo, axis=1, keepdims=True)
        done.append((peak, total, dot_nn(expo.astype(BF16), vals)))
    lane = lax.broadcasted_iota(jnp.int32, done[0][2].shape, 1)
    weighted = jnp.where(lane < 64, done[0][2], done[1][2]).T
    stats = jnp.zeros(lane.shape, F32)
    for at, value in enumerate(done[0][:2] + done[1][:2]):
        stats = jnp.where(lane == at, value, stats)
    stats = stats.T
    sides = []
    for at in range(2):
        sides.append((stats[2 * at : 2 * at + 1], stats[2 * at + 1 : 2 * at + 2], weighted[64 * at : 64 * at + 64]))
    return tuple(jnp.concatenate(pair, axis=1) for pair in zip(*sides))


def chunk_lanes(index):
    return pl.ds(pl.multiple_of((chunk_of_device() ^ index) * 128, 128), 128)


def project_chunk(index, mine, other, w_key, w_value, both):
    lanes = chunk_lanes(index)
    weights = jnp.concatenate([w_key[:, lanes], w_value[:, lanes]], axis=1)
    tokens = mine.shape[0]
    block = 512
    for source, start in ((mine, 0), (other, tokens)):
        for at in range(0, tokens, block):
            both[start + at : start + at + block, :] = dot_nn(source[at : at + block, :], weights).astype(BF16)


def project_kernel(mine, other, w_key, w_value, both):
    project_chunk(1, mine, other, w_key, w_value, both)


def second_project_kernel(mine, other, w_key, w_value, first, after, both, values):
    project_chunk(0, mine, other, w_key, w_value, both)
    tokens = mine.shape[0]
    values[:, chunk_lanes(0)] = both[0:tokens, 128:256]
    values[:, chunk_lanes(1)] = first[0:tokens, 128:256]
    lanes = pl.ds(pl.multiple_of((1 - chunk_of_device() // 2) * 256, 256), 256)
    weights = w_value[:, lanes]
    for at in range(0, tokens, 512):
        values[at : at + 512, lanes] = dot_nn(mine[at : at + 512, :], weights).astype(BF16)


def first_band_kernel(scale, both, tissue, other_tissue, agents, payload):
    put_narrow(payload, chunk_state(1, scale, both, tissue, other_tissue, agents))


def second_band_kernel(scale, both, tissue, other_tissue, agents, keep):
    put_wide(keep, chunk_state(0, scale, both, tissue, other_tissue, agents))


def merge(first, second):
    peak_1, total_1, weighted_1 = first
    peak_2, total_2, weighted_2 = second
    peak = jnp.maximum(peak_1, peak_2)
    factor_1 = jnp.exp(peak_1 - peak)
    factor_2 = jnp.exp(peak_2 - peak)
    return peak, total_1 * factor_1 + total_2 * factor_2, weighted_1 * factor_1 + weighted_2 * factor_2


def wide(ref, index=None):
    array = ref[...] if index is None else ref[index]
    return array[64:65], array[65:66], array[0:64]


def thirds(value):
    high = value.astype(BF16).astype(F32)
    rest = value - high
    middle = rest.astype(BF16).astype(F32)
    return high, middle, rest - middle


def put_wide(ref, state):
    peak, total, weighted = state
    row_id = lax.broadcasted_iota(jnp.int32, (8, weighted.shape[1]), 0)
    ref[0:64] = weighted
    ref[64:72] = jnp.where(row_id == 0, peak, jnp.where(row_id == 1, total, 0.0))


def put_narrow(ref, state):
    peak, total, weighted = state
    row_id = lax.broadcasted_iota(jnp.int32, (16, weighted.shape[1]), 0)
    stats = jnp.zeros((16, weighted.shape[1]), F32)
    for at, part in enumerate(thirds(peak) + thirds(total)):
        stats = jnp.where(row_id == at, part, stats)
    ref[0:64] = weighted.astype(BF16)
    ref[64:80] = stats.astype(BF16)


def narrow(ref):
    stats = ref[64:80].astype(F32)
    peak = stats[0:1] + stats[1:2] + stats[2:3]
    total = stats[3:4] + stats[4:5] + stats[5:6]
    return peak, total, ref[0:64].astype(F32)


def next_merge_kernel(held, got, before, own, payload):
    state = merge(wide(held), narrow(got))
    put_narrow(payload, state)
    put_wide(own, state)


def last_merge_kernel(held, got, before, agent_values):
    _, total, weighted = merge(wide(held), narrow(got))
    agent_values[...] = (weighted / total).astype(BF16)


def token_kernel(scale, patches, w_query, agents, after, weights, queries):
    heads = weights.shape[1] // agents.shape[0]
    queries[...] = dot_nn(patches[...], w_query[...]).astype(BF16)

    def scores_of(head):
        lanes = slice(head // 2 * 128, head // 2 * 128 + 128)
        return dot_nt(queries[:, lanes], head_tokens(agents[:, lanes], head % 2, scale))

    ahead = scores_of(0)
    for head in range(heads):
        scores = ahead
        if head + 1 < heads:
            ahead = scores_of(head + 1)
        expo = jnp.exp(scores - jnp.max(scores, axis=1, keepdims=True))
        part = expo * (1.0 / jnp.sum(expo, axis=1, keepdims=True))
        weights[:, head * 256 : head * 256 + 256] = part.astype(BF16)


def pass_kernel(border, same):
    del border, same


def halo_kernel(other, outer, w_value, after, above, below):
    rows = outer.shape[0]
    odd = (lax.axis_index("col") % 2) == 1
    inner_part = other[pl.ds(pl.multiple_of((lax.axis_index("col") % 2) * (other.shape[0] - rows), 128), rows), :]
    inner = dot_nn(inner_part, w_value[...]).astype(BF16)
    outside = dot_nn(outer[...], w_value[...]).astype(BF16)
    above[...] = jnp.where(odd, inner, outside)
    below[...] = jnp.where(odd, outside, inner)


def relay_kernel(own, near, after, both):
    both[0:64] = own[...]
    both[64:128] = near[...]


TAP_COUNTS = (2, 2, 2, 2, 2, 2, 2, 2, 1)


def split_rows(rows):
    return [
        [rows[at] - rows[at + 1] for at in range(0, len(rows) - 1, 2)],
        [rows[at + 1] for at in range(0, len(rows) - 1, 2)],
        [rows[at + 2] - rows[at + 1] for at in range(0, len(rows) - 2, 2)],
    ]


def split_taps(taps):
    even, odd = taps[0::2], taps[1::2]
    both = [even[at] + odd[at] if at < len(odd) else even[at] for at in range(len(even))]
    return [even, both, odd]


def joined_rows(first, second, third):
    return [row for a, b, c in zip(first, second, third) for row in (a + b, b + c)]


def taps_kernel(seven, five, three, after, taps):
    for q in range(7):
        column = [seven[p, q : q + 1, :] for p in range(7)]
        if 1 <= q <= 5:
            column[1:6] = [tap + five[p, q - 1 : q, :] for p, tap in enumerate(column[1:6])]
        if 2 <= q <= 4:
            column[2:5] = [tap + three[p, q - 2 : q - 1, :] for p, tap in enumerate(column[2:5])]
        parts = [tap for part in split_taps(column) for piece in split_taps(part) for tap in piece]
        parts += [jnp.zeros_like(parts[0])] * (taps.shape[1] - len(parts))
        taps[q] = jnp.concatenate(parts, axis=0)


def conv_kernel(first_lane, values, above, below, all_taps, after, position, points, taps):
    width = position.shape[1]
    lanes, step = 128, 16
    tap_count = sum(TAP_COUNTS)
    zero = jnp.zeros((8, lanes), F32)
    for group in range(position.shape[2] // lanes):
        here = slice(first_lane + group * lanes, first_lane + (group + 1) * lanes)
        there = slice(group * lanes, (group + 1) * lanes)
        for q in range(7):
            for at in range(tap_count):
                taps[q, at] = jnp.broadcast_to(all_taps[q, at : at + 1, here], (8, lanes))
        for at in range(points.shape[0]):
            points[at, 0:8, :] = zero
            points[at, 8 + width : 16 + width, :] = zero
        for at in range(0, width, step):
            rows = []
            for ref in (above, values, below):
                for row in range(0, ref.shape[0], width):
                    rows.append(ref[row + at : row + at + step, here].astype(F32))
            even, odd = rows[0::2], rows[1::2]
            streams = (
                [a - b for a, b in zip(even, odd)],
                odd,
                [a - b for a, b in zip(even[1:], odd)],
            )
            parts = [plane for stream in streams for piece in split_rows(stream) for plane in piece]
            for index, plane in enumerate(parts):
                points[index, 8 + at : 8 + at + step, :] = plane
        for at in range(0, width, step):
            columns = (at, at + 8)
            sums = [[[zero, zero] for _ in TAP_COUNTS] for _ in columns]
            for q in range(7):
                first_point = first_tap = 0
                for piece, count in enumerate(TAP_COUNTS):
                    tap = [taps[q, first_tap + k] for k in range(count)]
                    for total, column in zip(sums, columns):
                        start = column + 5 + q
                        point = [points[first_point + k, start : start + 8, :] for k in range(count + 1)]
                        for out in range(2):
                            for k in range(count):
                                total[piece][out] = total[piece][out] + point[out + k] * tap[k]
                    first_point += count + 1
                    first_tap += count
            for total, column in zip(sums, columns):
                thirds_of = [joined_rows(*total[3 * part : 3 * part + 3]) for part in range(3)]
                for row, plane in enumerate(joined_rows(*thirds_of)):
                    position[row, column : column + 8, there] = plane


def blend_block(here, weights, position, spread, w_out, rows):
    parts = [dot_nt(weights[here, at * 512 : at * 512 + 512], spread[at]) for at in range(2)]
    blended = (jnp.concatenate(parts, axis=1) + position[here, :]).astype(BF16)
    return dot_nn(blended, w_out[rows, :])


def fill_spread(pair, spread):
    spread[...] = jnp.zeros_like(spread)
    for index in range(2):
        place = (chunk_of_device() % 2) ^ index
        for half in range(2):
            cols = slice(half * 256, half * 256 + 256)
            spread[place, half * 64 : half * 64 + 64, cols] = pair[index * 64 : index * 64 + 64, cols]


def own_out_kernel(weights_low, weights_high, pair, position_low, position_high, w_out, partial, spread):
    fill_spread(pair, spread)
    block = partial.shape[0] // 2
    for group, (weights, position) in enumerate(((weights_low, position_low), (weights_high, position_high))):

        @pl.when(chunk_of_device() // 2 == group)
        def _(group=group, weights=weights, position=position):
            rows = slice(group * 256, group * 256 + 256)
            for index in range(2):
                here = slice(index * block, index * block + block)
                partial[here, :] = blend_block(here, weights, position, spread, w_out, rows)


def out_kernel(
    weights_low, weights_high, pair, position_low, position_high, w_out, partial, mixed, spread, buffer, sems
):
    fill_spread(pair, spread)
    block = partial.shape[0] // 2
    copies = []
    for index in range(2):
        here = slice(index * block, index * block + block)
        for group, (weights, position) in enumerate(((weights_low, position_low), (weights_high, position_high))):

            @pl.when(chunk_of_device() // 2 != group)
            def _(group=group, weights=weights, position=position, here=here):
                rows = slice(group * 256, group * 256 + 256)
                total = partial[here, :] + blend_block(here, weights, position, spread, w_out, rows)
                buffer[here, :] = total.astype(BF16)

        copies.append(pltpu.make_async_copy(buffer.at[here, :], mixed.at[here, :], sems.at[index]))
        copies[-1].start()
    for copy in copies:
        copy.wait()


def params(megabytes=48):
    return pltpu.CompilerParams(vmem_limit_bytes=megabytes << 20)


def cost(flops, moved, exps=0):
    return pl.CostEstimate(flops=int(flops), bytes_accessed=int(moved), transcendentals=int(exps))


def shape(dims, dtype):
    return jax.ShapeDtypeStruct(dims, dtype)


def exchange(x, bit):
    peers = lax.axis_size("col")
    return lax.ppermute(x, "col", [(i, i ^ bit) for i in range(peers)])


def on_device(patches, tissue, w_query, w_key, w_value, w_out, agent_tokens, seven, five, three):
    band_rows, width, dim = patches.shape
    tokens = band_rows * width
    agents = agent_tokens.shape[0]
    half_dim = dim // 2
    scale = (dim // HEADS) ** (-0.5)
    flat = patches.reshape(tokens, dim)
    peers = lax.axis_size("col")
    place = lax.axis_index("col")
    odd = place % 2
    vmem = pl.BlockSpec(memory_space=VMEM)
    anywhere = pl.BlockSpec(memory_space=pl.ANY)

    other = exchange(flat, 1)
    other_tissue = exchange(tissue, 1)

    border = lax.dynamic_slice_in_dim(flat, odd * (tokens - 3 * width), 3 * width, 0)
    border = pl.pallas_call(
        pass_kernel,
        out_shape=shape((3 * width, dim), BF16),
        in_specs=[anywhere],
        out_specs=anywhere,
        input_output_aliases={0: 0},
        compiler_params=params(16),
        cost_estimate=cost(1e11, 1e6),
        name="pass",
    )(border)
    rest = [(i, i + 1) for i in range(1, peers - 1, 2)]
    outer = lax.ppermute(border, "col", rest + [(j, i) for i, j in rest])

    wide_shape, narrow_shape = shape((72, 512), F32), shape((80, 512), BF16)
    both_bands = shape((2 * tokens, half_dim), BF16)
    first = pl.pallas_call(
        project_kernel,
        out_shape=both_bands,
        in_specs=[vmem] * 4,
        out_specs=vmem,
        compiler_params=params(20),
        cost_estimate=cost(6e8, 4e6),
        name="project",
    )(flat, other, w_key, w_value)

    def band(kernel, out_shape, both):
        return pl.pallas_call(
            functools.partial(kernel, scale),
            out_shape=out_shape,
            in_specs=[vmem] * 4,
            out_specs=vmem,
            compiler_params=params(20),
            cost_estimate=cost(6e8, 4e6, 1e6),
            name="band",
        )(both, tissue, other_tissue, agent_tokens)

    payload = band(first_band_kernel, narrow_shape, first)

    def token(at, after):
        lanes = slice(at * half_dim, (at + 1) * half_dim)
        return pl.pallas_call(
            functools.partial(token_kernel, scale),
            out_shape=shape((tokens, HEADS // 2 * agents), BF16),
            grid=(1,),
            in_specs=[
                vmem,
                pl.BlockSpec((dim, half_dim), lambda i: (0, at)),
                pl.BlockSpec((agents, half_dim), lambda i: (0, at)),
                anywhere,
            ],
            out_specs=vmem,
            scratch_shapes=[VMEM((tokens, half_dim), BF16)],
            compiler_params=params(20),
            cost_estimate=cost(2e9, 6e6, 1e6),
            name="token",
        )(flat, w_query, agent_tokens, after)

    def conv(at, after):
        return pl.pallas_call(
            functools.partial(conv_kernel, at * half_dim),
            out_shape=shape((band_rows, width, half_dim), F32),
            in_specs=[vmem] * 4 + [anywhere],
            out_specs=vmem,
            scratch_shapes=[
                VMEM((sum(TAP_COUNTS) + len(TAP_COUNTS), width + 16, 128), F32),
                VMEM((7, sum(TAP_COUNTS), 8, 128), F32),
            ],
            compiler_params=params(20),
            cost_estimate=cost(3e9, 4e6),
            name="conv",
        )(values, above, below, taps, after).reshape(tokens, half_dim)

    hop = dict(in_specs=[vmem, vmem, anywhere], compiler_params=params(16), cost_estimate=cost(1e6, 1e6))

    def next_merge(held, got, before):
        return pl.pallas_call(
            next_merge_kernel, out_shape=(wide_shape, narrow_shape), out_specs=[vmem] * 2, name="merge_next", **hop
        )(held, got, before)

    got = exchange(payload, 4)
    second, values = pl.pallas_call(
        second_project_kernel,
        out_shape=(both_bands, shape((tokens, dim), BF16)),
        in_specs=[vmem] * 5 + [anywhere],
        out_specs=[vmem] * 2,
        compiler_params=params(20),
        cost_estimate=cost(8e8, 4e6),
        name="project_second",
    )(flat, other, w_key, w_value, first, payload)
    held = band(second_band_kernel, wide_shape, second)
    taps = pl.pallas_call(
        taps_kernel,
        out_shape=shape((7, 24, dim), F32),
        in_specs=[vmem] * 3 + [anywhere],
        out_specs=vmem,
        compiler_params=params(16),
        cost_estimate=cost(5e8, 1e6),
        name="taps",
    )(seven, five, three, payload)
    held, payload = next_merge(held, got, taps)
    bit = 8
    weights_low = None
    while bit < peers:
        got = exchange(payload, bit)
        if weights_low is None:
            weights_low = token(0, payload)
            above, below = pl.pallas_call(
                halo_kernel,
                out_shape=(shape((3 * width, dim), BF16), shape((3 * width, dim), BF16)),
                in_specs=[vmem] * 3 + [anywhere],
                out_specs=[vmem] * 2,
                compiler_params=params(16),
                cost_estimate=cost(4e8, 2e6),
                name="halo",
            )(other, outer, w_value, weights_low)
            weights_high = token(1, above)
        held, payload = next_merge(held, got, weights_high)
        bit *= 2
    got = exchange(payload, 2)
    position_low = conv(0, payload)
    own = pl.pallas_call(
        last_merge_kernel, out_shape=shape((64, 512), BF16), out_specs=vmem, name="merge_last", **hop
    )(held, got, position_low)
    near = exchange(own, 4)
    position_high = conv(1, own)
    pair = pl.pallas_call(
        relay_kernel,
        out_shape=shape((128, 512), BF16),
        in_specs=[vmem, vmem, anywhere],
        out_specs=vmem,
        compiler_params=params(16),
        cost_estimate=cost(1e6, 1e6),
        name="relay",
    )(own, near, position_high)
    other_pair = exchange(pair, 1)

    partial = pl.pallas_call(
        own_out_kernel,
        out_shape=shape((tokens, dim), F32),
        in_specs=[vmem] * 6,
        out_specs=vmem,
        scratch_shapes=[VMEM((2, 128, 512), BF16)],
        compiler_params=params(20),
        cost_estimate=cost(1.1e9, 4e6),
        name="own_out",
    )(weights_low, weights_high, pair, position_low, position_high, w_out)
    mixed = pl.pallas_call(
        out_kernel,
        out_shape=shape((tokens, dim), BF16),
        in_specs=[vmem] * 7,
        out_specs=anywhere,
        scratch_shapes=[
            VMEM((2, 128, 512), BF16),
            VMEM((tokens, dim), BF16),
            pltpu.SemaphoreType.DMA((2,)),
        ],
        compiler_params=params(20),
        cost_estimate=cost(1.1e9, 8e6),
        name="out",
    )(weights_low, weights_high, other_pair, position_low, position_high, w_out, partial)
    return mixed.reshape(band_rows, width, dim)


def solution(mesh):
    return jax.shard_map(
        on_device,
        mesh=mesh,
        in_specs=(
            P(("slide", "col"), None, None),
            P(("slide", "col"), None),
            P(),
            P(),
            P(),
            P(),
            P(),
            P(),
            P(),
            P(),
        ),
        out_specs=P(("slide", "col"), None, None),
        check_vma=False,
    )
```

```python
import functools

import jax
import jax.numpy as jnp
from jax import lax
from jax.experimental import pallas as pl
from jax.experimental.pallas import tpu as pltpu
from jax.sharding import PartitionSpec as P

HEADS = 8
NO_SCORE = -1e30
F32 = jnp.float32
BF16 = jnp.bfloat16
VMEM = pltpu.VMEM


def dot_nt(a, b):
    return lax.dot_general(a, b, (((1,), (1,)), ((), ())), preferred_element_type=F32)


def dot_nn(a, b):
    return lax.dot_general(a, b, (((1,), (0,)), ((), ())), preferred_element_type=F32)


def head_tokens(pair, half, scale):
    lane = lax.broadcasted_iota(jnp.int32, pair.shape, 1)
    mine = (lane >= 64) if half else (lane < 64)
    return jnp.where(mine, pair.astype(F32) * scale, 0.0).astype(BF16)


def chunk_of_device():
    place = lax.axis_index("col")
    return (place & 1) * 2 + ((place >> 2) & 1)


def chunk_state(index, scale, both, tissue, other_tissue, agents):
    lines = []
    for grid in (tissue, other_tissue):
        bias = jnp.where(grid[...] > 0, 0.0, NO_SCORE).astype(F32)
        lines += [bias[row : row + 1] for row in range(bias.shape[0])]
    bias_line = jnp.concatenate(lines, axis=1)
    pair_agents = agents[:, chunk_lanes(index)]
    keys, vals = both[:, 0:128], both[:, 128:256]
    all_scores = [dot_nt(head_tokens(pair_agents, half, scale), keys) + bias_line for half in range(2)]
    done = []
    for scores in all_scores:
        peak = jnp.max(scores, axis=1, keepdims=True)
        expo = jnp.exp(scores - peak)
        total = jnp.sum(expo, axis=1, keepdims=True)
        done.append((peak, total, dot_nn(expo.astype(BF16), vals)))
    lane = lax.broadcasted_iota(jnp.int32, done[0][2].shape, 1)
    weighted = jnp.where(lane < 64, done[0][2], done[1][2]).T
    stats = jnp.zeros(lane.shape, F32)
    for at, value in enumerate(done[0][:2] + done[1][:2]):
        stats = jnp.where(lane == at, value, stats)
    stats = stats.T
    sides = []
    for at in range(2):
        sides.append((stats[2 * at : 2 * at + 1], stats[2 * at + 1 : 2 * at + 2], weighted[64 * at : 64 * at + 64]))
    return tuple(jnp.concatenate(pair, axis=1) for pair in zip(*sides))


def chunk_lanes(index):
    return pl.ds(pl.multiple_of((chunk_of_device() ^ index) * 128, 128), 128)


def project_chunk(index, mine, other, w_key, w_value, both):
    lanes = chunk_lanes(index)
    weights = jnp.concatenate([w_key[:, lanes], w_value[:, lanes]], axis=1)
    tokens = mine.shape[0]
    block = 512
    for source, start in ((mine, 0), (other, tokens)):
        for at in range(0, tokens, block):
            both[start + at : start + at + block, :] = dot_nn(source[at : at + block, :], weights).astype(BF16)


def project_kernel(mine, other, w_key, w_value, both):
    project_chunk(1, mine, other, w_key, w_value, both)


def second_project_kernel(mine, other, w_key, w_value, first, after, both, values):
    project_chunk(0, mine, other, w_key, w_value, both)
    tokens = mine.shape[0]
    values[:, chunk_lanes(0)] = both[0:tokens, 128:256]
    values[:, chunk_lanes(1)] = first[0:tokens, 128:256]
    lanes = pl.ds(pl.multiple_of((1 - chunk_of_device() // 2) * 256, 256), 256)
    weights = w_value[:, lanes]
    for at in range(0, tokens, 512):
        values[at : at + 512, lanes] = dot_nn(mine[at : at + 512, :], weights).astype(BF16)


def first_band_kernel(scale, both, tissue, other_tissue, agents, payload):
    put_narrow(payload, chunk_state(1, scale, both, tissue, other_tissue, agents))


def second_band_kernel(scale, both, tissue, other_tissue, agents, keep):
    put_wide(keep, chunk_state(0, scale, both, tissue, other_tissue, agents))


def merge(first, second):
    peak_1, total_1, weighted_1 = first
    peak_2, total_2, weighted_2 = second
    peak = jnp.maximum(peak_1, peak_2)
    factor_1 = jnp.exp(peak_1 - peak)
    factor_2 = jnp.exp(peak_2 - peak)
    return peak, total_1 * factor_1 + total_2 * factor_2, weighted_1 * factor_1 + weighted_2 * factor_2


def wide(ref, index=None):
    array = ref[...] if index is None else ref[index]
    return array[64:65], array[65:66], array[0:64]


def thirds(value):
    high = value.astype(BF16).astype(F32)
    rest = value - high
    middle = rest.astype(BF16).astype(F32)
    return high, middle, rest - middle


def put_wide(ref, state):
    peak, total, weighted = state
    row_id = lax.broadcasted_iota(jnp.int32, (8, weighted.shape[1]), 0)
    ref[0:64] = weighted
    ref[64:72] = jnp.where(row_id == 0, peak, jnp.where(row_id == 1, total, 0.0))


def put_narrow(ref, state):
    peak, total, weighted = state
    row_id = lax.broadcasted_iota(jnp.int32, (8, weighted.shape[1]), 0)
    stats = jnp.zeros((8, weighted.shape[1]), F32)
    for at, part in enumerate(thirds(peak) + thirds(total)):
        stats = jnp.where(row_id == at, part, stats)
    ref[...] = jnp.concatenate([weighted, stats], axis=0).astype(BF16)


def narrow(ref):
    rows = ref[...].astype(F32)
    peak = rows[64:65] + rows[65:66] + rows[66:67]
    total = rows[67:68] + rows[68:69] + rows[69:70]
    return peak, total, rows[0:64]


def next_merge_kernel(held, got, before, own, payload):
    state = merge(wide(held), narrow(got))
    put_narrow(payload, state)
    put_wide(own, state)


def last_merge_kernel(held, got, before, agent_values):
    _, total, weighted = merge(wide(held), narrow(got))
    agent_values[...] = (weighted / total).astype(BF16)


def token_kernel(scale, patches, w_query, agents, after, weights, queries):
    heads = weights.shape[1] // agents.shape[0]
    queries[...] = dot_nn(patches[...], w_query[...]).astype(BF16)

    def scores_of(head):
        lanes = slice(head // 2 * 128, head // 2 * 128 + 128)
        return dot_nt(queries[:, lanes], head_tokens(agents[:, lanes], head % 2, scale))

    ahead = scores_of(0)
    for head in range(heads):
        scores = ahead
        if head + 1 < heads:
            ahead = scores_of(head + 1)
        expo = jnp.exp(scores - jnp.max(scores, axis=1, keepdims=True))
        part = expo * (1.0 / jnp.sum(expo, axis=1, keepdims=True))
        weights[:, head * 256 : head * 256 + 256] = part.astype(BF16)


def pass_kernel(border, same):
    del border, same


def halo_kernel(other, outer, w_value, after, above, below):
    rows = outer.shape[0]
    odd = (lax.axis_index("col") % 2) == 1
    inner_part = other[pl.ds(pl.multiple_of((lax.axis_index("col") % 2) * (other.shape[0] - rows), 128), rows), :]
    inner = dot_nn(inner_part, w_value[...]).astype(BF16)
    outside = dot_nn(outer[...], w_value[...]).astype(BF16)
    above[...] = jnp.where(odd, inner, outside)
    below[...] = jnp.where(odd, outside, inner)


def relay_kernel(own, near, after, both):
    both[0:64] = own[...]
    both[64:128] = near[...]


TAP_COUNTS = (2, 2, 2, 2, 2, 2, 2, 2, 1)


def split_rows(rows):
    return [
        [rows[at] - rows[at + 1] for at in range(0, len(rows) - 1, 2)],
        [rows[at + 1] for at in range(0, len(rows) - 1, 2)],
        [rows[at + 2] - rows[at + 1] for at in range(0, len(rows) - 2, 2)],
    ]


def split_taps(taps):
    even, odd = taps[0::2], taps[1::2]
    both = [even[at] + odd[at] if at < len(odd) else even[at] for at in range(len(even))]
    return [even, both, odd]


def joined_rows(first, second, third):
    return [row for a, b, c in zip(first, second, third) for row in (a + b, b + c)]


def taps_kernel(seven, five, three, after, taps):
    for q in range(7):
        column = [seven[p, q : q + 1, :] for p in range(7)]
        if 1 <= q <= 5:
            column[1:6] = [tap + five[p, q - 1 : q, :] for p, tap in enumerate(column[1:6])]
        if 2 <= q <= 4:
            column[2:5] = [tap + three[p, q - 2 : q - 1, :] for p, tap in enumerate(column[2:5])]
        parts = [tap for part in split_taps(column) for piece in split_taps(part) for tap in piece]
        parts += [jnp.zeros_like(parts[0])] * (taps.shape[1] - len(parts))
        taps[q] = jnp.concatenate(parts, axis=0)


def conv_kernel(first_lane, values, above, below, all_taps, after, position, points, taps):
    width = position.shape[1]
    lanes, step = 128, 16
    tap_count = sum(TAP_COUNTS)
    zero = jnp.zeros((8, lanes), F32)
    for group in range(position.shape[2] // lanes):
        here = slice(first_lane + group * lanes, first_lane + (group + 1) * lanes)
        there = slice(group * lanes, (group + 1) * lanes)
        for q in range(7):
            for at in range(tap_count):
                taps[q, at] = jnp.broadcast_to(all_taps[q, at : at + 1, here], (8, lanes))
        for at in range(points.shape[0]):
            points[at, 0:8, :] = zero
            points[at, 8 + width : 16 + width, :] = zero
        for at in range(0, width, step):
            rows = []
            for ref in (above, values, below):
                for row in range(0, ref.shape[0], width):
                    rows.append(ref[row + at : row + at + step, here].astype(F32))
            even, odd = rows[0::2], rows[1::2]
            streams = (
                [a - b for a, b in zip(even, odd)],
                odd,
                [a - b for a, b in zip(even[1:], odd)],
            )
            parts = [plane for stream in streams for piece in split_rows(stream) for plane in piece]
            for index, plane in enumerate(parts):
                points[index, 8 + at : 8 + at + step, :] = plane
        for at in range(0, width, step):
            columns = (at, at + 8)
            sums = [[[zero, zero] for _ in TAP_COUNTS] for _ in columns]
            for q in range(7):
                first_point = first_tap = 0
                for piece, count in enumerate(TAP_COUNTS):
                    tap = [taps[q, first_tap + k] for k in range(count)]
                    for total, column in zip(sums, columns):
                        start = column + 5 + q
                        point = [points[first_point + k, start : start + 8, :] for k in range(count + 1)]
                        for out in range(2):
                            for k in range(count):
                                total[piece][out] = total[piece][out] + point[out + k] * tap[k]
                    first_point += count + 1
                    first_tap += count
            for total, column in zip(sums, columns):
                thirds_of = [joined_rows(*total[3 * part : 3 * part + 3]) for part in range(3)]
                for row, plane in enumerate(joined_rows(*thirds_of)):
                    position[row, column : column + 8, there] = plane


def blend_block(here, weights, position, spread, w_out, rows):
    parts = [dot_nt(weights[here, at * 512 : at * 512 + 512], spread[at]) for at in range(2)]
    blended = (jnp.concatenate(parts, axis=1) + position[here, :]).astype(BF16)
    return dot_nn(blended, w_out[rows, :])


def fill_spread(pair, spread):
    spread[...] = jnp.zeros_like(spread)
    for index in range(2):
        place = (chunk_of_device() % 2) ^ index
        for half in range(2):
            cols = slice(half * 256, half * 256 + 256)
            spread[place, half * 64 : half * 64 + 64, cols] = pair[index * 64 : index * 64 + 64, cols]


def own_out_kernel(weights_low, weights_high, pair, position_low, position_high, w_out, partial, spread):
    fill_spread(pair, spread)
    block = partial.shape[0] // 2
    for group, (weights, position) in enumerate(((weights_low, position_low), (weights_high, position_high))):

        @pl.when(chunk_of_device() // 2 == group)
        def _(group=group, weights=weights, position=position):
            rows = slice(group * 256, group * 256 + 256)
            for index in range(2):
                here = slice(index * block, index * block + block)
                partial[here, :] = blend_block(here, weights, position, spread, w_out, rows)


def out_kernel(
    weights_low, weights_high, pair, position_low, position_high, w_out, partial, mixed, spread, buffer, sems
):
    fill_spread(pair, spread)
    block = partial.shape[0] // sems.shape[0]
    copies = []
    for index in range(sems.shape[0]):
        here = slice(index * block, index * block + block)
        copies.append((here, pltpu.make_async_copy(buffer.at[here, :], mixed.at[here, :], sems.at[index])))
    for group, (weights, position) in enumerate(((weights_low, position_low), (weights_high, position_high))):

        @pl.when(chunk_of_device() // 2 != group)
        def _(group=group, weights=weights, position=position):
            rows = slice(group * 256, group * 256 + 256)
            for here, copy in copies:
                total = partial[here, :] + blend_block(here, weights, position, spread, w_out, rows)
                buffer[here, :] = total.astype(BF16)
                copy.start()

    for _, copy in copies:
        copy.wait()


def params(megabytes=48):
    return pltpu.CompilerParams(vmem_limit_bytes=megabytes << 20)


def cost(flops, moved, exps=0):
    return pl.CostEstimate(flops=int(flops), bytes_accessed=int(moved), transcendentals=int(exps))


def shape(dims, dtype):
    return jax.ShapeDtypeStruct(dims, dtype)


def exchange(x, bit):
    peers = lax.axis_size("col")
    return lax.ppermute(x, "col", [(i, i ^ bit) for i in range(peers)])


def on_device(patches, tissue, w_query, w_key, w_value, w_out, agent_tokens, seven, five, three):
    band_rows, width, dim = patches.shape
    tokens = band_rows * width
    agents = agent_tokens.shape[0]
    half_dim = dim // 2
    scale = (dim // HEADS) ** (-0.5)
    flat = patches.reshape(tokens, dim)
    peers = lax.axis_size("col")
    place = lax.axis_index("col")
    odd = place % 2
    vmem = pl.BlockSpec(memory_space=VMEM)
    anywhere = pl.BlockSpec(memory_space=pl.ANY)

    other = exchange(flat, 1)
    other_tissue = exchange(tissue, 1)

    border = lax.dynamic_slice_in_dim(flat, odd * (tokens - 3 * width), 3 * width, 0)
    border = pl.pallas_call(
        pass_kernel,
        out_shape=shape((3 * width, dim), BF16),
        in_specs=[anywhere],
        out_specs=anywhere,
        input_output_aliases={0: 0},
        compiler_params=params(16),
        cost_estimate=cost(1e11, 1e6),
        name="pass",
    )(border)
    rest = [(i, i + 1) for i in range(1, peers - 1, 2)]
    outer = lax.ppermute(border, "col", rest + [(j, i) for i, j in rest])

    wide_shape, narrow_shape = shape((72, 512), F32), shape((72, 512), BF16)
    both_bands = shape((2 * tokens, half_dim), BF16)
    first = pl.pallas_call(
        project_kernel,
        out_shape=both_bands,
        in_specs=[vmem] * 4,
        out_specs=vmem,
        compiler_params=params(20),
        cost_estimate=cost(6e8, 4e6),
        name="project",
    )(flat, other, w_key, w_value)

    def band(kernel, out_shape, both):
        return pl.pallas_call(
            functools.partial(kernel, scale),
            out_shape=out_shape,
            in_specs=[vmem] * 4,
            out_specs=vmem,
            compiler_params=params(20),
            cost_estimate=cost(6e8, 4e6, 1e6),
            name="band",
        )(both, tissue, other_tissue, agent_tokens)

    payload = band(first_band_kernel, narrow_shape, first)

    def token(at, after):
        lanes = slice(at * half_dim, (at + 1) * half_dim)
        return pl.pallas_call(
            functools.partial(token_kernel, scale),
            out_shape=shape((tokens, HEADS // 2 * agents), BF16),
            grid=(1,),
            in_specs=[
                vmem,
                pl.BlockSpec((dim, half_dim), lambda i: (0, at)),
                pl.BlockSpec((agents, half_dim), lambda i: (0, at)),
                anywhere,
            ],
            out_specs=vmem,
            scratch_shapes=[VMEM((tokens, half_dim), BF16)],
            compiler_params=params(20),
            cost_estimate=cost(2e9, 6e6, 1e6),
            name="token",
        )(flat, w_query, agent_tokens, after)

    def conv(at, after):
        return pl.pallas_call(
            functools.partial(conv_kernel, at * half_dim),
            out_shape=shape((band_rows, width, half_dim), F32),
            in_specs=[vmem] * 4 + [anywhere],
            out_specs=vmem,
            scratch_shapes=[
                VMEM((sum(TAP_COUNTS) + len(TAP_COUNTS), width + 16, 128), F32),
                VMEM((7, sum(TAP_COUNTS), 8, 128), F32),
            ],
            compiler_params=params(20),
            cost_estimate=cost(3e9, 4e6),
            name="conv",
        )(values, above, below, taps, after).reshape(tokens, half_dim)

    hop = dict(in_specs=[vmem, vmem, anywhere], compiler_params=params(16), cost_estimate=cost(1e6, 1e6))

    def next_merge(held, got, before):
        return pl.pallas_call(
            next_merge_kernel, out_shape=(wide_shape, narrow_shape), out_specs=[vmem] * 2, name="merge_next", **hop
        )(held, got, before)

    got = exchange(payload, 4)
    second, values = pl.pallas_call(
        second_project_kernel,
        out_shape=(both_bands, shape((tokens, dim), BF16)),
        in_specs=[vmem] * 5 + [anywhere],
        out_specs=[vmem] * 2,
        compiler_params=params(20),
        cost_estimate=cost(8e8, 4e6),
        name="project_second",
    )(flat, other, w_key, w_value, first, payload)
    held = band(second_band_kernel, wide_shape, second)
    taps = pl.pallas_call(
        taps_kernel,
        out_shape=shape((7, 24, dim), F32),
        in_specs=[vmem] * 3 + [anywhere],
        out_specs=vmem,
        compiler_params=params(16),
        cost_estimate=cost(5e8, 1e6),
        name="taps",
    )(seven, five, three, payload)
    held, payload = next_merge(held, got, taps)
    bit = 8
    weights_low = None
    while bit < peers:
        got = exchange(payload, bit)
        if weights_low is None:
            weights_low = token(0, payload)
            above, below = pl.pallas_call(
                halo_kernel,
                out_shape=(shape((3 * width, dim), BF16), shape((3 * width, dim), BF16)),
                in_specs=[vmem] * 3 + [anywhere],
                out_specs=[vmem] * 2,
                compiler_params=params(16),
                cost_estimate=cost(4e8, 2e6),
                name="halo",
            )(other, outer, w_value, weights_low)
            weights_high = token(1, above)
        held, payload = next_merge(held, got, weights_high)
        bit *= 2
    got = exchange(payload, 2)
    position_low = conv(0, payload)
    own = pl.pallas_call(
        last_merge_kernel, out_shape=shape((64, 512), BF16), out_specs=vmem, name="merge_last", **hop
    )(held, got, position_low)
    near = exchange(own, 4)
    position_high = conv(1, own)
    pair = pl.pallas_call(
        relay_kernel,
        out_shape=shape((128, 512), BF16),
        in_specs=[vmem, vmem, anywhere],
        out_specs=vmem,
        compiler_params=params(16),
        cost_estimate=cost(1e6, 1e6),
        name="relay",
    )(own, near, position_high)
    other_pair = exchange(pair, 1)

    partial = pl.pallas_call(
        own_out_kernel,
        out_shape=shape((tokens, dim), F32),
        in_specs=[vmem] * 6,
        out_specs=vmem,
        scratch_shapes=[VMEM((2, 128, 512), BF16)],
        compiler_params=params(20),
        cost_estimate=cost(1.1e9, 4e6),
        name="own_out",
    )(weights_low, weights_high, pair, position_low, position_high, w_out)
    mixed = pl.pallas_call(
        out_kernel,
        out_shape=shape((tokens, dim), BF16),
        in_specs=[vmem] * 7,
        out_specs=anywhere,
        scratch_shapes=[
            VMEM((2, 128, 512), BF16),
            VMEM((tokens, dim), BF16),
            pltpu.SemaphoreType.DMA((2,)),
        ],
        compiler_params=params(20),
        cost_estimate=cost(1.1e9, 8e6),
        name="out",
    )(weights_low, weights_high, other_pair, position_low, position_high, w_out, partial)
    return mixed.reshape(band_rows, width, dim)


def solution(mesh):
    return jax.shard_map(
        on_device,
        mesh=mesh,
        in_specs=(
            P(("slide", "col"), None, None),
            P(("slide", "col"), None),
            P(),
            P(),
            P(),
            P(),
            P(),
            P(),
            P(),
            P(),
        ),
        out_specs=P(("slide", "col"), None, None),
        check_vma=False,
    )
```

```python
import functools

import jax
import jax.numpy as jnp
from jax import lax
from jax.experimental import pallas as pl
from jax.experimental.pallas import tpu as pltpu
from jax.sharding import PartitionSpec as P

HEADS = 8
NO_SCORE = -1e30
F32 = jnp.float32
BF16 = jnp.bfloat16
VMEM = pltpu.VMEM


def dot_nt(a, b):
    return lax.dot_general(a, b, (((1,), (1,)), ((), ())), preferred_element_type=F32)


def dot_nn(a, b):
    return lax.dot_general(a, b, (((1,), (0,)), ((), ())), preferred_element_type=F32)


def head_tokens(pair, half, scale):
    lane = lax.broadcasted_iota(jnp.int32, pair.shape, 1)
    mine = (lane >= 64) if half else (lane < 64)
    return jnp.where(mine, pair.astype(F32) * scale, 0.0).astype(BF16)


def chunk_of_device():
    place = lax.axis_index("col")
    return (place & 1) * 2 + ((place >> 2) & 1)


def chunk_state(index, scale, both, tissue, other_tissue, agents):
    lines = []
    for grid in (tissue, other_tissue):
        bias = jnp.where(grid[...] > 0, 0.0, NO_SCORE).astype(F32)
        lines += [bias[row : row + 1] for row in range(bias.shape[0])]
    bias_line = jnp.concatenate(lines, axis=1)
    pair_agents = agents[:, chunk_lanes(index)]
    keys, vals = both[:, 0:128], both[:, 128:256]
    all_scores = [dot_nt(head_tokens(pair_agents, half, scale), keys) + bias_line for half in range(2)]
    done = []
    for scores in all_scores:
        peak = jnp.max(scores, axis=1, keepdims=True)
        expo = jnp.exp(scores - peak)
        total = jnp.sum(expo, axis=1, keepdims=True)
        done.append((peak, total, dot_nn(expo.astype(BF16), vals)))
    lane = lax.broadcasted_iota(jnp.int32, done[0][2].shape, 1)
    weighted = jnp.where(lane < 64, done[0][2], done[1][2]).T
    stats = jnp.zeros(lane.shape, F32)
    for at, value in enumerate(done[0][:2] + done[1][:2]):
        stats = jnp.where(lane == at, value, stats)
    stats = stats.T
    sides = []
    for at in range(2):
        sides.append((stats[2 * at : 2 * at + 1], stats[2 * at + 1 : 2 * at + 2], weighted[64 * at : 64 * at + 64]))
    return tuple(jnp.concatenate(pair, axis=1) for pair in zip(*sides))


def chunk_lanes(index):
    return pl.ds(pl.multiple_of((chunk_of_device() ^ index) * 128, 128), 128)


def project_chunk(index, mine, other, w_key, w_value, both):
    lanes = chunk_lanes(index)
    weights = jnp.concatenate([w_key[:, lanes], w_value[:, lanes]], axis=1)
    tokens = mine.shape[0]
    block = 512
    for source, start in ((mine, 0), (other, tokens)):
        for at in range(0, tokens, block):
            both[start + at : start + at + block, :] = dot_nn(source[at : at + block, :], weights).astype(BF16)


def project_kernel(mine, other, w_key, w_value, both):
    project_chunk(1, mine, other, w_key, w_value, both)


def second_project_kernel(mine, other, w_key, w_value, first, after, both, values):
    project_chunk(0, mine, other, w_key, w_value, both)
    tokens = mine.shape[0]
    values[:, chunk_lanes(0)] = both[0:tokens, 128:256]
    values[:, chunk_lanes(1)] = first[0:tokens, 128:256]
    lanes = pl.ds(pl.multiple_of((1 - chunk_of_device() // 2) * 256, 256), 256)
    weights = w_value[:, lanes]
    for at in range(0, tokens, 512):
        values[at : at + 512, lanes] = dot_nn(mine[at : at + 512, :], weights).astype(BF16)


def first_band_kernel(scale, both, tissue, other_tissue, agents, payload):
    put_narrow(payload, chunk_state(1, scale, both, tissue, other_tissue, agents))


def second_band_kernel(scale, both, tissue, other_tissue, agents, keep):
    put_wide(keep, chunk_state(0, scale, both, tissue, other_tissue, agents))


def merge(first, second):
    peak_1, total_1, weighted_1 = first
    peak_2, total_2, weighted_2 = second
    peak = jnp.maximum(peak_1, peak_2)
    factor_1 = jnp.exp(peak_1 - peak)
    factor_2 = jnp.exp(peak_2 - peak)
    return peak, total_1 * factor_1 + total_2 * factor_2, weighted_1 * factor_1 + weighted_2 * factor_2


def wide(ref, index=None):
    array = ref[...] if index is None else ref[index]
    return array[64:65], array[65:66], array[0:64]


def thirds(value):
    high = value.astype(BF16).astype(F32)
    rest = value - high
    middle = rest.astype(BF16).astype(F32)
    return high, middle, rest - middle


def put_wide(ref, state):
    peak, total, weighted = state
    row_id = lax.broadcasted_iota(jnp.int32, (8, weighted.shape[1]), 0)
    ref[0:64] = weighted
    ref[64:72] = jnp.where(row_id == 0, peak, jnp.where(row_id == 1, total, 0.0))


def put_narrow(ref, state):
    peak, total, weighted = state
    row_id = lax.broadcasted_iota(jnp.int32, (8, weighted.shape[1]), 0)
    stats = jnp.zeros((8, weighted.shape[1]), F32)
    for at, part in enumerate(thirds(peak) + thirds(total)):
        stats = jnp.where(row_id == at, part, stats)
    ref[...] = jnp.concatenate([weighted, stats], axis=0).astype(BF16)


def narrow(ref):
    rows = ref[...].astype(F32)
    peak = rows[64:65] + rows[65:66] + rows[66:67]
    total = rows[67:68] + rows[68:69] + rows[69:70]
    return peak, total, rows[0:64]


def next_merge_kernel(held, got, before, own, payload):
    state = merge(wide(held), narrow(got))
    put_narrow(payload, state)
    put_wide(own, state)


def last_merge_kernel(held, got, before, agent_values):
    _, total, weighted = merge(wide(held), narrow(got))
    agent_values[...] = (weighted / total).astype(BF16)


def token_kernel(scale, patches, w_query, agents, after, weights, queries):
    heads = weights.shape[1] // agents.shape[0]
    queries[...] = dot_nn(patches[...], w_query[...]).astype(BF16)

    def scores_of(head):
        lanes = slice(head // 2 * 128, head // 2 * 128 + 128)
        return dot_nt(queries[:, lanes], head_tokens(agents[:, lanes], head % 2, scale))

    ahead = scores_of(0)
    for head in range(heads):
        scores = ahead
        if head + 1 < heads:
            ahead = scores_of(head + 1)
        expo = jnp.exp(scores - jnp.max(scores, axis=1, keepdims=True))
        part = expo * (1.0 / jnp.sum(expo, axis=1, keepdims=True))
        weights[:, head * 256 : head * 256 + 256] = part.astype(BF16)


def pass_kernel(border, same):
    del border, same


def halo_kernel(other, outer, w_value, after, above, below):
    rows = outer.shape[0]
    odd = (lax.axis_index("col") % 2) == 1
    inner_part = other[pl.ds(pl.multiple_of((lax.axis_index("col") % 2) * (other.shape[0] - rows), 128), rows), :]
    inner = dot_nn(inner_part, w_value[...]).astype(BF16)
    outside = dot_nn(outer[...], w_value[...]).astype(BF16)
    above[...] = jnp.where(odd, inner, outside)
    below[...] = jnp.where(odd, outside, inner)


def relay_kernel(own, near, after, both):
    both[0:64] = own[...]
    both[64:128] = near[...]


TAP_COUNTS = (2, 2, 2, 2, 2, 2, 2, 2, 1)


def split_rows(rows):
    return [
        [rows[at] - rows[at + 1] for at in range(0, len(rows) - 1, 2)],
        [rows[at + 1] for at in range(0, len(rows) - 1, 2)],
        [rows[at + 2] - rows[at + 1] for at in range(0, len(rows) - 2, 2)],
    ]


def split_taps(taps):
    even, odd = taps[0::2], taps[1::2]
    both = [even[at] + odd[at] if at < len(odd) else even[at] for at in range(len(even))]
    return [even, both, odd]


def joined_rows(first, second, third):
    return [row for a, b, c in zip(first, second, third) for row in (a + b, b + c)]


def taps_kernel(seven, five, three, after, taps):
    for q in range(7):
        column = [seven[p, q : q + 1, :] for p in range(7)]
        if 1 <= q <= 5:
            column[1:6] = [tap + five[p, q - 1 : q, :] for p, tap in enumerate(column[1:6])]
        if 2 <= q <= 4:
            column[2:5] = [tap + three[p, q - 2 : q - 1, :] for p, tap in enumerate(column[2:5])]
        parts = [tap for part in split_taps(column) for piece in split_taps(part) for tap in piece]
        parts += [jnp.zeros_like(parts[0])] * (taps.shape[1] - len(parts))
        taps[q] = jnp.concatenate(parts, axis=0)


def conv_kernel(first_lane, values, above, below, all_taps, after, position, points, taps):
    width = position.shape[1]
    lanes, step = 128, 16
    tap_count = sum(TAP_COUNTS)
    zero = jnp.zeros((8, lanes), F32)
    for group in range(position.shape[2] // lanes):
        here = slice(first_lane + group * lanes, first_lane + (group + 1) * lanes)
        there = slice(group * lanes, (group + 1) * lanes)
        for q in range(7):
            for at in range(tap_count):
                taps[q, at] = jnp.broadcast_to(all_taps[q, at : at + 1, here], (8, lanes))
        for at in range(points.shape[0]):
            points[at, 0:8, :] = zero
            points[at, 8 + width : 16 + width, :] = zero
        for at in range(0, width, step):
            rows = []
            for ref in (above, values, below):
                for row in range(0, ref.shape[0], width):
                    rows.append(ref[row + at : row + at + step, here].astype(F32))
            even, odd = rows[0::2], rows[1::2]
            streams = (
                [a - b for a, b in zip(even, odd)],
                odd,
                [a - b for a, b in zip(even[1:], odd)],
            )
            parts = [plane for stream in streams for piece in split_rows(stream) for plane in piece]
            for index, plane in enumerate(parts):
                points[index, 8 + at : 8 + at + step, :] = plane
        for at in range(0, width, step):
            columns = (at, at + 8)
            sums = [[[zero, zero] for _ in TAP_COUNTS] for _ in columns]
            for q in range(7):
                first_point = first_tap = 0
                for piece, count in enumerate(TAP_COUNTS):
                    tap = [taps[q, first_tap + k] for k in range(count)]
                    for total, column in zip(sums, columns):
                        start = column + 5 + q
                        point = [points[first_point + k, start : start + 8, :] for k in range(count + 1)]
                        for out in range(2):
                            for k in range(count):
                                total[piece][out] = total[piece][out] + point[out + k] * tap[k]
                    first_point += count + 1
                    first_tap += count
            for total, column in zip(sums, columns):
                thirds_of = [joined_rows(*total[3 * part : 3 * part + 3]) for part in range(3)]
                for row, plane in enumerate(joined_rows(*thirds_of)):
                    position[row, column : column + 8, there] = plane


def blend_block(here, weights, position, spread, w_out, rows):
    parts = [dot_nt(weights[here, at * 512 : at * 512 + 512], spread[at]) for at in range(2)]
    blended = (jnp.concatenate(parts, axis=1) + position[here, :]).astype(BF16)
    return dot_nn(blended, w_out[rows, :])


def fill_spread(pair, spread):
    spread[...] = jnp.zeros_like(spread)
    for index in range(2):
        place = (chunk_of_device() % 2) ^ index
        for half in range(2):
            cols = slice(half * 256, half * 256 + 256)
            spread[place, half * 64 : half * 64 + 64, cols] = pair[index * 64 : index * 64 + 64, cols]


def own_out_kernel(weights_low, weights_high, pair, position_low, position_high, w_out, partial, spread):
    fill_spread(pair, spread)
    block = partial.shape[0] // 2
    for group, (weights, position) in enumerate(((weights_low, position_low), (weights_high, position_high))):

        @pl.when(chunk_of_device() // 2 == group)
        def _(group=group, weights=weights, position=position):
            rows = slice(group * 256, group * 256 + 256)
            for index in range(2):
                here = slice(index * block, index * block + block)
                partial[here, :] = blend_block(here, weights, position, spread, w_out, rows)


def out_kernel(
    weights_low, weights_high, pair, position_low, position_high, w_out, partial, mixed, spread, buffer, sems
):
    fill_spread(pair, spread)
    block = partial.shape[0] // sems.shape[0]
    copies = []
    for index in range(sems.shape[0]):
        here = slice(index * block, index * block + block)
        copies.append((here, pltpu.make_async_copy(buffer.at[here, :], mixed.at[here, :], sems.at[index])))
    for group, (weights, position) in enumerate(((weights_low, position_low), (weights_high, position_high))):

        @pl.when(chunk_of_device() // 2 != group)
        def _(group=group, weights=weights, position=position):
            rows = slice(group * 256, group * 256 + 256)
            for here, copy in copies:
                total = partial[here, :] + blend_block(here, weights, position, spread, w_out, rows)
                buffer[here, :] = total.astype(BF16)
                copy.start()

    for _, copy in copies:
        copy.wait()


def params(megabytes=48):
    return pltpu.CompilerParams(vmem_limit_bytes=megabytes << 20)


def cost(flops, moved, exps=0):
    return pl.CostEstimate(flops=int(flops), bytes_accessed=int(moved), transcendentals=int(exps))


def shape(dims, dtype):
    return jax.ShapeDtypeStruct(dims, dtype)


def exchange(x, bit):
    peers = lax.axis_size("col")
    return lax.ppermute(x, "col", [(i, i ^ bit) for i in range(peers)])


def on_device(patches, tissue, w_query, w_key, w_value, w_out, agent_tokens, seven, five, three):
    band_rows, width, dim = patches.shape
    tokens = band_rows * width
    agents = agent_tokens.shape[0]
    half_dim = dim // 2
    scale = (dim // HEADS) ** (-0.5)
    flat = patches.reshape(tokens, dim)
    peers = lax.axis_size("col")
    place = lax.axis_index("col")
    odd = place % 2
    vmem = pl.BlockSpec(memory_space=VMEM)
    anywhere = pl.BlockSpec(memory_space=pl.ANY)

    other = exchange(flat, 1)
    other_tissue = exchange(tissue, 1)

    border = lax.dynamic_slice_in_dim(flat, odd * (tokens - 3 * width), 3 * width, 0)
    border = pl.pallas_call(
        pass_kernel,
        out_shape=shape((3 * width, dim), BF16),
        in_specs=[anywhere],
        out_specs=anywhere,
        input_output_aliases={0: 0},
        compiler_params=params(16),
        cost_estimate=cost(1e11, 1e6),
        name="pass",
    )(border)
    rest = [(i, i + 1) for i in range(1, peers - 1, 2)]
    outer = lax.ppermute(border, "col", rest + [(j, i) for i, j in rest])

    wide_shape, narrow_shape = shape((72, 512), F32), shape((72, 512), BF16)
    both_bands = shape((2 * tokens, half_dim), BF16)
    first = pl.pallas_call(
        project_kernel,
        out_shape=both_bands,
        in_specs=[vmem] * 4,
        out_specs=vmem,
        compiler_params=params(20),
        cost_estimate=cost(6e8, 4e6),
        name="project",
    )(flat, other, w_key, w_value)

    def band(kernel, out_shape, both):
        return pl.pallas_call(
            functools.partial(kernel, scale),
            out_shape=out_shape,
            in_specs=[vmem] * 4,
            out_specs=vmem,
            compiler_params=params(20),
            cost_estimate=cost(6e8, 4e6, 1e6),
            name="band",
        )(both, tissue, other_tissue, agent_tokens)

    payload = band(first_band_kernel, narrow_shape, first)

    def token(at, after):
        lanes = slice(at * half_dim, (at + 1) * half_dim)
        return pl.pallas_call(
            functools.partial(token_kernel, scale),
            out_shape=shape((tokens, HEADS // 2 * agents), BF16),
            grid=(1,),
            in_specs=[
                vmem,
                pl.BlockSpec((dim, half_dim), lambda i: (0, at)),
                pl.BlockSpec((agents, half_dim), lambda i: (0, at)),
                anywhere,
            ],
            out_specs=vmem,
            scratch_shapes=[VMEM((tokens, half_dim), BF16)],
            compiler_params=params(20),
            cost_estimate=cost(2e9, 6e6, 1e6),
            name="token",
        )(flat, w_query, agent_tokens, after)

    def conv(at, after):
        return pl.pallas_call(
            functools.partial(conv_kernel, at * half_dim),
            out_shape=shape((band_rows, width, half_dim), F32),
            in_specs=[vmem] * 4 + [anywhere],
            out_specs=vmem,
            scratch_shapes=[
                VMEM((sum(TAP_COUNTS) + len(TAP_COUNTS), width + 16, 128), F32),
                VMEM((7, sum(TAP_COUNTS), 8, 128), F32),
            ],
            compiler_params=params(20),
            cost_estimate=cost(3e9, 4e6),
            name="conv",
        )(values, above, below, taps, after).reshape(tokens, half_dim)

    hop = dict(in_specs=[vmem, vmem, anywhere], compiler_params=params(16), cost_estimate=cost(1e6, 1e6))

    def next_merge(held, got, before):
        return pl.pallas_call(
            next_merge_kernel, out_shape=(wide_shape, narrow_shape), out_specs=[vmem] * 2, name="merge_next", **hop
        )(held, got, before)

    got = exchange(payload, 4)
    second, values = pl.pallas_call(
        second_project_kernel,
        out_shape=(both_bands, shape((tokens, dim), BF16)),
        in_specs=[vmem] * 5 + [anywhere],
        out_specs=[vmem] * 2,
        compiler_params=params(20),
        cost_estimate=cost(8e8, 4e6),
        name="project_second",
    )(flat, other, w_key, w_value, first, payload)
    held = band(second_band_kernel, wide_shape, second)
    taps = pl.pallas_call(
        taps_kernel,
        out_shape=shape((7, 24, dim), F32),
        in_specs=[vmem] * 3 + [anywhere],
        out_specs=vmem,
        compiler_params=params(16),
        cost_estimate=cost(5e8, 1e6),
        name="taps",
    )(seven, five, three, payload)
    held, payload = next_merge(held, got, taps)
    got = exchange(payload, 2)
    weights_low = token(0, payload)
    above, below = pl.pallas_call(
        halo_kernel,
        out_shape=(shape((3 * width, dim), BF16), shape((3 * width, dim), BF16)),
        in_specs=[vmem] * 3 + [anywhere],
        out_specs=[vmem] * 2,
        compiler_params=params(16),
        cost_estimate=cost(4e8, 2e6),
        name="halo",
    )(other, outer, w_value, weights_low)
    held, payload = next_merge(held, got, above)
    bit = 8
    while bit * 2 < peers:
        got = exchange(payload, bit)
        held, payload = next_merge(held, got, payload)
        bit *= 2
    got = exchange(payload, bit)
    weights_high = token(1, payload)
    position_low = conv(0, weights_high)
    own = pl.pallas_call(
        last_merge_kernel, out_shape=shape((64, 512), BF16), out_specs=vmem, name="merge_last", **hop
    )(held, got, position_low)
    near = exchange(own, 4)
    position_high = conv(1, own)
    pair = pl.pallas_call(
        relay_kernel,
        out_shape=shape((128, 512), BF16),
        in_specs=[vmem, vmem, anywhere],
        out_specs=vmem,
        compiler_params=params(16),
        cost_estimate=cost(1e6, 1e6),
        name="relay",
    )(own, near, position_high)
    other_pair = exchange(pair, 1)

    partial = pl.pallas_call(
        own_out_kernel,
        out_shape=shape((tokens, dim), F32),
        in_specs=[vmem] * 6,
        out_specs=vmem,
        scratch_shapes=[VMEM((2, 128, 512), BF16)],
        compiler_params=params(20),
        cost_estimate=cost(1.1e9, 4e6),
        name="own_out",
    )(weights_low, weights_high, pair, position_low, position_high, w_out)
    mixed = pl.pallas_call(
        out_kernel,
        out_shape=shape((tokens, dim), BF16),
        in_specs=[vmem] * 7,
        out_specs=anywhere,
        scratch_shapes=[
            VMEM((2, 128, 512), BF16),
            VMEM((tokens, dim), BF16),
            pltpu.SemaphoreType.DMA((2,)),
        ],
        compiler_params=params(20),
        cost_estimate=cost(1.1e9, 8e6),
        name="out",
    )(weights_low, weights_high, other_pair, position_low, position_high, w_out, partial)
    return mixed.reshape(band_rows, width, dim)


def solution(mesh):
    return jax.shard_map(
        on_device,
        mesh=mesh,
        in_specs=(
            P(("slide", "col"), None, None),
            P(("slide", "col"), None),
            P(),
            P(),
            P(),
            P(),
            P(),
            P(),
            P(),
            P(),
        ),
        out_specs=P(("slide", "col"), None, None),
        check_vma=False,
    )
```

```python
import functools

import jax
import jax.numpy as jnp
from jax import lax
from jax.experimental import pallas as pl
from jax.experimental.pallas import tpu as pltpu
from jax.sharding import PartitionSpec as P

HEADS = 8
NO_SCORE = -1e30
F32 = jnp.float32
BF16 = jnp.bfloat16
VMEM = pltpu.VMEM


def dot_nt(a, b):
    return lax.dot_general(a, b, (((1,), (1,)), ((), ())), preferred_element_type=F32)


def dot_nn(a, b):
    return lax.dot_general(a, b, (((1,), (0,)), ((), ())), preferred_element_type=F32)


def head_tokens(pair, half, scale):
    lane = lax.broadcasted_iota(jnp.int32, pair.shape, 1)
    mine = (lane >= 64) if half else (lane < 64)
    return jnp.where(mine, pair.astype(F32) * scale, 0.0).astype(BF16)


def chunk_of_device():
    place = lax.axis_index("col")
    return (place & 1) * 2 + ((place >> 2) & 1)


def chunk_state(index, scale, both, tissue, other_tissue, agents):
    lines = []
    for grid in (tissue, other_tissue):
        bias = jnp.where(grid[...] > 0, 0.0, NO_SCORE).astype(F32)
        lines += [bias[row : row + 1] for row in range(bias.shape[0])]
    bias_line = jnp.concatenate(lines, axis=1)
    pair_agents = agents[:, chunk_lanes(index)]
    keys, vals = both[:, 0:128], both[:, 128:256]
    all_scores = [dot_nt(head_tokens(pair_agents, half, scale), keys) + bias_line for half in range(2)]
    done = []
    for scores in all_scores:
        peak = jnp.max(scores, axis=1, keepdims=True)
        expo = jnp.exp(scores - peak)
        total = jnp.sum(expo, axis=1, keepdims=True)
        done.append((peak, total, dot_nn(expo.astype(BF16), vals)))
    lane = lax.broadcasted_iota(jnp.int32, done[0][2].shape, 1)
    weighted = jnp.where(lane < 64, done[0][2], done[1][2]).T
    stats = jnp.zeros(lane.shape, F32)
    for at, value in enumerate(done[0][:2] + done[1][:2]):
        stats = jnp.where(lane == at, value, stats)
    stats = stats.T
    sides = []
    for at in range(2):
        sides.append((stats[2 * at : 2 * at + 1], stats[2 * at + 1 : 2 * at + 2], weighted[64 * at : 64 * at + 64]))
    return tuple(jnp.concatenate(pair, axis=1) for pair in zip(*sides))


def chunk_lanes(index):
    return pl.ds(pl.multiple_of((chunk_of_device() ^ index) * 128, 128), 128)


def project_chunk(index, mine, other, w_key, w_value, both):
    lanes = chunk_lanes(index)
    weights = jnp.concatenate([w_key[:, lanes], w_value[:, lanes]], axis=1)
    tokens = mine.shape[0]
    block = 512
    for source, start in ((mine, 0), (other, tokens)):
        for at in range(0, tokens, block):
            both[start + at : start + at + block, :] = dot_nn(source[at : at + block, :], weights).astype(BF16)


def project_kernel(mine, other, w_key, w_value, both):
    project_chunk(1, mine, other, w_key, w_value, both)


def second_project_kernel(mine, other, w_key, w_value, first, after, both, values):
    project_chunk(0, mine, other, w_key, w_value, both)
    tokens = mine.shape[0]
    values[:, chunk_lanes(0)] = both[0:tokens, 128:256]
    values[:, chunk_lanes(1)] = first[0:tokens, 128:256]
    lanes = pl.ds(pl.multiple_of((1 - chunk_of_device() // 2) * 256, 256), 256)
    weights = w_value[:, lanes]
    for at in range(0, tokens, 512):
        values[at : at + 512, lanes] = dot_nn(mine[at : at + 512, :], weights).astype(BF16)


def first_band_kernel(scale, both, tissue, other_tissue, agents, payload):
    put_narrow(payload, chunk_state(1, scale, both, tissue, other_tissue, agents))


def second_band_kernel(scale, both, tissue, other_tissue, agents, keep):
    put_wide(keep, chunk_state(0, scale, both, tissue, other_tissue, agents))


def merge(first, second):
    peak_1, total_1, weighted_1 = first
    peak_2, total_2, weighted_2 = second
    peak = jnp.maximum(peak_1, peak_2)
    factor_1 = jnp.exp(peak_1 - peak)
    factor_2 = jnp.exp(peak_2 - peak)
    return peak, total_1 * factor_1 + total_2 * factor_2, weighted_1 * factor_1 + weighted_2 * factor_2


def wide(ref, index=None):
    array = ref[...] if index is None else ref[index]
    return array[64:65], array[65:66], array[0:64]


def thirds(value):
    high = value.astype(BF16).astype(F32)
    rest = value - high
    middle = rest.astype(BF16).astype(F32)
    return high, middle, rest - middle


def put_wide(ref, state):
    peak, total, weighted = state
    row_id = lax.broadcasted_iota(jnp.int32, (8, weighted.shape[1]), 0)
    ref[0:64] = weighted
    ref[64:72] = jnp.where(row_id == 0, peak, jnp.where(row_id == 1, total, 0.0))


def put_narrow(ref, state):
    peak, total, weighted = state
    row_id = lax.broadcasted_iota(jnp.int32, (8, weighted.shape[1]), 0)
    stats = jnp.zeros((8, weighted.shape[1]), F32)
    for at, part in enumerate(thirds(peak) + thirds(total)):
        stats = jnp.where(row_id == at, part, stats)
    ref[...] = jnp.concatenate([weighted, stats], axis=0).astype(BF16)


def narrow(ref):
    rows = ref[...].astype(F32)
    peak = rows[64:65] + rows[65:66] + rows[66:67]
    total = rows[67:68] + rows[68:69] + rows[69:70]
    return peak, total, rows[0:64]


def next_merge_kernel(held, got, before, own, payload):
    state = merge(wide(held), narrow(got))
    put_narrow(payload, state)
    put_wide(own, state)


def last_merge_kernel(held, got, before, agent_values):
    _, total, weighted = merge(wide(held), narrow(got))
    agent_values[...] = (weighted / total).astype(BF16)


def token_kernel(scale, patches, w_query, agents, after, weights, queries):
    heads = weights.shape[1] // agents.shape[0]
    queries[...] = dot_nn(patches[...], w_query[...]).astype(BF16)

    def scores_of(head):
        lanes = slice(head // 2 * 128, head // 2 * 128 + 128)
        return dot_nt(queries[:, lanes], head_tokens(agents[:, lanes], head % 2, scale))

    ahead = scores_of(0)
    for head in range(heads):
        scores = ahead
        if head + 1 < heads:
            ahead = scores_of(head + 1)
        expo = jnp.exp(scores - jnp.max(scores, axis=1, keepdims=True))
        part = expo * (1.0 / jnp.sum(expo, axis=1, keepdims=True))
        weights[:, head * 256 : head * 256 + 256] = part.astype(BF16)


def pass_kernel(border, same):
    del border, same


def halo_kernel(other, outer, w_value, after, above, below):
    rows = outer.shape[0]
    odd = (lax.axis_index("col") % 2) == 1
    inner_part = other[pl.ds(pl.multiple_of((lax.axis_index("col") % 2) * (other.shape[0] - rows), 128), rows), :]
    inner = dot_nn(inner_part, w_value[...]).astype(BF16)
    outside = dot_nn(outer[...], w_value[...]).astype(BF16)
    above[...] = jnp.where(odd, inner, outside)
    below[...] = jnp.where(odd, outside, inner)


def relay_kernel(own, near, after, both):
    both[0:64] = own[...]
    both[64:128] = near[...]


TAP_COUNTS = (2, 2, 2, 2, 2, 2, 2, 2, 1)


def split_rows(rows):
    return [
        [rows[at] - rows[at + 1] for at in range(0, len(rows) - 1, 2)],
        [rows[at + 1] for at in range(0, len(rows) - 1, 2)],
        [rows[at + 2] - rows[at + 1] for at in range(0, len(rows) - 2, 2)],
    ]


def split_taps(taps):
    even, odd = taps[0::2], taps[1::2]
    both = [even[at] + odd[at] if at < len(odd) else even[at] for at in range(len(even))]
    return [even, both, odd]


def joined_rows(first, second, third):
    return [row for a, b, c in zip(first, second, third) for row in (a + b, b + c)]


def taps_kernel(seven, five, three, after, taps):
    for q in range(7):
        column = [seven[p, q : q + 1, :] for p in range(7)]
        if 1 <= q <= 5:
            column[1:6] = [tap + five[p, q - 1 : q, :] for p, tap in enumerate(column[1:6])]
        if 2 <= q <= 4:
            column[2:5] = [tap + three[p, q - 2 : q - 1, :] for p, tap in enumerate(column[2:5])]
        parts = [tap for part in split_taps(column) for piece in split_taps(part) for tap in piece]
        parts += [jnp.zeros_like(parts[0])] * (taps.shape[1] - len(parts))
        taps[q] = jnp.concatenate(parts, axis=0)


def conv_kernel(first_lane, values, above, below, all_taps, after, *rest):
    positions, points, taps = rest[:-2], rest[-2], rest[-1]
    width = positions[0].shape[1]
    lanes, step = 128, 16
    tap_count = sum(TAP_COUNTS)
    zero = jnp.zeros((8, lanes), F32)
    for group, position in enumerate(positions):
        here = slice(first_lane + group * lanes, first_lane + (group + 1) * lanes)
        for q in range(7):
            for at in range(tap_count):
                taps[q, at] = jnp.broadcast_to(all_taps[q, at : at + 1, here], (8, lanes))
        for at in range(points.shape[0]):
            points[at, 0:8, :] = zero
            points[at, 8 + width : 16 + width, :] = zero
        for at in range(0, width, step):
            rows = []
            for ref in (above, values, below):
                for row in range(0, ref.shape[0], width):
                    rows.append(ref[row + at : row + at + step, here].astype(F32))
            even, odd = rows[0::2], rows[1::2]
            streams = (
                [a - b for a, b in zip(even, odd)],
                odd,
                [a - b for a, b in zip(even[1:], odd)],
            )
            parts = [plane for stream in streams for piece in split_rows(stream) for plane in piece]
            for index, plane in enumerate(parts):
                points[index, 8 + at : 8 + at + step, :] = plane
        for at in range(0, width, step):
            columns = (at, at + 8)
            sums = [[[zero, zero] for _ in TAP_COUNTS] for _ in columns]
            for q in range(7):
                first_point = first_tap = 0
                for piece, count in enumerate(TAP_COUNTS):
                    tap = [taps[q, first_tap + k] for k in range(count)]
                    for total, column in zip(sums, columns):
                        start = column + 5 + q
                        point = [points[first_point + k, start : start + 8, :] for k in range(count + 1)]
                        for out in range(2):
                            for k in range(count):
                                total[piece][out] = total[piece][out] + point[out + k] * tap[k]
                    first_point += count + 1
                    first_tap += count
            for total, column in zip(sums, columns):
                thirds_of = [joined_rows(*total[3 * part : 3 * part + 3]) for part in range(3)]
                for row, plane in enumerate(joined_rows(*thirds_of)):
                    position[row, column : column + 8, :] = plane


def blend_block(here, weights, positions, spread, w_out, rows):
    parts = [
        dot_nt(weights[here, at * 512 : at * 512 + 512], spread[at]) + positions[at][here, :] for at in range(2)
    ]
    return dot_nn(jnp.concatenate(parts, axis=1).astype(BF16), w_out[rows, :])


def fill_spread(pair, spread):
    spread[...] = jnp.zeros_like(spread)
    for index in range(2):
        place = (chunk_of_device() % 2) ^ index
        for half in range(2):
            cols = slice(half * 256, half * 256 + 256)
            spread[place, half * 64 : half * 64 + 64, cols] = pair[index * 64 : index * 64 + 64, cols]


def own_out_kernel(weights_low, weights_high, pair, p_0, p_1, p_2, p_3, w_out, partial, spread):
    fill_spread(pair, spread)
    block = partial.shape[0] // 2
    for group, (weights, position) in enumerate(((weights_low, (p_0, p_1)), (weights_high, (p_2, p_3)))):

        @pl.when(chunk_of_device() // 2 == group)
        def _(group=group, weights=weights, position=position):
            rows = slice(group * 256, group * 256 + 256)
            for index in range(2):
                here = slice(index * block, index * block + block)
                partial[here, :] = blend_block(here, weights, position, spread, w_out, rows)


def out_kernel(weights_low, weights_high, pair, p_0, p_1, p_2, p_3, w_out, partial, mixed, spread, buffer, sems):
    fill_spread(pair, spread)
    block = partial.shape[0] // sems.shape[0]
    copies = []
    for index in range(sems.shape[0]):
        here = slice(index * block, index * block + block)
        copies.append((here, pltpu.make_async_copy(buffer.at[here, :], mixed.at[here, :], sems.at[index])))
    for group, (weights, position) in enumerate(((weights_low, (p_0, p_1)), (weights_high, (p_2, p_3)))):

        @pl.when(chunk_of_device() // 2 != group)
        def _(group=group, weights=weights, position=position):
            rows = slice(group * 256, group * 256 + 256)
            for here, copy in copies:
                total = partial[here, :] + blend_block(here, weights, position, spread, w_out, rows)
                buffer[here, :] = total.astype(BF16)
                copy.start()

    for _, copy in copies:
        copy.wait()


def params(megabytes=48):
    return pltpu.CompilerParams(vmem_limit_bytes=megabytes << 20)


def cost(flops, moved, exps=0):
    return pl.CostEstimate(flops=int(flops), bytes_accessed=int(moved), transcendentals=int(exps))


def shape(dims, dtype):
    return jax.ShapeDtypeStruct(dims, dtype)


def exchange(x, bit):
    peers = lax.axis_size("col")
    return lax.ppermute(x, "col", [(i, i ^ bit) for i in range(peers)])


def on_device(patches, tissue, w_query, w_key, w_value, w_out, agent_tokens, seven, five, three):
    band_rows, width, dim = patches.shape
    tokens = band_rows * width
    agents = agent_tokens.shape[0]
    half_dim = dim // 2
    scale = (dim // HEADS) ** (-0.5)
    flat = patches.reshape(tokens, dim)
    peers = lax.axis_size("col")
    place = lax.axis_index("col")
    odd = place % 2
    vmem = pl.BlockSpec(memory_space=VMEM)
    anywhere = pl.BlockSpec(memory_space=pl.ANY)

    other = exchange(flat, 1)
    other_tissue = exchange(tissue, 1)

    border = lax.dynamic_slice_in_dim(flat, odd * (tokens - 3 * width), 3 * width, 0)
    border = pl.pallas_call(
        pass_kernel,
        out_shape=shape((3 * width, dim), BF16),
        in_specs=[anywhere],
        out_specs=anywhere,
        input_output_aliases={0: 0},
        compiler_params=params(16),
        cost_estimate=cost(1e11, 1e6),
        name="pass",
    )(border)
    rest = [(i, i + 1) for i in range(1, peers - 1, 2)]
    outer = lax.ppermute(border, "col", rest + [(j, i) for i, j in rest])

    wide_shape, narrow_shape = shape((72, 512), F32), shape((72, 512), BF16)
    both_bands = shape((2 * tokens, half_dim), BF16)
    first = pl.pallas_call(
        project_kernel,
        out_shape=both_bands,
        in_specs=[vmem] * 4,
        out_specs=vmem,
        compiler_params=params(20),
        cost_estimate=cost(6e8, 4e6),
        name="project",
    )(flat, other, w_key, w_value)

    def band(kernel, out_shape, both):
        return pl.pallas_call(
            functools.partial(kernel, scale),
            out_shape=out_shape,
            in_specs=[vmem] * 4,
            out_specs=vmem,
            compiler_params=params(20),
            cost_estimate=cost(6e8, 4e6, 1e6),
            name="band",
        )(both, tissue, other_tissue, agent_tokens)

    payload = band(first_band_kernel, narrow_shape, first)

    def token(at, after):
        lanes = slice(at * half_dim, (at + 1) * half_dim)
        return pl.pallas_call(
            functools.partial(token_kernel, scale),
            out_shape=shape((tokens, HEADS // 2 * agents), BF16),
            grid=(1,),
            in_specs=[
                vmem,
                pl.BlockSpec((dim, half_dim), lambda i: (0, at)),
                pl.BlockSpec((agents, half_dim), lambda i: (0, at)),
                anywhere,
            ],
            out_specs=vmem,
            scratch_shapes=[VMEM((tokens, half_dim), BF16)],
            compiler_params=params(20),
            cost_estimate=cost(2e9, 6e6, 1e6),
            name="token",
        )(flat, w_query, agent_tokens, after)

    def conv(chunks, after):
        parts = pl.pallas_call(
            functools.partial(conv_kernel, chunks[0] * 128),
            out_shape=[shape((band_rows, width, 128), F32)] * len(chunks),
            in_specs=[vmem] * 4 + [anywhere],
            out_specs=[vmem] * len(chunks),
            scratch_shapes=[
                VMEM((sum(TAP_COUNTS) + len(TAP_COUNTS), width + 16, 128), F32),
                VMEM((7, sum(TAP_COUNTS), 8, 128), F32),
            ],
            compiler_params=params(20),
            cost_estimate=cost(3e9, 4e6),
            name="conv",
        )(values, above, below, taps, after)
        return [part.reshape(tokens, 128) for part in parts]

    hop = dict(in_specs=[vmem, vmem, anywhere], compiler_params=params(16), cost_estimate=cost(1e6, 1e6))

    def next_merge(held, got, before):
        return pl.pallas_call(
            next_merge_kernel, out_shape=(wide_shape, narrow_shape), out_specs=[vmem] * 2, name="merge_next", **hop
        )(held, got, before)

    got = exchange(payload, 4)
    second, values = pl.pallas_call(
        second_project_kernel,
        out_shape=(both_bands, shape((tokens, dim), BF16)),
        in_specs=[vmem] * 5 + [anywhere],
        out_specs=[vmem] * 2,
        compiler_params=params(20),
        cost_estimate=cost(8e8, 4e6),
        name="project_second",
    )(flat, other, w_key, w_value, first, payload)
    held = band(second_band_kernel, wide_shape, second)
    taps = pl.pallas_call(
        taps_kernel,
        out_shape=shape((7, 24, dim), F32),
        in_specs=[vmem] * 3 + [anywhere],
        out_specs=vmem,
        compiler_params=params(16),
        cost_estimate=cost(5e8, 1e6),
        name="taps",
    )(seven, five, three, payload)
    held, payload = next_merge(held, got, taps)
    got = exchange(payload, 2)
    weights_low = token(0, payload)
    above, below = pl.pallas_call(
        halo_kernel,
        out_shape=(shape((3 * width, dim), BF16), shape((3 * width, dim), BF16)),
        in_specs=[vmem] * 3 + [anywhere],
        out_specs=[vmem] * 2,
        compiler_params=params(16),
        cost_estimate=cost(4e8, 2e6),
        name="halo",
    )(other, outer, w_value, weights_low)
    held, payload = next_merge(held, got, above)
    bit = 8
    while bit * 2 < peers:
        got = exchange(payload, bit)
        held, payload = next_merge(held, got, payload)
        bit *= 2
    got = exchange(payload, bit)
    weights_high = token(1, payload)
    positions = conv([0], weights_high)
    own = pl.pallas_call(
        last_merge_kernel, out_shape=shape((64, 512), BF16), out_specs=vmem, name="merge_last", **hop
    )(held, got, positions[0])
    near = exchange(own, 4)
    positions += conv([1, 2, 3], own)
    pair = pl.pallas_call(
        relay_kernel,
        out_shape=shape((128, 512), BF16),
        in_specs=[vmem, vmem, anywhere],
        out_specs=vmem,
        compiler_params=params(16),
        cost_estimate=cost(1e6, 1e6),
        name="relay",
    )(own, near, positions[3])
    other_pair = exchange(pair, 1)

    partial = pl.pallas_call(
        own_out_kernel,
        out_shape=shape((tokens, dim), F32),
        in_specs=[vmem] * 8,
        out_specs=vmem,
        scratch_shapes=[VMEM((2, 128, 512), BF16)],
        compiler_params=params(20),
        cost_estimate=cost(1.1e9, 4e6),
        name="own_out",
    )(weights_low, weights_high, pair, *positions, w_out)
    mixed = pl.pallas_call(
        out_kernel,
        out_shape=shape((tokens, dim), BF16),
        in_specs=[vmem] * 9,
        out_specs=anywhere,
        scratch_shapes=[
            VMEM((2, 128, 512), BF16),
            VMEM((tokens, dim), BF16),
            pltpu.SemaphoreType.DMA((2,)),
        ],
        compiler_params=params(20),
        cost_estimate=cost(1.1e9, 8e6),
        name="out",
    )(weights_low, weights_high, other_pair, *positions, w_out, partial)
    return mixed.reshape(band_rows, width, dim)


def solution(mesh):
    return jax.shard_map(
        on_device,
        mesh=mesh,
        in_specs=(
            P(("slide", "col"), None, None),
            P(("slide", "col"), None),
            P(),
            P(),
            P(),
            P(),
            P(),
            P(),
            P(),
            P(),
        ),
        out_specs=P(("slide", "col"), None, None),
        check_vma=False,
    )
```

```python
import functools

import jax
import jax.numpy as jnp
from jax import lax
from jax.experimental import pallas as pl
from jax.experimental.pallas import tpu as pltpu
from jax.sharding import PartitionSpec as P

HEADS = 8
NO_SCORE = -1e30
F32 = jnp.float32
BF16 = jnp.bfloat16
VMEM = pltpu.VMEM


def dot_nt(a, b):
    return lax.dot_general(a, b, (((1,), (1,)), ((), ())), preferred_element_type=F32)


def dot_nn(a, b):
    return lax.dot_general(a, b, (((1,), (0,)), ((), ())), preferred_element_type=F32)


def head_tokens(pair, half, scale):
    lane = lax.broadcasted_iota(jnp.int32, pair.shape, 1)
    mine = (lane >= 64) if half else (lane < 64)
    return jnp.where(mine, pair.astype(F32) * scale, 0.0).astype(BF16)


def chunk_of_device():
    place = lax.axis_index("col")
    return (place & 1) * 2 + ((place >> 2) & 1)


def chunk_state(index, scale, both, tissue, other_tissue, agents):
    lines = []
    for grid in (tissue, other_tissue):
        bias = jnp.where(grid[...] > 0, 0.0, NO_SCORE).astype(F32)
        lines += [bias[row : row + 1] for row in range(bias.shape[0])]
    bias_line = jnp.concatenate(lines, axis=1)
    pair_agents = agents[:, chunk_lanes(index)]
    keys, vals = both[:, 0:128], both[:, 128:256]
    all_scores = [dot_nt(head_tokens(pair_agents, half, scale), keys) + bias_line for half in range(2)]
    done = []
    for scores in all_scores:
        peak = jnp.max(scores, axis=1, keepdims=True)
        expo = jnp.exp(scores - peak)
        total = jnp.sum(expo, axis=1, keepdims=True)
        done.append((peak, total, dot_nn(expo.astype(BF16), vals)))
    lane = lax.broadcasted_iota(jnp.int32, done[0][2].shape, 1)
    weighted = jnp.where(lane < 64, done[0][2], done[1][2]).T
    stats = jnp.zeros(lane.shape, F32)
    for at, value in enumerate(done[0][:2] + done[1][:2]):
        stats = jnp.where(lane == at, value, stats)
    stats = stats.T
    sides = []
    for at in range(2):
        sides.append((stats[2 * at : 2 * at + 1], stats[2 * at + 1 : 2 * at + 2], weighted[64 * at : 64 * at + 64]))
    return tuple(jnp.concatenate(pair, axis=1) for pair in zip(*sides))


def chunk_lanes(index):
    return pl.ds(pl.multiple_of((chunk_of_device() ^ index) * 128, 128), 128)


def project_chunk(index, mine, other, w_key, w_value, both):
    lanes = chunk_lanes(index)
    weights = jnp.concatenate([w_key[:, lanes], w_value[:, lanes]], axis=1)
    tokens = mine.shape[0]
    block = 512
    for source, start in ((mine, 0), (other, tokens)):
        for at in range(0, tokens, block):
            both[start + at : start + at + block, :] = dot_nn(source[at : at + block, :], weights).astype(BF16)


def project_kernel(mine, other, w_key, w_value, both):
    project_chunk(1, mine, other, w_key, w_value, both)


def second_project_kernel(mine, other, w_key, w_value, first, after, both, values):
    project_chunk(0, mine, other, w_key, w_value, both)
    tokens = mine.shape[0]
    values[:, chunk_lanes(0)] = both[0:tokens, 128:256]
    values[:, chunk_lanes(1)] = first[0:tokens, 128:256]
    lanes = pl.ds(pl.multiple_of((1 - chunk_of_device() // 2) * 256, 256), 256)
    weights = w_value[:, lanes]
    for at in range(0, tokens, 512):
        values[at : at + 512, lanes] = dot_nn(mine[at : at + 512, :], weights).astype(BF16)


def first_band_kernel(scale, both, tissue, other_tissue, agents, payload):
    put_narrow(payload, chunk_state(1, scale, both, tissue, other_tissue, agents))


def second_band_kernel(scale, both, tissue, other_tissue, agents, keep):
    put_wide(keep, chunk_state(0, scale, both, tissue, other_tissue, agents))


def merge(first, second):
    peak_1, total_1, weighted_1 = first
    peak_2, total_2, weighted_2 = second
    peak = jnp.maximum(peak_1, peak_2)
    factor_1 = jnp.exp(peak_1 - peak)
    factor_2 = jnp.exp(peak_2 - peak)
    return peak, total_1 * factor_1 + total_2 * factor_2, weighted_1 * factor_1 + weighted_2 * factor_2


def wide(ref, index=None):
    array = ref[...] if index is None else ref[index]
    return array[64:65], array[65:66], array[0:64]


def thirds(value):
    high = value.astype(BF16).astype(F32)
    rest = value - high
    middle = rest.astype(BF16).astype(F32)
    return high, middle, rest - middle


def put_wide(ref, state):
    peak, total, weighted = state
    row_id = lax.broadcasted_iota(jnp.int32, (8, weighted.shape[1]), 0)
    ref[0:64] = weighted
    ref[64:72] = jnp.where(row_id == 0, peak, jnp.where(row_id == 1, total, 0.0))


def put_narrow(ref, state):
    peak, total, weighted = state
    row_id = lax.broadcasted_iota(jnp.int32, (8, weighted.shape[1]), 0)
    stats = jnp.zeros((8, weighted.shape[1]), F32)
    for at, part in enumerate(thirds(peak) + thirds(total)):
        stats = jnp.where(row_id == at, part, stats)
    ref[...] = jnp.concatenate([weighted, stats], axis=0).astype(BF16)


def narrow(ref):
    rows = ref[...].astype(F32)
    peak = rows[64:65] + rows[65:66] + rows[66:67]
    total = rows[67:68] + rows[68:69] + rows[69:70]
    return peak, total, rows[0:64]


def next_merge_kernel(held, got, before, own, payload):
    state = merge(wide(held), narrow(got))
    put_narrow(payload, state)
    put_wide(own, state)


def last_merge_kernel(held, got, before, agent_values):
    _, total, weighted = merge(wide(held), narrow(got))
    agent_values[...] = (weighted / total).astype(BF16)


def token_kernel(scale, patches, w_query, agents, after, weights, queries):
    heads = weights.shape[1] // agents.shape[0]
    queries[...] = dot_nn(patches[...], w_query[...]).astype(BF16)

    def scores_of(head):
        lanes = slice(head // 2 * 128, head // 2 * 128 + 128)
        return dot_nt(queries[:, lanes], head_tokens(agents[:, lanes], head % 2, scale))

    ahead = scores_of(0)
    for head in range(heads):
        scores = ahead
        if head + 1 < heads:
            ahead = scores_of(head + 1)
        expo = jnp.exp(scores - jnp.max(scores, axis=1, keepdims=True))
        part = expo * (1.0 / jnp.sum(expo, axis=1, keepdims=True))
        weights[:, head * 256 : head * 256 + 256] = part.astype(BF16)


def pass_kernel(border, same):
    del border, same


def halo_kernel(other, outer, w_value, after, above, below):
    rows = outer.shape[0]
    odd = (lax.axis_index("col") % 2) == 1
    inner_part = other[pl.ds(pl.multiple_of((lax.axis_index("col") % 2) * (other.shape[0] - rows), 128), rows), :]
    inner = dot_nn(inner_part, w_value[...]).astype(BF16)
    outside = dot_nn(outer[...], w_value[...]).astype(BF16)
    above[...] = jnp.where(odd, inner, outside)
    below[...] = jnp.where(odd, outside, inner)


def relay_kernel(own, near, after, both):
    both[0:64] = own[...]
    both[64:128] = near[...]


TAP_COUNTS = (2, 2, 2, 2, 2, 2, 2, 2, 1)


def split_rows(rows):
    return [
        [rows[at] - rows[at + 1] for at in range(0, len(rows) - 1, 2)],
        [rows[at + 1] for at in range(0, len(rows) - 1, 2)],
        [rows[at + 2] - rows[at + 1] for at in range(0, len(rows) - 2, 2)],
    ]


def split_taps(taps):
    even, odd = taps[0::2], taps[1::2]
    both = [even[at] + odd[at] if at < len(odd) else even[at] for at in range(len(even))]
    return [even, both, odd]


def joined_rows(first, second, third):
    return [row for a, b, c in zip(first, second, third) for row in (a + b, b + c)]


def taps_kernel(seven, five, three, after, taps):
    for q in range(7):
        column = [seven[p, q : q + 1, :] for p in range(7)]
        if 1 <= q <= 5:
            column[1:6] = [tap + five[p, q - 1 : q, :] for p, tap in enumerate(column[1:6])]
        if 2 <= q <= 4:
            column[2:5] = [tap + three[p, q - 2 : q - 1, :] for p, tap in enumerate(column[2:5])]
        parts = [tap for part in split_taps(column) for piece in split_taps(part) for tap in piece]
        parts += [jnp.zeros_like(parts[0])] * (taps.shape[1] - len(parts))
        taps[q] = jnp.concatenate(parts, axis=0)


def conv_kernel(first_lane, values, above, below, all_taps, after, *rest):
    positions, points, taps = rest[:-2], rest[-2], rest[-1]
    width = positions[0].shape[1]
    lanes, step = 128, 16
    tap_count = sum(TAP_COUNTS)
    zero = jnp.zeros((8, lanes), F32)
    for group, position in enumerate(positions):
        here = slice(first_lane + group * lanes, first_lane + (group + 1) * lanes)
        for q in range(7):
            for at in range(tap_count):
                taps[q, at] = jnp.broadcast_to(all_taps[q, at : at + 1, here], (8, lanes))
        for at in range(points.shape[0]):
            points[at, 0:8, :] = zero
            points[at, 8 + width : 16 + width, :] = zero
        for at in range(0, width, step):
            rows = []
            for ref in (above, values, below):
                for row in range(0, ref.shape[0], width):
                    rows.append(ref[row + at : row + at + step, here].astype(F32))
            even, odd = rows[0::2], rows[1::2]
            streams = (
                [a - b for a, b in zip(even, odd)],
                odd,
                [a - b for a, b in zip(even[1:], odd)],
            )
            parts = [plane for stream in streams for piece in split_rows(stream) for plane in piece]
            for index, plane in enumerate(parts):
                points[index, 8 + at : 8 + at + step, :] = plane
        for at in range(0, width, step):
            columns = (at, at + 8)
            sums = [[[zero, zero] for _ in TAP_COUNTS] for _ in columns]
            for q in range(7):
                first_point = first_tap = 0
                for piece, count in enumerate(TAP_COUNTS):
                    tap = [taps[q, first_tap + k] for k in range(count)]
                    for total, column in zip(sums, columns):
                        start = column + 5 + q
                        point = [points[first_point + k, start : start + 8, :] for k in range(count + 1)]
                        for out in range(2):
                            for k in range(count):
                                total[piece][out] = total[piece][out] + point[out + k] * tap[k]
                    first_point += count + 1
                    first_tap += count
            for total, column in zip(sums, columns):
                thirds_of = [joined_rows(*total[3 * part : 3 * part + 3]) for part in range(3)]
                for row, plane in enumerate(joined_rows(*thirds_of)):
                    position[row, column : column + 8, :] = plane


def blend_block(here, weights, positions, spread, w_out, rows):
    parts = [
        dot_nt(weights[here, at * 512 : at * 512 + 512], spread[at]) + positions[at][here, :] for at in range(2)
    ]
    return dot_nn(jnp.concatenate(parts, axis=1).astype(BF16), w_out[rows, :])


def fill_spread(pair, spread):
    spread[...] = jnp.zeros_like(spread)
    for index in range(2):
        place = (chunk_of_device() % 2) ^ index
        for half in range(2):
            cols = slice(half * 256, half * 256 + 256)
            spread[place, half * 64 : half * 64 + 64, cols] = pair[index * 64 : index * 64 + 64, cols]


def own_out_kernel(weights_low, weights_high, pair, p_0, p_1, p_2, p_3, w_out, partial, spread):
    fill_spread(pair, spread)
    block = partial.shape[0] // 2
    for group, (weights, position) in enumerate(((weights_low, (p_0, p_1)), (weights_high, (p_2, p_3)))):

        @pl.when(chunk_of_device() // 2 == group)
        def _(group=group, weights=weights, position=position):
            rows = slice(group * 256, group * 256 + 256)
            for index in range(2):
                here = slice(index * block, index * block + block)
                partial[here, :] = blend_block(here, weights, position, spread, w_out, rows)


def out_kernel(weights_low, weights_high, pair, p_0, p_1, p_2, p_3, w_out, partial, mixed, spread, buffer, sems):
    fill_spread(pair, spread)
    quarter = partial.shape[0] // 4
    copies = []
    for index, (start, stop) in enumerate(((0, 2), (2, 3), (3, 4))):
        here = slice(start * quarter, stop * quarter)
        copies.append((here, pltpu.make_async_copy(buffer.at[here, :], mixed.at[here, :], sems.at[index])))
    for group, (weights, position) in enumerate(((weights_low, (p_0, p_1)), (weights_high, (p_2, p_3)))):

        @pl.when(chunk_of_device() // 2 != group)
        def _(group=group, weights=weights, position=position):
            rows = slice(group * 256, group * 256 + 256)
            for here, copy in copies:
                total = partial[here, :] + blend_block(here, weights, position, spread, w_out, rows)
                buffer[here, :] = total.astype(BF16)
                copy.start()

    for _, copy in copies:
        copy.wait()


def params(megabytes=48):
    return pltpu.CompilerParams(vmem_limit_bytes=megabytes << 20)


def cost(flops, moved, exps=0):
    return pl.CostEstimate(flops=int(flops), bytes_accessed=int(moved), transcendentals=int(exps))


def shape(dims, dtype):
    return jax.ShapeDtypeStruct(dims, dtype)


def exchange(x, bit):
    peers = lax.axis_size("col")
    return lax.ppermute(x, "col", [(i, i ^ bit) for i in range(peers)])


def on_device(patches, tissue, w_query, w_key, w_value, w_out, agent_tokens, seven, five, three):
    band_rows, width, dim = patches.shape
    tokens = band_rows * width
    agents = agent_tokens.shape[0]
    half_dim = dim // 2
    scale = (dim // HEADS) ** (-0.5)
    flat = patches.reshape(tokens, dim)
    peers = lax.axis_size("col")
    place = lax.axis_index("col")
    odd = place % 2
    vmem = pl.BlockSpec(memory_space=VMEM)
    anywhere = pl.BlockSpec(memory_space=pl.ANY)

    other = exchange(flat, 1)
    other_tissue = exchange(tissue, 1)

    border = lax.dynamic_slice_in_dim(flat, odd * (tokens - 3 * width), 3 * width, 0)
    border = pl.pallas_call(
        pass_kernel,
        out_shape=shape((3 * width, dim), BF16),
        in_specs=[anywhere],
        out_specs=anywhere,
        input_output_aliases={0: 0},
        compiler_params=params(16),
        cost_estimate=cost(1e11, 1e6),
        name="pass",
    )(border)
    rest = [(i, i + 1) for i in range(1, peers - 1, 2)]
    outer = lax.ppermute(border, "col", rest + [(j, i) for i, j in rest])

    wide_shape, narrow_shape = shape((72, 512), F32), shape((72, 512), BF16)
    both_bands = shape((2 * tokens, half_dim), BF16)
    first = pl.pallas_call(
        project_kernel,
        out_shape=both_bands,
        in_specs=[vmem] * 4,
        out_specs=vmem,
        compiler_params=params(20),
        cost_estimate=cost(6e8, 4e6),
        name="project",
    )(flat, other, w_key, w_value)

    def band(kernel, out_shape, both):
        return pl.pallas_call(
            functools.partial(kernel, scale),
            out_shape=out_shape,
            in_specs=[vmem] * 4,
            out_specs=vmem,
            compiler_params=params(20),
            cost_estimate=cost(6e8, 4e6, 1e6),
            name="band",
        )(both, tissue, other_tissue, agent_tokens)

    payload = band(first_band_kernel, narrow_shape, first)

    def token(at, after):
        lanes = slice(at * half_dim, (at + 1) * half_dim)
        return pl.pallas_call(
            functools.partial(token_kernel, scale),
            out_shape=shape((tokens, HEADS // 2 * agents), BF16),
            grid=(1,),
            in_specs=[
                vmem,
                pl.BlockSpec((dim, half_dim), lambda i: (0, at)),
                pl.BlockSpec((agents, half_dim), lambda i: (0, at)),
                anywhere,
            ],
            out_specs=vmem,
            scratch_shapes=[VMEM((tokens, half_dim), BF16)],
            compiler_params=params(20),
            cost_estimate=cost(2e9, 6e6, 1e6),
            name="token",
        )(flat, w_query, agent_tokens, after)

    def conv(chunks, after):
        parts = pl.pallas_call(
            functools.partial(conv_kernel, chunks[0] * 128),
            out_shape=[shape((band_rows, width, 128), F32)] * len(chunks),
            in_specs=[vmem] * 4 + [anywhere],
            out_specs=[vmem] * len(chunks),
            scratch_shapes=[
                VMEM((sum(TAP_COUNTS) + len(TAP_COUNTS), width + 16, 128), F32),
                VMEM((7, sum(TAP_COUNTS), 8, 128), F32),
            ],
            compiler_params=params(20),
            cost_estimate=cost(3e9, 4e6),
            name="conv",
        )(values, above, below, taps, after)
        return [part.reshape(tokens, 128) for part in parts]

    hop = dict(in_specs=[vmem, vmem, anywhere], compiler_params=params(16), cost_estimate=cost(1e6, 1e6))

    def next_merge(held, got, before):
        return pl.pallas_call(
            next_merge_kernel, out_shape=(wide_shape, narrow_shape), out_specs=[vmem] * 2, name="merge_next", **hop
        )(held, got, before)

    got = exchange(payload, 4)
    second, values = pl.pallas_call(
        second_project_kernel,
        out_shape=(both_bands, shape((tokens, dim), BF16)),
        in_specs=[vmem] * 5 + [anywhere],
        out_specs=[vmem] * 2,
        compiler_params=params(20),
        cost_estimate=cost(8e8, 4e6),
        name="project_second",
    )(flat, other, w_key, w_value, first, payload)
    held = band(second_band_kernel, wide_shape, second)
    taps = pl.pallas_call(
        taps_kernel,
        out_shape=shape((7, 24, dim), F32),
        in_specs=[vmem] * 3 + [anywhere],
        out_specs=vmem,
        compiler_params=params(16),
        cost_estimate=cost(5e8, 1e6),
        name="taps",
    )(seven, five, three, payload)
    held, payload = next_merge(held, got, taps)
    got = exchange(payload, 2)
    weights_low = token(0, payload)
    above, below = pl.pallas_call(
        halo_kernel,
        out_shape=(shape((3 * width, dim), BF16), shape((3 * width, dim), BF16)),
        in_specs=[vmem] * 3 + [anywhere],
        out_specs=[vmem] * 2,
        compiler_params=params(16),
        cost_estimate=cost(4e8, 2e6),
        name="halo",
    )(other, outer, w_value, weights_low)
    held, payload = next_merge(held, got, above)
    bit = 8
    while bit * 2 < peers:
        got = exchange(payload, bit)
        held, payload = next_merge(held, got, payload)
        bit *= 2
    got = exchange(payload, bit)
    weights_high = token(1, payload)
    positions = conv([0], weights_high)
    own = pl.pallas_call(
        last_merge_kernel, out_shape=shape((64, 512), BF16), out_specs=vmem, name="merge_last", **hop
    )(held, got, positions[0])
    near = exchange(own, 4)
    positions += conv([1, 2, 3], own)
    pair = pl.pallas_call(
        relay_kernel,
        out_shape=shape((128, 512), BF16),
        in_specs=[vmem, vmem, anywhere],
        out_specs=vmem,
        compiler_params=params(16),
        cost_estimate=cost(1e6, 1e6),
        name="relay",
    )(own, near, positions[3])
    other_pair = exchange(pair, 1)

    partial = pl.pallas_call(
        own_out_kernel,
        out_shape=shape((tokens, dim), F32),
        in_specs=[vmem] * 8,
        out_specs=vmem,
        scratch_shapes=[VMEM((2, 128, 512), BF16)],
        compiler_params=params(20),
        cost_estimate=cost(1.1e9, 4e6),
        name="own_out",
    )(weights_low, weights_high, pair, *positions, w_out)
    mixed = pl.pallas_call(
        out_kernel,
        out_shape=shape((tokens, dim), BF16),
        in_specs=[vmem] * 9,
        out_specs=anywhere,
        scratch_shapes=[
            VMEM((2, 128, 512), BF16),
            VMEM((tokens, dim), BF16),
            pltpu.SemaphoreType.DMA((3,)),
        ],
        compiler_params=params(20),
        cost_estimate=cost(1.1e9, 8e6),
        name="out",
    )(weights_low, weights_high, other_pair, *positions, w_out, partial)
    return mixed.reshape(band_rows, width, dim)


def solution(mesh):
    return jax.shard_map(
        on_device,
        mesh=mesh,
        in_specs=(
            P(("slide", "col"), None, None),
            P(("slide", "col"), None),
            P(),
            P(),
            P(),
            P(),
            P(),
            P(),
            P(),
            P(),
        ),
        out_specs=P(("slide", "col"), None, None),
        check_vma=False,
    )
```
